128 devices in a mesh: dp: 16 (over z, x_lo, core), ctx: 8 (over y, x_hi).
Axes of the slice: x: 4 (x_hi: 2, x_lo: 2; x = x_hi * 2 + x_lo), y: 4, z: 4, core: 2. Of those that a mesh axis runs over, the one named last changes fastest.
Arguments:
- layer_input: bfloat16 [4096, 8192], P('ctx'), may hold values from -6 to 6
- queries: bfloat16 [4096, 8192], P('ctx', 'dp'), may hold values from -13 to 13
- key_vectors: bfloat16 [4096, 1024], P('ctx'), may hold values from -6 to 6
- value_vectors: bfloat16 [4096, 1024], P('ctx'), may hold values from -6 to 6
- grad_output: bfloat16 [4096, 8192], P('ctx', 'dp'), may hold values from -1.5 to 1.5
- positions: int32 [4096], P('ctx'), may hold values from 0 to 4095, as said below
Outputs:
- grad_queries: bfloat16 [4096, 8192], P('ctx', 'dp')
- grad_keys: bfloat16 [4096, 1024], P('ctx', 'dp')
- grad_values: bfloat16 [4096, 1024], P('ctx', 'dp')
- grad_wq: float32 [8192, 8192], P('ctx', 'dp')
- grad_wk: float32 [8192, 1024], P('ctx', 'dp')
- grad_wv: float32 [8192, 1024], P('ctx', 'dp')
The draws below stay inside these ranges and needn't reach their ends.
Inputs may be any that keep to these rules, and one draw needn't show every extreme that they name: The positions are 0 to 4095, each once, in aligned runs of 256 rows that hold consecutive ascending positions starting at a multiple of 256.
All inputs are finite; a program needn't handle non-finite values.
Results may differ from the reference program's by a relative error of at most 0.0061.
Values may be sent and summed in bfloat16 or wider, within the bound.
No kernel may reach another device: no remote copies, remote signals or barrier semaphores. Data moves between devices by JAX's collectives and lax.ppermute only.
A program may use at most 128 MiB of HBM per device.

```python
import math
import jax
import jax.numpy as jnp
from jax import lax

D = 8192
HD = 128
QH = 64
KVH = 8
TOK_DEV = 512
LEN = 4096


def draw_queries(key, part):
    key = jax.random.fold_in(key, 11)
    return jnp.clip(jax.random.normal(key, (LEN, QH * HD), jnp.float32), -6.0, 6.0).astype(jnp.bfloat16)


def draw_key_vectors(key, part):
    key = jax.random.fold_in(key, 12)
    return jnp.clip(jax.random.normal(key, (LEN, KVH * HD), jnp.float32), -6.0, 6.0).astype(jnp.bfloat16)


def draw_positions(key, part):
    key = jax.random.fold_in(key, 13)
    half = TOK_DEV // 2
    runs = LEN // half
    order = jax.random.permutation(key, runs)
    offsets = jnp.arange(half)
    placed = order[:, None] * half + offsets[None, :]
    return placed.reshape(LEN).astype(jnp.int32)


def spiked(entries, stream_key, source, target, shards_of, factor):
    owner, partner = [(jnp.arange(entries.shape[position]) // (entries.shape[position] // shards_of)).reshape([-1 if axis == position else 1 for axis in range(entries.ndim)]) for position in (source, target)]
    chosen = jax.random.permutation(stream_key, shards_of)[partner]
    strong = (owner == chosen) | (owner == (partner + shards_of // 2) % shards_of)
    return jnp.where(strong, factor * entries, entries)


def levels(stream_key, shape, split, smallest, high):
    loudness, own = 1.0, jax.random.fold_in(stream_key, 6)
    for dim, shards_of in split:
        heights = jnp.exp(jax.random.uniform(jax.random.fold_in(own, dim), (shards_of,), jnp.float32, smallest / len(split), high / len(split)))
        loudness = loudness * jnp.repeat(heights, shape[dim] // shards_of).reshape([-1 if axis == dim else 1 for axis in range(len(shape))])
    return loudness


def bell_draw(stream_key, shape, width, most, cuts=(), held_as=jnp.bfloat16):
    entries = jax.random.normal(stream_key, shape, jnp.float32) * width
    if len(cuts) > 0:
        entries = levels(stream_key, shape, cuts, -0.22, 0.18) * entries
    return jnp.clip(entries, min=-most, max=most).astype(held_as)


def bell_draw_with(rng, extent, spread, limit, shards, heavy, dtype=jnp.bfloat16):
    result = spread * jax.random.normal(rng, extent, jnp.float32)
    if shards:
        result = result * levels(rng, extent, shards, -0.22, 0.18)
    return jnp.clip(spiked(result, jax.random.fold_in(rng, 3), *heavy), -limit, limit).astype(dtype)


def setup_inputs(seed: int = 0) -> dict:
    key_of = jax.random.split(jax.random.key(seed), 7)
    return {
        "layer_input": bell_draw_with(key_of[0], (LEN, D), 1.0, 6.0, ((0, 8),), (0, 1, 8, 2.0)),
        "queries": draw_queries(jax.random.fold_in(key_of[6], 71), 0),
        "key_vectors": draw_key_vectors(jax.random.fold_in(key_of[6], 71), 0),
        "value_vectors": bell_draw(key_of[3], (LEN, KVH * HD), 1.0, 6.0, ((0, 8),)),
        "grad_output": bell_draw(key_of[4], (LEN, QH * HD), 0.25, 1.5, ((0, 8), (1, 16))),
        "positions": draw_positions(jax.random.fold_in(key_of[6], 71), 0),
    }


LOW_VALUE = -1e+30

def group_grads(items, pos_all):
    query_group, key_all, value_all, grad_group = items
    factor = 1.0 / math.sqrt(HD)
    group = QH // KVH
    block = TOK_DEV
    count = group * LEN // block
    query_blocks = query_group.reshape(LEN, group, HD).transpose(1, 0, 2).reshape(count, block, HD)
    grad_blocks = grad_group.reshape(LEN, group, HD).transpose(1, 0, 2).reshape(count, block, HD)
    pos_blocks = jnp.tile(pos_all, group).reshape(count, block)

    def advance(state, part):
        query_rows, grad_rows, query_pos = part
        key_acc, value_acc = state
        scores = jnp.dot(query_rows, key_all.T, preferred_element_type=jnp.float32) * factor
        visible = pos_all[None, :] <= query_pos[:, None]
        scores = jnp.where(visible, scores, LOW_VALUE)
        row_max = lax.optimization_barrier(jnp.max(scores, axis=1, keepdims=True))
        denom = lax.optimization_barrier(jnp.sum(jnp.where(visible, jnp.exp(scores - row_max), 0.0), axis=1, keepdims=True))
        lse = row_max + jnp.log(denom)
        probs = jnp.where(visible, jnp.exp(scores - lse), 0.0)
        grad_probs = jnp.dot(grad_rows, value_all.T, preferred_element_type=jnp.float32)
        row_dots = lax.optimization_barrier(jnp.sum(probs * grad_probs, axis=1, keepdims=True))
        grad_scores = (probs * (grad_probs - row_dots)).astype(jnp.bfloat16)
        probs_low = probs.astype(jnp.bfloat16)
        grad_query = (jnp.dot(grad_scores, key_all, preferred_element_type=jnp.float32) * factor).astype(jnp.bfloat16)
        key_acc = key_acc + jnp.dot(grad_scores.T, query_rows, preferred_element_type=jnp.float32)
        value_acc = value_acc + jnp.dot(probs_low.T, grad_rows, preferred_element_type=jnp.float32)
        return ((key_acc, value_acc), grad_query)
    zeros = jnp.zeros((LEN, HD), jnp.float32)
    (key_acc, value_acc), grad_query = lax.scan(advance, (zeros, zeros), (query_blocks, grad_blocks, pos_blocks))
    grad_query = grad_query.reshape(group, LEN, HD).transpose(1, 0, 2).reshape(LEN, group * HD)
    return (grad_query, (key_acc * factor).astype(jnp.bfloat16), value_acc.astype(jnp.bfloat16))

def reference(layer_input, queries, key_vectors, value_vectors, grad_output, positions):
    group = QH // KVH
    query_heads = queries.reshape(LEN, KVH, group * HD).transpose(1, 0, 2)
    grad_heads = grad_output.reshape(LEN, KVH, group * HD).transpose(1, 0, 2)
    key_heads = key_vectors.reshape(LEN, KVH, HD).transpose(1, 0, 2)
    value_heads = value_vectors.reshape(LEN, KVH, HD).transpose(1, 0, 2)
    grad_q, grad_k, grad_v = lax.map(lambda items: group_grads(items, positions), (query_heads, key_heads, value_heads, grad_heads))
    grad_queries = grad_q.transpose(1, 0, 2).reshape(LEN, QH * HD)
    grad_keys = grad_k.transpose(1, 0, 2).reshape(LEN, KVH * HD)
    grad_values = grad_v.transpose(1, 0, 2).reshape(LEN, KVH * HD)
    scale = 1.0 / math.sqrt(LEN)
    grad_wq = jnp.dot(layer_input.T, grad_queries, preferred_element_type=jnp.float32) * scale
    grad_wk = jnp.dot(layer_input.T, grad_keys, preferred_element_type=jnp.float32) * scale
    grad_wv = jnp.dot(layer_input.T, grad_values, preferred_element_type=jnp.float32) * scale
    return (grad_queries, grad_keys, grad_values, grad_wq, grad_wk, grad_wv)
```

```python
import functools
import math

import jax
import jax.numpy as jnp
from jax import lax
from jax.experimental import pallas as pl
from jax.experimental.pallas import tpu as pltpu
from jax.sharding import PartitionSpec as P

HD = 128
QH = 64
KVH = 8
RUN = 256
LOW = -1e30
LOG2E = 1.4426950408889634
VMEM_BYTES = 60 * 1024 * 1024


def contract(left, right, left_dim, right_dim):
    return lax.dot_general(
        left, right, (((left_dim,), (right_dim,)), ((), ())), preferred_element_type=jnp.float32
    )


def ctx_peer(index, dy, dx):
    return ((index // 2 + dy) % 4) * 2 + (index % 2 + dx) % 2


def to_peer(value, dy, dx):
    return lax.ppermute(value, "ctx", [(i, ctx_peer(i, dy, dx)) for i in range(8)])


def swap_cores(value):
    return lax.ppermute(value, "dp", [(i, i ^ 1) for i in range(16)])


SHIFTS = [(s // 2, s % 2) for s in range(8)]


def attention_kernel(
    heads, info_ref, q_ref, g_ref, a_ref, b_ref, dq_ref, keep_ref, give_ref,
    ks, vs, kt, scores, grads, dka, dva, qh, gh, dqt,
):
    slots, slot_rows, _ = a_ref.shape
    runs_per_slot = 2
    scale = 1.0 / math.sqrt(HD)
    core = info_ref[2 * slots]
    for b in range(slots * runs_per_slot):
        slot, part = b // runs_per_slot, b % runs_per_slot
        rows = slice(part * RUN, (part + 1) * RUN)
        at = pl.multiple_of(info_ref[b] * RUN, RUN)
        first, second = a_ref[slot, rows, :], b_ref[slot, rows, :]
        key_block = jnp.where(core == 0, first, second)
        ks[pl.ds(at, RUN), :] = key_block
        kt[:, pl.ds(at, RUN)] = key_block.T
        vs[pl.ds(at, RUN), :] = jnp.where(core == 0, second, first)
    dka[...] = jnp.zeros_like(dka)
    dva[...] = jnp.zeros_like(dva)
    for half in range(2):
        run = info_ref[half]
        rows = slice(half * RUN, (half + 1) * RUN)
        for h in range(heads):
            qh[h * RUN : (h + 1) * RUN, :] = q_ref[rows, h * HD : (h + 1) * HD]
            gh[h * RUN : (h + 1) * RUN, :] = g_ref[rows, h * HD : (h + 1) * HD]

        def stat_step(j, state, diagonal):
            at = pl.multiple_of(j * RUN, RUN)
            key_block = ks[pl.ds(at, RUN), :]
            value_block = vs[pl.ds(at, RUN), :]
            new_state = []
            for h in range(heads):
                row_max, denom, weighted = state[h]
                cols = slice(h * RUN, (h + 1) * RUN)
                s = contract(key_block, qh[cols, :], 1, 1) * (scale * LOG2E)
                if diagonal:
                    key_at = lax.broadcasted_iota(jnp.int32, (RUN, RUN), 0)
                    query_at = lax.broadcasted_iota(jnp.int32, (RUN, RUN), 1)
                    s = jnp.where(key_at <= query_at, s, LOW)
                scores[pl.ds(at, RUN), cols] = s
                dp = contract(value_block, gh[cols, :], 1, 1)
                grads[pl.ds(at, RUN), cols] = dp
                s3 = s.reshape(RUN // 8, 8, RUN)
                dp3 = dp.reshape(RUN // 8, 8, RUN)
                new_max = jnp.maximum(row_max, jnp.max(s3, axis=0))
                fade = jnp.exp2(row_max - new_max)
                expo = jnp.exp2(s3 - new_max[None])
                if diagonal:
                    expo = jnp.where(s3 > 0.5 * LOW, expo, 0.0)
                new_state.append(
                    (
                        new_max,
                        denom * fade + jnp.sum(expo, axis=0),
                        weighted * fade + jnp.sum(expo * dp3, axis=0),
                    )
                )
            return tuple(new_state)

        zeros = jnp.zeros((8, RUN), jnp.float32)
        state = tuple((jnp.full((8, RUN), LOW, jnp.float32), zeros, zeros) for _ in range(heads))
        state = lax.fori_loop(0, run, lambda j, st: stat_step(j, st, False), state)
        state = stat_step(run, state, True)
        lse, dots = [], []
        for h in range(heads):
            row_max, denom, weighted = state[h]
            top = jnp.max(row_max, axis=0, keepdims=True)
            fade = jnp.exp2(row_max - top)
            total = jnp.sum(denom * fade, axis=0, keepdims=True)
            lse.append(top + jnp.log2(total))
            dots.append(jnp.sum(weighted * fade, axis=0, keepdims=True) / total)
        dqt[...] = jnp.zeros_like(dqt)

        def grad_step(j, carry):
            at = pl.multiple_of(j * RUN, RUN)
            key_cols = kt[:, pl.ds(at, RUN)]
            dk, dv = 0.0, 0.0
            for h in range(heads):
                cols = slice(h * RUN, (h + 1) * RUN)
                p = jnp.exp2(scores[pl.ds(at, RUN), cols] - lse[h])
                ds = (p * (grads[pl.ds(at, RUN), cols] - dots[h])).astype(jnp.bfloat16)
                dv += contract(p.astype(jnp.bfloat16), gh[cols, :], 1, 0)
                dk += contract(ds, qh[cols, :], 1, 0)
                dqt[:, cols] += contract(key_cols, ds, 1, 0)
            dka[pl.ds(at, RUN), :] += dk
            dva[pl.ds(at, RUN), :] += dv
            return carry

        lax.fori_loop(0, run + 1, grad_step, 0)
        for h in range(heads):
            cols = slice(h * RUN, (h + 1) * RUN)
            dq_ref[rows, h * HD : (h + 1) * HD] = (dqt[:, cols] * scale).T.astype(jnp.bfloat16)
    half_head = HD // 2
    for b in range(slots * runs_per_slot):
        slot, part = b // runs_per_slot, b % runs_per_slot
        rows = slice(part * RUN, (part + 1) * RUN)
        at = pl.multiple_of(info_ref[b] * RUN, RUN)
        dk = dka[pl.ds(at, RUN), :] * scale
        dv = dva[pl.ds(at, RUN), :]
        low = jnp.concatenate([dk[:, :half_head], dv[:, :half_head]], axis=1)
        high = jnp.concatenate([dk[:, half_head:], dv[:, half_head:]], axis=1)
        keep_ref[slot, rows, :] = jnp.where(core == 0, low, high).astype(jnp.bfloat16)
        give_ref[slot, rows, :] = jnp.where(core == 0, high, low).astype(jnp.bfloat16)


def attention(info, queries, grad_output, mine, other):
    slots = mine.shape[0]
    count = slots * 2 * RUN
    heads = queries.shape[1] // HD
    wide = heads * RUN
    smem = pl.BlockSpec(memory_space=pltpu.SMEM)
    vmem = pl.BlockSpec(memory_space=pltpu.VMEM)
    shared = jax.ShapeDtypeStruct((slots, 2 * RUN, HD), jnp.bfloat16)
    pairs = heads * 2 * RUN * count // 2
    return pl.pallas_call(
        functools.partial(attention_kernel, heads),
        out_shape=(jax.ShapeDtypeStruct(queries.shape, jnp.bfloat16), shared, shared),
        in_specs=[smem, vmem, vmem, vmem, vmem],
        out_specs=(vmem, vmem, vmem),
        scratch_shapes=[
            pltpu.VMEM((count, HD), jnp.bfloat16),
            pltpu.VMEM((count, HD), jnp.bfloat16),
            pltpu.VMEM((HD, count), jnp.bfloat16),
            pltpu.VMEM((count, wide), jnp.float32),
            pltpu.VMEM((count, wide), jnp.float32),
            pltpu.VMEM((count, HD), jnp.float32),
            pltpu.VMEM((count, HD), jnp.float32),
            pltpu.VMEM((wide, HD), jnp.bfloat16),
            pltpu.VMEM((wide, HD), jnp.bfloat16),
            pltpu.VMEM((HD, wide), jnp.float32),
        ],
        compiler_params=pltpu.CompilerParams(vmem_limit_bytes=VMEM_BYTES),
        cost_estimate=pl.CostEstimate(
            flops=5 * 4 * pairs * HD, bytes_accessed=8 * 1024 * 1024, transcendentals=2 * pairs
        ),
    )(info, queries, grad_output, mine, other)


def local(layer_input, queries, key_vectors, value_vectors, grad_output, positions):
    member = lax.axis_index("dp") % 2
    here = lax.axis_index("ctx")
    head = lax.axis_index("dp") // 2
    count = queries.shape[0]
    width = layer_input.shape[1] // 8
    half = width // 2
    first = member == 0

    key_local = lax.dynamic_slice_in_dim(key_vectors, head * HD, HD, 1)
    value_local = lax.dynamic_slice_in_dim(value_vectors, head * HD, HD, 1)
    runs_here = (positions[::RUN] // RUN).astype(jnp.bfloat16)
    tail = jnp.broadcast_to(jnp.pad(runs_here, (0, HD - 2))[None], (16, HD))
    own = jnp.concatenate([jnp.where(first, key_local, value_local), tail], axis=0)
    got = [own] + [to_peer(own, dy, dx) for dy, dx in SHIFTS[1:]]
    mine = jnp.stack(got)
    other = swap_cores(mine)
    info = jnp.concatenate(
        [mine[:, count, :2].reshape(16).astype(jnp.int32), member.astype(jnp.int32)[None]]
    )

    base = layer_input
    blocks = []
    for dy, dx in SHIFTS:
        target = ((here // 2 + dy) % 4) * 2 + (here % 2 + dx) % 2
        part = lax.dynamic_slice(base, (0, target * width + member * half), (count, half))
        blocks.append(part if (dy, dx) == (0, 0) else to_peer(part, dy, dx))
    input_mine = jnp.concatenate(blocks, axis=0)
    input_other = swap_cores(input_mine)

    grad_query, keep, give = attention(info, queries, grad_output, mine, other)

    summed = (keep.astype(jnp.float32) + swap_cores(give).astype(jnp.float32)).astype(jnp.bfloat16)
    terms = [summed[0]] + [
        to_peer(summed[s], -dy, dx) for s, (dy, dx) in enumerate(SHIFTS) if s > 0
    ]
    total = sum(term.astype(jnp.float32) for term in terms).astype(jnp.bfloat16)

    queries_all = jnp.concatenate([grad_query] + [to_peer(grad_query, dy, dx) for dy, dx in SHIFTS[1:]])
    shared_all = jnp.concatenate([total] + [to_peer(total, dy, dx) for dy, dx in SHIFTS[1:]])
    norm = 1.0 / math.sqrt(count * 8)

    def in_order(a, b):
        return jnp.concatenate([jnp.where(first, a, b), jnp.where(first, b, a)], axis=0)

    grad_wq = in_order(
        contract(input_mine, queries_all, 0, 0), contract(input_other, queries_all, 0, 0)
    )
    grad_wkv = in_order(
        contract(input_mine, shared_all, 0, 0), contract(input_other, shared_all, 0, 0)
    )
    share = HD // 2
    return (
        grad_query,
        total[:, :share],
        total[:, share:],
        grad_wq * norm,
        grad_wkv[:, :share] * norm,
        grad_wkv[:, share:] * norm,
    )


def solution(mesh):
    in_specs = (
        P("ctx", None),
        P("ctx", "dp"),
        P("ctx", None),
        P("ctx", None),
        P("ctx", "dp"),
        P("ctx"),
    )
    out_specs = (P("ctx", "dp"),) * 6
    return jax.shard_map(local, mesh=mesh, in_specs=in_specs, out_specs=out_specs, check_vma=False)
```

```python
import functools
import math

import jax
import jax.numpy as jnp
from jax import lax
from jax.experimental import pallas as pl
from jax.experimental.pallas import tpu as pltpu
from jax.sharding import PartitionSpec as P

HD = 128
QH = 64
KVH = 8
RUN = 256
LOW = -1e30
LOG2E = 1.4426950408889634
VMEM_BYTES = 60 * 1024 * 1024


def contract(left, right, left_dim, right_dim):
    return lax.dot_general(
        left, right, (((left_dim,), (right_dim,)), ((), ())), preferred_element_type=jnp.float32
    )


def along_y(value, step):
    return lax.ppermute(value, "ctx", [(i, (i + 2 * step) % 8) for i in range(8)])


def swap_x(value):
    return lax.ppermute(value, "ctx", [(i, i ^ 1) for i in range(8)])


def along_z(value, step):
    return lax.ppermute(value, "dp", [(i, (i + 4 * step) % 16) for i in range(16)])


def swap_cores(value):
    return lax.ppermute(value, "dp", [(i, i ^ 1) for i in range(16)])


def to_all_y(value):
    return [along_y(value, step) for step in (1, 3, 2)]


def by_source(one, three, two):
    return [one, two, three]


def attention_kernel(
    heads, info_ref, q_ref, g_ref, mine_refs, other_refs, dq_ref, keep_ref, give_ref,
    ks, vs, kt, scores, grads, dka, dva, qh, gh, dqt,
):
    per_ref = mine_refs[0].shape[0]
    slots = per_ref * len(mine_refs)
    runs_per_slot = 2
    scale = 1.0 / math.sqrt(HD)
    core = info_ref[2 * slots]
    for b in range(slots * runs_per_slot):
        slot, part = b // runs_per_slot, b % runs_per_slot
        rows = slice(part * RUN, (part + 1) * RUN)
        at = pl.multiple_of(info_ref[b] * RUN, RUN)
        first = mine_refs[slot // per_ref][slot % per_ref, rows, :]
        second = other_refs[slot // per_ref][slot % per_ref, rows, :]
        key_block = jnp.where(core == 0, first, second)
        ks[pl.ds(at, RUN), :] = key_block
        kt[:, pl.ds(at, RUN)] = key_block.T
        vs[pl.ds(at, RUN), :] = jnp.where(core == 0, second, first)
    dka[...] = jnp.zeros_like(dka)
    dva[...] = jnp.zeros_like(dva)
    for half in range(2):
        run = info_ref[half]
        rows = slice(half * RUN, (half + 1) * RUN)
        for h in range(heads):
            qh[h * RUN : (h + 1) * RUN, :] = q_ref[rows, h * HD : (h + 1) * HD]
            gh[h * RUN : (h + 1) * RUN, :] = g_ref[rows, h * HD : (h + 1) * HD]

        def stat_step(j, state, diagonal):
            at = pl.multiple_of(j * RUN, RUN)
            key_block = ks[pl.ds(at, RUN), :]
            value_block = vs[pl.ds(at, RUN), :]
            new_state = []
            for h in range(heads):
                row_max, denom, weighted = state[h]
                cols = slice(h * RUN, (h + 1) * RUN)
                s = contract(key_block, qh[cols, :], 1, 1) * (scale * LOG2E)
                if diagonal:
                    key_at = lax.broadcasted_iota(jnp.int32, (RUN, RUN), 0)
                    query_at = lax.broadcasted_iota(jnp.int32, (RUN, RUN), 1)
                    s = jnp.where(key_at <= query_at, s, LOW)
                scores[pl.ds(at, RUN), cols] = s
                dp = contract(value_block, gh[cols, :], 1, 1)
                grads[pl.ds(at, RUN), cols] = dp
                s3 = s.reshape(RUN // 8, 8, RUN)
                dp3 = dp.reshape(RUN // 8, 8, RUN)
                new_max = jnp.maximum(row_max, jnp.max(s3, axis=0))
                fade = jnp.exp2(row_max - new_max)
                expo = jnp.exp2(s3 - new_max[None])
                if diagonal:
                    expo = jnp.where(s3 > 0.5 * LOW, expo, 0.0)
                new_state.append(
                    (
                        new_max,
                        denom * fade + jnp.sum(expo, axis=0),
                        weighted * fade + jnp.sum(expo * dp3, axis=0),
                    )
                )
            return tuple(new_state)

        zeros = jnp.zeros((8, RUN), jnp.float32)
        state = tuple((jnp.full((8, RUN), LOW, jnp.float32), zeros, zeros) for _ in range(heads))
        state = lax.fori_loop(0, run, lambda j, st: stat_step(j, st, False), state)
        state = stat_step(run, state, True)
        lse, dots = [], []
        for h in range(heads):
            row_max, denom, weighted = state[h]
            top = jnp.max(row_max, axis=0, keepdims=True)
            fade = jnp.exp2(row_max - top)
            total = jnp.sum(denom * fade, axis=0, keepdims=True)
            lse.append(top + jnp.log2(total))
            dots.append(jnp.sum(weighted * fade, axis=0, keepdims=True) / total)
        dqt[...] = jnp.zeros_like(dqt)

        def grad_step(j, carry):
            at = pl.multiple_of(j * RUN, RUN)
            key_cols = kt[:, pl.ds(at, RUN)]
            dk, dv = 0.0, 0.0
            for h in range(heads):
                cols = slice(h * RUN, (h + 1) * RUN)
                p = jnp.exp2(scores[pl.ds(at, RUN), cols] - lse[h])
                ds = (p * (grads[pl.ds(at, RUN), cols] - dots[h])).astype(jnp.bfloat16)
                dv += contract(p.astype(jnp.bfloat16), gh[cols, :], 1, 0)
                dk += contract(ds, qh[cols, :], 1, 0)
                dqt[:, cols] += contract(key_cols, ds, 1, 0)
            dka[pl.ds(at, RUN), :] += dk
            dva[pl.ds(at, RUN), :] += dv
            return carry

        lax.fori_loop(0, run + 1, grad_step, 0)
        for h in range(heads):
            cols = slice(h * RUN, (h + 1) * RUN)
            dq_ref[rows, h * HD : (h + 1) * HD] = (dqt[:, cols] * scale).T.astype(jnp.bfloat16)
    half_head = HD // 2
    for b in range(slots * runs_per_slot):
        slot, part = b // runs_per_slot, b % runs_per_slot
        rows = slice(part * RUN, (part + 1) * RUN)
        at = pl.multiple_of(info_ref[b] * RUN, RUN)
        dk = dka[pl.ds(at, RUN), :] * scale
        dv = dva[pl.ds(at, RUN), :]
        low = jnp.concatenate([dk[:, :half_head], dv[:, :half_head]], axis=1)
        high = jnp.concatenate([dk[:, half_head:], dv[:, half_head:]], axis=1)
        keep_ref[slot, rows, :] = jnp.where(core == 0, low, high).astype(jnp.bfloat16)
        give_ref[slot, rows, :] = jnp.where(core == 0, high, low).astype(jnp.bfloat16)


def attention(info, queries, grad_output, mine, other):
    slots = mine[0].shape[0] * len(mine)
    count = slots * 2 * RUN
    heads = queries.shape[1] // HD
    wide = heads * RUN
    smem = pl.BlockSpec(memory_space=pltpu.SMEM)
    vmem = pl.BlockSpec(memory_space=pltpu.VMEM)
    shared = jax.ShapeDtypeStruct((slots, 2 * RUN, HD), jnp.bfloat16)
    pairs = heads * 2 * RUN * count // 2
    return pl.pallas_call(
        functools.partial(attention_kernel, heads),
        out_shape=(jax.ShapeDtypeStruct(queries.shape, jnp.bfloat16), shared, shared),
        in_specs=[smem, vmem, vmem, [vmem] * len(mine), [vmem] * len(other)],
        out_specs=(vmem, vmem, vmem),
        scratch_shapes=[
            pltpu.VMEM((count, HD), jnp.bfloat16),
            pltpu.VMEM((count, HD), jnp.bfloat16),
            pltpu.VMEM((HD, count), jnp.bfloat16),
            pltpu.VMEM((count, wide), jnp.float32),
            pltpu.VMEM((count, wide), jnp.float32),
            pltpu.VMEM((count, HD), jnp.float32),
            pltpu.VMEM((count, HD), jnp.float32),
            pltpu.VMEM((wide, HD), jnp.bfloat16),
            pltpu.VMEM((wide, HD), jnp.bfloat16),
            pltpu.VMEM((HD, wide), jnp.float32),
        ],
        compiler_params=pltpu.CompilerParams(vmem_limit_bytes=VMEM_BYTES),
        cost_estimate=pl.CostEstimate(
            flops=5 * 4 * pairs * HD, bytes_accessed=8 * 1024 * 1024, transcendentals=2 * pairs
        ),
    )(info, queries, grad_output, mine, other)


def local(layer_input, queries, key_vectors, value_vectors, grad_output, positions):
    group = lax.axis_index("dp")
    member, head, z = group % 2, group // 2, group // 4
    here = lax.axis_index("ctx")
    y, x_hi = here // 2, here % 2
    count = queries.shape[0]
    width = layer_input.shape[1] // 8
    slab = width // 8
    first = member == 0

    key_local = lax.dynamic_slice_in_dim(key_vectors, head * HD, HD, 1)
    value_local = lax.dynamic_slice_in_dim(value_vectors, head * HD, HD, 1)
    runs_here = (positions[::RUN] // RUN).astype(jnp.bfloat16)
    tail = jnp.broadcast_to(jnp.pad(runs_here, (0, HD - 2))[None], (16, HD))
    own = jnp.concatenate([jnp.where(first, key_local, value_local), tail], axis=0)
    column = jnp.stack([own] + by_source(*to_all_y(own)))
    start = (2 * z + member) * slab

    def block(dy, dx):
        target = ((y + dy) % 4) * 2 + (x_hi + dx) % 2
        return lax.dynamic_slice(layer_input, (0, target * width + start), (count, slab))

    from_x = swap_x(jnp.stack([block(dy, 1) for dy in range(4)]))
    partner_column = swap_x(column)
    column_other = swap_cores(column)
    pairs = [jnp.stack([block(dy, 0), from_x[dy]]) for dy in range(4)]
    pairs = [pairs[0]] + [along_y(pairs[dy], dy) for dy in range(1, 4)]
    slab_own = jnp.concatenate([p[dx] for dx in range(2) for p in pairs], axis=0)
    partner_other = swap_cores(partner_column)
    info = jnp.concatenate(
        [
            column[:, count, :2].reshape(8).astype(jnp.int32),
            partner_column[:, count, :2].reshape(8).astype(jnp.int32),
            member.astype(jnp.int32)[None],
        ]
    )
    slab_back, slab_ahead = along_z(slab_own, 1), along_z(slab_own, 3)

    grad_query, keep, give = attention(
        info, queries, grad_output, [column, partner_column], [column_other, partner_other]
    )

    cut = slab_own.shape[0] // 2
    slab_far = jnp.concatenate([along_z(slab_back[:cut], 1), along_z(slab_ahead[cut:], 3)])
    slabs = jnp.zeros((4, 2) + slab_own.shape, jnp.bfloat16)
    for away, value in ((0, slab_own), (3, slab_back), (1, slab_ahead), (2, slab_far)):
        other = swap_cores(value)
        slabs = lax.dynamic_update_slice(slabs, value[None, None], ((z + away) % 4, member, 0, 0))
        slabs = lax.dynamic_update_slice(slabs, other[None, None], ((z + away) % 4, 1 - member, 0, 0))
    slabs = slabs.reshape((8,) + slab_own.shape)

    summed = (keep.astype(jnp.float32) + swap_cores(give).astype(jnp.float32)).astype(jnp.bfloat16)
    summed = summed.reshape(2, 4, count, HD)
    rows_y = summed[:, 0].astype(jnp.float32)
    for dy in (1, 3, 2):
        rows_y = rows_y + along_y(summed[:, dy], -dy).astype(jnp.float32)
    total = rows_y[0] + swap_x(rows_y[1].astype(jnp.bfloat16)).astype(jnp.float32)
    total = total.astype(jnp.bfloat16)
    both = jnp.stack([total, swap_x(total)])
    shared = jnp.stack([both] + by_source(*to_all_y(both)), axis=1)
    shared = shared.reshape(8 * count, HD)

    mark = count * 3 // 4
    part_a, part_b = grad_query[:mark], grad_query[mark:]
    column_a = jnp.stack([part_a] + by_source(*to_all_y(part_a)))
    all_a = jnp.concatenate([column_a, swap_x(column_a)])
    both_b = jnp.stack([part_b, swap_x(part_b)])
    all_b = jnp.stack([both_b] + by_source(*to_all_y(both_b)), axis=1)
    all_b = all_b.reshape((8,) + part_b.shape)
    queries_all = jnp.concatenate([all_a, all_b], axis=1).reshape(8 * count, -1)

    norm = 1.0 / math.sqrt(8 * count)
    grad_wq = contract(slabs, queries_all, 1, 0).reshape(width, -1) * norm
    grad_wkv = contract(slabs, shared, 1, 0).reshape(width, -1) * norm
    share = HD // 2
    return (
        grad_query,
        total[:, :share],
        total[:, share:],
        grad_wq,
        grad_wkv[:, :share],
        grad_wkv[:, share:],
    )


def solution(mesh):
    in_specs = (
        P("ctx", None),
        P("ctx", "dp"),
        P("ctx", None),
        P("ctx", None),
        P("ctx", "dp"),
        P("ctx"),
    )
    out_specs = (P("ctx", "dp"),) * 6
    return jax.shard_map(local, mesh=mesh, in_specs=in_specs, out_specs=out_specs, check_vma=False)
```

```python
import functools
import math

import jax
import jax.numpy as jnp
from jax import lax
from jax.experimental import pallas as pl
from jax.experimental.pallas import tpu as pltpu
from jax.sharding import PartitionSpec as P

HD = 128
QH = 64
KVH = 8
RUN = 256
LOW = -1e30
LOG2E = 1.4426950408889634
VMEM_BYTES = 60 * 1024 * 1024


def contract(left, right, left_dim, right_dim):
    return lax.dot_general(
        left, right, (((left_dim,), (right_dim,)), ((), ())), preferred_element_type=jnp.float32
    )


def along_y(value, step):
    return lax.ppermute(value, "ctx", [(i, (i + 2 * step) % 8) for i in range(8)])


def swap_x(value):
    return lax.ppermute(value, "ctx", [(i, i ^ 1) for i in range(8)])


def along_z(value, step):
    return lax.ppermute(value, "dp", [(i, (i + 4 * step) % 16) for i in range(16)])


def swap_cores(value):
    return lax.ppermute(value, "dp", [(i, i ^ 1) for i in range(16)])


def to_all_y(value):
    return [along_y(value, step) for step in (1, 3, 2)]


def by_source(one, three, two):
    return [one, two, three]


def attention_kernel(
    heads, info_ref, q_ref, g_ref, mine_refs, other_refs, dq_ref, dqt_ref, keep_ref, give_ref,
    ks, vs, kt, scores, grads, dka, dva, qh, gh, dqt,
):
    per_ref = mine_refs[0].shape[0]
    slots = per_ref * len(mine_refs)
    runs_per_slot = 2
    scale = 1.0 / math.sqrt(HD)
    core = info_ref[2 * slots]
    for b in range(slots * runs_per_slot):
        slot, part = b // runs_per_slot, b % runs_per_slot
        rows = slice(part * RUN, (part + 1) * RUN)
        at = pl.multiple_of(info_ref[b] * RUN, RUN)
        first = mine_refs[slot // per_ref][slot % per_ref, rows, :]
        second = other_refs[slot // per_ref][slot % per_ref, rows, :]
        key_block = jnp.where(core == 0, first, second)
        ks[pl.ds(at, RUN), :] = key_block
        kt[:, pl.ds(at, RUN)] = key_block.T
        vs[pl.ds(at, RUN), :] = jnp.where(core == 0, second, first)
    dka[...] = jnp.zeros_like(dka)
    dva[...] = jnp.zeros_like(dva)
    for half in range(2):
        run = info_ref[half]
        rows = slice(half * RUN, (half + 1) * RUN)
        for h in range(heads):
            qh[h * RUN : (h + 1) * RUN, :] = q_ref[rows, h * HD : (h + 1) * HD]
            gh[h * RUN : (h + 1) * RUN, :] = g_ref[rows, h * HD : (h + 1) * HD]

        def stat_step(j, state, diagonal):
            at = pl.multiple_of(j * RUN, RUN)
            key_block = ks[pl.ds(at, RUN), :]
            value_block = vs[pl.ds(at, RUN), :]
            new_state = []
            for h in range(heads):
                row_max, denom, weighted = state[h]
                cols = slice(h * RUN, (h + 1) * RUN)
                s = contract(key_block, qh[cols, :], 1, 1) * (scale * LOG2E)
                if diagonal:
                    key_at = lax.broadcasted_iota(jnp.int32, (RUN, RUN), 0)
                    query_at = lax.broadcasted_iota(jnp.int32, (RUN, RUN), 1)
                    s = jnp.where(key_at <= query_at, s, LOW)
                scores[pl.ds(at, RUN), cols] = s
                dp = contract(value_block, gh[cols, :], 1, 1)
                grads[pl.ds(at, RUN), cols] = dp
                s3 = s.reshape(RUN // 8, 8, RUN)
                dp3 = dp.reshape(RUN // 8, 8, RUN)
                new_max = jnp.maximum(row_max, jnp.max(s3, axis=0))
                fade = jnp.exp2(row_max - new_max)
                expo = jnp.exp2(s3 - new_max[None])
                if diagonal:
                    expo = jnp.where(s3 > 0.5 * LOW, expo, 0.0)
                new_state.append(
                    (
                        new_max,
                        denom * fade + jnp.sum(expo, axis=0),
                        weighted * fade + jnp.sum(expo * dp3, axis=0),
                    )
                )
            return tuple(new_state)

        zeros = jnp.zeros((8, RUN), jnp.float32)
        state = tuple((jnp.full((8, RUN), LOW, jnp.float32), zeros, zeros) for _ in range(heads))
        state = lax.fori_loop(0, run, lambda j, st: stat_step(j, st, False), state)
        state = stat_step(run, state, True)
        lse, dots = [], []
        for h in range(heads):
            row_max, denom, weighted = state[h]
            top = jnp.max(row_max, axis=0, keepdims=True)
            fade = jnp.exp2(row_max - top)
            total = jnp.sum(denom * fade, axis=0, keepdims=True)
            lse.append(top + jnp.log2(total))
            dots.append(jnp.sum(weighted * fade, axis=0, keepdims=True) / total)
        dqt[...] = jnp.zeros_like(dqt)

        def grad_step(j, carry):
            at = pl.multiple_of(j * RUN, RUN)
            key_cols = kt[:, pl.ds(at, RUN)]
            dk, dv = 0.0, 0.0
            for h in range(heads):
                cols = slice(h * RUN, (h + 1) * RUN)
                p = jnp.exp2(scores[pl.ds(at, RUN), cols] - lse[h])
                ds = (p * (grads[pl.ds(at, RUN), cols] - dots[h])).astype(jnp.bfloat16)
                dv += contract(p.astype(jnp.bfloat16), gh[cols, :], 1, 0)
                dk += contract(ds, qh[cols, :], 1, 0)
                dqt[:, cols] += contract(key_cols, ds, 1, 0)
            dka[pl.ds(at, RUN), :] += dk
            dva[pl.ds(at, RUN), :] += dv
            return carry

        lax.fori_loop(0, run + 1, grad_step, 0)
        for h in range(heads):
            cols = slice(h * RUN, (h + 1) * RUN)
            dq = dqt[:, cols] * scale
            dq_ref[rows, h * HD : (h + 1) * HD] = dq.T.astype(jnp.bfloat16)
            dqt_ref[h * HD : (h + 1) * HD, rows] = dq.astype(jnp.bfloat16)
    half_head = HD // 2
    for b in range(slots * runs_per_slot):
        slot, part = b // runs_per_slot, b % runs_per_slot
        rows = slice(part * RUN, (part + 1) * RUN)
        at = pl.multiple_of(info_ref[b] * RUN, RUN)
        dk = dka[pl.ds(at, RUN), :] * scale
        dv = dva[pl.ds(at, RUN), :]
        low = jnp.concatenate([dk[:, :half_head], dv[:, :half_head]], axis=1)
        high = jnp.concatenate([dk[:, half_head:], dv[:, half_head:]], axis=1)
        keep_ref[slot, rows, :] = jnp.where(core == 0, low, high).astype(jnp.bfloat16)
        give_ref[slot, rows, :] = jnp.where(core == 0, high, low).astype(jnp.bfloat16)


def attention(info, queries, grad_output, mine, other):
    slots = mine[0].shape[0] * len(mine)
    count = slots * 2 * RUN
    heads = queries.shape[1] // HD
    wide = heads * RUN
    smem = pl.BlockSpec(memory_space=pltpu.SMEM)
    vmem = pl.BlockSpec(memory_space=pltpu.VMEM)
    shared = jax.ShapeDtypeStruct((slots, 2 * RUN, HD), jnp.bfloat16)
    pairs = heads * 2 * RUN * count // 2
    return pl.pallas_call(
        functools.partial(attention_kernel, heads),
        out_shape=(
            jax.ShapeDtypeStruct(queries.shape, jnp.bfloat16),
            jax.ShapeDtypeStruct(queries.shape[::-1], jnp.bfloat16),
            shared,
            shared,
        ),
        in_specs=[smem, vmem, vmem, [vmem] * len(mine), [vmem] * len(other)],
        out_specs=(vmem, vmem, vmem, vmem),
        scratch_shapes=[
            pltpu.VMEM((count, HD), jnp.bfloat16),
            pltpu.VMEM((count, HD), jnp.bfloat16),
            pltpu.VMEM((HD, count), jnp.bfloat16),
            pltpu.VMEM((count, wide), jnp.float32),
            pltpu.VMEM((count, wide), jnp.float32),
            pltpu.VMEM((count, HD), jnp.float32),
            pltpu.VMEM((count, HD), jnp.float32),
            pltpu.VMEM((wide, HD), jnp.bfloat16),
            pltpu.VMEM((wide, HD), jnp.bfloat16),
            pltpu.VMEM((HD, wide), jnp.float32),
        ],
        compiler_params=pltpu.CompilerParams(vmem_limit_bytes=VMEM_BYTES),
        cost_estimate=pl.CostEstimate(
            flops=5 * 4 * pairs * HD, bytes_accessed=8 * 1024 * 1024, transcendentals=2 * pairs
        ),
    )(info, queries, grad_output, mine, other)


def join_kernel(in_refs, out_ref, sems):
    copies, at = [], 0
    for i, ref in enumerate(in_refs):
        copies.append(pltpu.make_async_copy(ref, out_ref.at[pl.ds(at, ref.shape[0])], sems.at[i]))
        copies[-1].start()
        at += ref.shape[0]
    for copy in copies:
        copy.wait()


def join(pieces):
    hbm = pl.BlockSpec(memory_space=pl.ANY)
    total = sum(p.shape[0] for p in pieces)
    return pl.pallas_call(
        join_kernel,
        out_shape=jax.ShapeDtypeStruct((total,) + pieces[0].shape[1:], pieces[0].dtype),
        in_specs=[[hbm] * len(pieces)],
        out_specs=hbm,
        scratch_shapes=[pltpu.SemaphoreType.DMA((len(pieces),))],
        cost_estimate=pl.CostEstimate(flops=0, bytes_accessed=2 * 1024 * 1024, transcendentals=0),
    )(list(pieces))


def weight_kernel(dx, last, place_ref, own_refs, other_refs, grad_refs, *rest):
    if last:
        sum_ref, shared_refs, wq_ref, wk_ref, wv_ref, inputs, sems = rest
        sides = (dx, 1 - dx)
    else:
        sum_ref, inputs, sems = rest
        sides = (dx,)
    core, z = place_ref[0], place_ref[1]
    lanes = own_refs[0].shape[-1]
    mine_at = pl.multiple_of(core * lanes, lanes)
    other_at = pl.multiple_of((1 - core) * lanes, lanes)
    copies = {}
    for away in range(4):
        for n, side in enumerate(sides):
            for which, (ref, at) in enumerate(((own_refs[away], mine_at), (other_refs[away], other_at))):
                copies[away, n, which] = pltpu.make_async_copy(
                    ref.at[:, side], inputs.at[away, n, :, :, pl.ds(at, lanes)], sems.at[away, n, which]
                )
                copies[away, n, which].start()
    for away in range(4):
        for which in range(2):
            copies[away, 0, which].wait()
        total = sum_ref[away] if last else 0.0
        for dy in range(4):
            total += contract(grad_refs[dy][...], inputs[away, 0, dy], 1, 0)
        if not last:
            sum_ref[away] = total
            continue
        norm = 1.0 / math.sqrt(8 * inputs.shape[3])
        at = pl.multiple_of(lax.rem(z + away, 4) * 2 * lanes, 2 * lanes)
        wq_ref[pl.ds(at, 2 * lanes), :] = (total * norm).T
    if not last:
        return
    shared = [[shared_refs[dy][side].T for dy in range(4)] for side in sides]
    for away in range(4):
        for which in range(2):
            copies[away, 1, which].wait()
        total = 0.0
        for n in range(2):
            for dy in range(4):
                total += contract(shared[n][dy], inputs[away, n, dy], 1, 0)
        at = pl.multiple_of(lax.rem(z + away, 4) * 2 * lanes, 2 * lanes)
        total = (total * norm).T
        half = lanes // 2
        wk_ref[pl.ds(at, 2 * lanes), :] = total[:, :half]
        wv_ref[pl.ds(at, 2 * lanes), :] = total[:, half:]


def weights(dx, place, own, other, grads, total=None, shared=None):
    last = total is not None
    smem = pl.BlockSpec(memory_space=pltpu.SMEM)
    vmem = pl.BlockSpec(memory_space=pltpu.VMEM)
    hbm = pl.BlockSpec(memory_space=pl.ANY)
    lanes, count, cols = own[0].shape[-1], own[0].shape[2], grads[0].shape[0]
    sides = 2 if last else 1
    f32 = jnp.float32
    if last:
        out_shape = (
            jax.ShapeDtypeStruct((8 * lanes, cols), f32),
            jax.ShapeDtypeStruct((8 * lanes, lanes // 2), f32),
            jax.ShapeDtypeStruct((8 * lanes, lanes // 2), f32),
        )
        more, more_specs, out_specs = (total, shared), [vmem, [vmem] * 4], (vmem,) * 3
    else:
        out_shape = jax.ShapeDtypeStruct((4, cols, 2 * lanes), f32)
        more, more_specs, out_specs = (), [], vmem
    return pl.pallas_call(
        functools.partial(weight_kernel, dx, last),
        out_shape=out_shape,
        in_specs=[smem, [hbm] * 4, [hbm] * 4, [vmem] * 4] + more_specs,
        out_specs=out_specs,
        scratch_shapes=[
            pltpu.VMEM((4, sides, 4, count, 2 * lanes), jnp.bfloat16),
            pltpu.SemaphoreType.DMA((4, sides, 2)),
        ],
        compiler_params=pltpu.CompilerParams(vmem_limit_bytes=VMEM_BYTES),
        cost_estimate=pl.CostEstimate(
            flops=2 * 4 * count * cols * 8 * lanes, bytes_accessed=10 * 1024 * 1024, transcendentals=0
        ),
    )(place, list(own), list(other), list(grads), *more)


def local(layer_input, queries, key_vectors, value_vectors, grad_output, positions):
    group = lax.axis_index("dp")
    member, head, z = group % 2, group // 2, group // 4
    here = lax.axis_index("ctx")
    y, x_hi = here // 2, here % 2
    count = queries.shape[0]
    width = layer_input.shape[1] // 8
    slab = width // 8
    first = member == 0
    place = jnp.stack([member, z]).astype(jnp.int32)

    key_local = lax.dynamic_slice_in_dim(key_vectors, head * HD, HD, 1)
    value_local = lax.dynamic_slice_in_dim(value_vectors, head * HD, HD, 1)
    runs_here = (positions[::RUN] // RUN).astype(jnp.bfloat16)
    tail = jnp.broadcast_to(jnp.pad(runs_here, (0, HD - 2))[None], (16, HD))
    own = jnp.concatenate([jnp.where(first, key_local, value_local), tail], axis=0)
    column = jnp.stack([own] + by_source(*to_all_y(own)))
    start = (2 * z + member) * slab

    def block(dy, dx):
        target = ((y + dy) % 4) * 2 + (x_hi + dx) % 2
        return lax.dynamic_slice(layer_input, (0, target * width + start), (count, slab))

    from_x = swap_x(jnp.stack([block(dy, 1) for dy in range(4)]))
    partner_column = swap_x(column)
    column_other = swap_cores(column)
    pairs = [jnp.stack([block(dy, 0), from_x[dy]]) for dy in range(4)]
    pairs = [pairs[0]] + [along_y(pairs[dy], dy) for dy in range(1, 4)]
    partner_other = swap_cores(partner_column)
    info = jnp.concatenate(
        [
            column[:, count, :2].reshape(8).astype(jnp.int32),
            partner_column[:, count, :2].reshape(8).astype(jnp.int32),
            member.astype(jnp.int32)[None],
        ]
    )
    slab_own = join(pairs).reshape(4, 2, count, slab)
    slab_back, slab_ahead = along_z(slab_own, 1), along_z(slab_own, 3)

    grad_query, grad_query_t, keep, give = attention(
        info, queries, grad_output, [column, partner_column], [column_other, partner_other]
    )
    grad_query_t, give, slab_back, slab_ahead = lax.optimization_barrier(
        (grad_query_t, give, slab_back, slab_ahead)
    )

    summed = (keep.astype(jnp.float32) + swap_cores(give).astype(jnp.float32)).astype(jnp.bfloat16)
    summed = summed.reshape(2, 4, count, HD)
    queries_x = [swap_x(grad_query_t)]
    queries_y = {1: along_y(grad_query_t, 1), 3: along_y(grad_query_t, 3)}
    rows_y = summed[:, 0].astype(jnp.float32)
    for dy in (1, 3, 2):
        rows_y = rows_y + along_y(summed[:, dy], -dy).astype(jnp.float32)
    rows_y = rows_y.astype(jnp.bfloat16)
    both = (rows_y.astype(jnp.float32) + swap_x(rows_y).astype(jnp.float32)[::-1]).astype(jnp.bfloat16)
    total = both[0]
    queries_y[2] = along_y(grad_query_t, 2)
    queries_x += [swap_x(queries_y[dy]) for dy in (1, 2, 3)]
    shared = [both] + by_source(*to_all_y(both))

    slab_far = along_z(slab_own, 2)
    slabs = [slab_own, slab_ahead, slab_far, slab_back]
    slabs_other = [swap_cores(value) for value in slabs]
    partial = weights(
        0, place, slabs, slabs_other, [grad_query_t] + [queries_y[dy] for dy in (1, 2, 3)]
    )
    grad_wq, grad_wk, grad_wv = weights(1, place, slabs, slabs_other, queries_x, partial, shared)
    share = HD // 2
    return grad_query, total[:, :share], total[:, share:], grad_wq, grad_wk, grad_wv


def solution(mesh):
    in_specs = (
        P("ctx", None),
        P("ctx", "dp"),
        P("ctx", None),
        P("ctx", None),
        P("ctx", "dp"),
        P("ctx"),
    )
    out_specs = (P("ctx", "dp"),) * 6
    return jax.shard_map(local, mesh=mesh, in_specs=in_specs, out_specs=out_specs, check_vma=False)
```

```python
import functools
import math

import jax
import jax.numpy as jnp
from jax import lax
from jax.experimental import pallas as pl
from jax.experimental.pallas import tpu as pltpu
from jax.sharding import PartitionSpec as P

HD = 128
QH = 64
KVH = 8
RUN = 256
LOW = -1e30
LOG2E = 1.4426950408889634
VMEM_BYTES = 60 * 1024 * 1024


def contract(left, right, left_dim, right_dim):
    return lax.dot_general(
        left, right, (((left_dim,), (right_dim,)), ((), ())), preferred_element_type=jnp.float32
    )


def along_y(value, step):
    return lax.ppermute(value, "ctx", [(i, (i + 2 * step) % 8) for i in range(8)])


def swap_x(value):
    return lax.ppermute(value, "ctx", [(i, i ^ 1) for i in range(8)])


def along_z(value, step):
    return lax.ppermute(value, "dp", [(i, (i + 4 * step) % 16) for i in range(16)])


def swap_cores(value):
    return lax.ppermute(value, "dp", [(i, i ^ 1) for i in range(16)])


def to_all_y(value):
    return [along_y(value, step) for step in (1, 3, 2)]


def by_source(one, three, two):
    return [one, two, three]


def attention_kernel(
    heads, info_ref, q_ref, g_ref, mine_refs, other_refs, dq_ref, keep_ref, give_ref,
    ks, vs, kt, scores, grads, dka, dva, qh, gh, dqt,
):
    per_ref = mine_refs[0].shape[0]
    slots = per_ref * len(mine_refs)
    runs_per_slot = 2
    scale = 1.0 / math.sqrt(HD)
    core = info_ref[2 * slots]
    for b in range(slots * runs_per_slot):
        slot, part = b // runs_per_slot, b % runs_per_slot
        rows = slice(part * RUN, (part + 1) * RUN)
        at = pl.multiple_of(info_ref[b] * RUN, RUN)
        first = mine_refs[slot // per_ref][slot % per_ref, rows, :]
        second = other_refs[slot // per_ref][slot % per_ref, rows, :]
        key_block = jnp.where(core == 0, first, second)
        ks[pl.ds(at, RUN), :] = key_block
        kt[:, pl.ds(at, RUN)] = key_block.T
        vs[pl.ds(at, RUN), :] = jnp.where(core == 0, second, first)
    dka[...] = jnp.zeros_like(dka)
    dva[...] = jnp.zeros_like(dva)
    for half in range(2):
        run = info_ref[half]
        rows = slice(half * RUN, (half + 1) * RUN)
        for h in range(heads):
            qh[h * RUN : (h + 1) * RUN, :] = q_ref[rows, h * HD : (h + 1) * HD]
            gh[h * RUN : (h + 1) * RUN, :] = g_ref[rows, h * HD : (h + 1) * HD]

        def stat_step(j, state, diagonal):
            at = pl.multiple_of(j * RUN, RUN)
            key_block = ks[pl.ds(at, RUN), :]
            value_block = vs[pl.ds(at, RUN), :]
            new_state = []
            for h in range(heads):
                row_max, denom, weighted = state[h]
                cols = slice(h * RUN, (h + 1) * RUN)
                s = contract(key_block, qh[cols, :], 1, 1) * (scale * LOG2E)
                if diagonal:
                    key_at = lax.broadcasted_iota(jnp.int32, (RUN, RUN), 0)
                    query_at = lax.broadcasted_iota(jnp.int32, (RUN, RUN), 1)
                    s = jnp.where(key_at <= query_at, s, LOW)
                scores[pl.ds(at, RUN), cols] = s
                dp = contract(value_block, gh[cols, :], 1, 1)
                grads[pl.ds(at, RUN), cols] = dp
                s3 = s.reshape(RUN // 8, 8, RUN)
                dp3 = dp.reshape(RUN // 8, 8, RUN)
                new_max = jnp.maximum(row_max, jnp.max(s3, axis=0))
                fade = jnp.exp2(row_max - new_max)
                expo = jnp.exp2(s3 - new_max[None])
                if diagonal:
                    expo = jnp.where(s3 > 0.5 * LOW, expo, 0.0)
                new_state.append(
                    (
                        new_max,
                        denom * fade + jnp.sum(expo, axis=0),
                        weighted * fade + jnp.sum(expo * dp3, axis=0),
                    )
                )
            return tuple(new_state)

        zeros = jnp.zeros((8, RUN), jnp.float32)
        state = tuple((jnp.full((8, RUN), LOW, jnp.float32), zeros, zeros) for _ in range(heads))
        state = lax.fori_loop(0, run, lambda j, st: stat_step(j, st, False), state)
        state = stat_step(run, state, True)
        lse, dots = [], []
        for h in range(heads):
            row_max, denom, weighted = state[h]
            top = jnp.max(row_max, axis=0, keepdims=True)
            fade = jnp.exp2(row_max - top)
            total = jnp.sum(denom * fade, axis=0, keepdims=True)
            lse.append(top + jnp.log2(total))
            dots.append(jnp.sum(weighted * fade, axis=0, keepdims=True) / total)
        dqt[...] = jnp.zeros_like(dqt)

        def grad_step(j, carry):
            at = pl.multiple_of(j * RUN, RUN)
            key_cols = kt[:, pl.ds(at, RUN)]
            dk, dv = 0.0, 0.0
            for h in range(heads):
                cols = slice(h * RUN, (h + 1) * RUN)
                p = jnp.exp2(scores[pl.ds(at, RUN), cols] - lse[h])
                ds = (p * (grads[pl.ds(at, RUN), cols] - dots[h])).astype(jnp.bfloat16)
                dv += contract(p.astype(jnp.bfloat16), gh[cols, :], 1, 0)
                dk += contract(ds, qh[cols, :], 1, 0)
                dqt[:, cols] += contract(key_cols, ds, 1, 0)
            dka[pl.ds(at, RUN), :] += dk
            dva[pl.ds(at, RUN), :] += dv
            return carry

        lax.fori_loop(0, run + 1, grad_step, 0)
        for h in range(heads):
            cols = slice(h * RUN, (h + 1) * RUN)
            dq_ref[rows, h * HD : (h + 1) * HD] = (dqt[:, cols] * scale).T.astype(jnp.bfloat16)
    half_head = HD // 2
    for b in range(slots * runs_per_slot):
        slot, part = b // runs_per_slot, b % runs_per_slot
        rows = slice(part * RUN, (part + 1) * RUN)
        at = pl.multiple_of(info_ref[b] * RUN, RUN)
        dk = dka[pl.ds(at, RUN), :] * scale
        dv = dva[pl.ds(at, RUN), :]
        low = jnp.concatenate([dk[:, :half_head], dv[:, :half_head]], axis=1)
        high = jnp.concatenate([dk[:, half_head:], dv[:, half_head:]], axis=1)
        keep_ref[slot, rows, :] = jnp.where(core == 0, low, high).astype(jnp.bfloat16)
        give_ref[slot, rows, :] = jnp.where(core == 0, high, low).astype(jnp.bfloat16)


def attention(info, queries, grad_output, mine, other):
    slots = mine[0].shape[0] * len(mine)
    count = slots * 2 * RUN
    heads = queries.shape[1] // HD
    wide = heads * RUN
    smem = pl.BlockSpec(memory_space=pltpu.SMEM)
    vmem = pl.BlockSpec(memory_space=pltpu.VMEM)
    shared = jax.ShapeDtypeStruct((slots, 2 * RUN, HD), jnp.bfloat16)
    pairs = heads * 2 * RUN * count // 2
    return pl.pallas_call(
        functools.partial(attention_kernel, heads),
        out_shape=(
            jax.ShapeDtypeStruct(queries.shape, jnp.bfloat16),
            shared,
            shared,
        ),
        in_specs=[smem, vmem, vmem, [vmem] * len(mine), [vmem] * len(other)],
        out_specs=(vmem, vmem, vmem),
        scratch_shapes=[
            pltpu.VMEM((count, HD), jnp.bfloat16),
            pltpu.VMEM((count, HD), jnp.bfloat16),
            pltpu.VMEM((HD, count), jnp.bfloat16),
            pltpu.VMEM((count, wide), jnp.float32),
            pltpu.VMEM((count, wide), jnp.float32),
            pltpu.VMEM((count, HD), jnp.float32),
            pltpu.VMEM((count, HD), jnp.float32),
            pltpu.VMEM((wide, HD), jnp.bfloat16),
            pltpu.VMEM((wide, HD), jnp.bfloat16),
            pltpu.VMEM((HD, wide), jnp.float32),
        ],
        compiler_params=pltpu.CompilerParams(vmem_limit_bytes=VMEM_BYTES),
        cost_estimate=pl.CostEstimate(
            flops=5 * 4 * pairs * HD, bytes_accessed=8 * 1024 * 1024, transcendentals=2 * pairs
        ),
    )(info, queries, grad_output, mine, other)


def turn_kernel(in_refs, out_ref):
    for dy, ref in enumerate(in_refs):
        for dx in range(2):
            tokens = ref.shape[1]
            at = (dx * len(in_refs) + dy) * tokens
            out_ref[:, at : at + tokens] = ref[dx].T


def turn(pieces):
    vmem = pl.BlockSpec(memory_space=pltpu.VMEM)
    sides, tokens, lanes = pieces[0].shape
    return pl.pallas_call(
        turn_kernel,
        out_shape=jax.ShapeDtypeStruct((lanes, len(pieces) * sides * tokens), jnp.bfloat16),
        in_specs=[[vmem] * len(pieces)],
        out_specs=vmem,
        compiler_params=pltpu.CompilerParams(vmem_limit_bytes=VMEM_BYTES),
        cost_estimate=pl.CostEstimate(flops=0, bytes_accessed=2 * 1024 * 1024, transcendentals=0),
    )(list(pieces))


def weight_kernel(last, place_ref, own_refs, other_refs, grad_refs, *rest):
    if last:
        (sum_ref, shared_refs, wq_ref, wk_ref, wv_ref, k_ref, v_ref,
         inputs, grads, sums, shared, in_sems, grad_sems, sum_sems, shared_sems, out_sems) = rest
    else:
        wq_ref, inputs, grads, sums, in_sems, grad_sems, out_sems = rest
    core, z = place_ref[0], place_ref[1]
    tall, across = own_refs[0].shape
    tokens = grad_refs[0].shape[0]
    side = across // 2
    sides = (1, 0) if last else (0,)
    grad_copies = [
        pltpu.make_async_copy(ref, grads.at[pl.ds(dy * tokens, tokens)], grad_sems.at[dy])
        for dy, ref in enumerate(grad_refs)
    ]
    for copy in grad_copies:
        copy.start()
    row, in_copies, sum_copies = [], {}, []
    for away in range(4):
        row.append(pl.multiple_of(lax.rem(z + away, 4) * 2 * tall, 2 * tall))
    if last:
        shared_copies = [
            pltpu.make_async_copy(
                shared_refs[dy].at[dx],
                shared.at[pl.ds((dx * 4 + dy) * tokens, tokens)],
                shared_sems.at[dx, dy],
            )
            for dx in range(2)
            for dy in range(4)
        ]
    for away in range(4):
        for n, dx in enumerate(sides):
            for which, ref in enumerate((own_refs[away], other_refs[away])):
                at = pl.multiple_of((core if which == 0 else 1 - core) * tall, tall)
                in_copies[away, n, which] = pltpu.make_async_copy(
                    ref.at[:, pl.ds(dx * side, side)],
                    inputs.at[away, n, pl.ds(at, tall)],
                    in_sems.at[away, n, which],
                )
                in_copies[away, n, which].start()
        if last:
            sum_copies.append(
                pltpu.make_async_copy(
                    sum_ref.at[pl.ds(row[away], 2 * tall)], sums.at[away], sum_sems.at[away]
                )
            )
            sum_copies[away].start()
            if away == 0:
                for copy in shared_copies:
                    copy.start()
    for copy in grad_copies:
        copy.wait()
    norm = 1.0 / math.sqrt(8 * tokens)
    out_copies = []
    for away in range(4):
        for which in range(2):
            in_copies[away, 0, which].wait()
        total = contract(inputs[away, 0], grads[...], 1, 0)
        if last:
            sum_copies[away].wait()
            total = (total + sums[away]) * norm
        sums[away] = total
        out_copies.append(
            pltpu.make_async_copy(
                sums.at[away], wq_ref.at[pl.ds(row[away], 2 * tall)], out_sems.at[away]
            )
        )
        out_copies[away].start()
        if last:
            if away == 0:
                for copy in shared_copies:
                    copy.wait()
            for which in range(2):
                in_copies[away, 1, which].wait()
            part = contract(inputs[away, 0], shared[side:], 1, 0)
            part += contract(inputs[away, 1], shared[:side], 1, 0)
            part = (part * norm).T
            half = part.shape[0] // 2
            wk_ref[:, pl.ds(row[away], 2 * tall)] = part[:half]
            wv_ref[:, pl.ds(row[away], 2 * tall)] = part[half:]
    if last:
        here = shared[:tokens].T
        k_ref[...] = here[: here.shape[0] // 2]
        v_ref[...] = here[here.shape[0] // 2 :]
    for copy in out_copies:
        copy.wait()


def weights(place, own, other, grads, total=None, shared=None):
    last = total is not None
    smem = pl.BlockSpec(memory_space=pltpu.SMEM)
    vmem = pl.BlockSpec(memory_space=pltpu.VMEM)
    hbm = pl.BlockSpec(memory_space=pl.ANY)
    tall, across = own[0].shape
    tokens, cols = grads[0].shape
    f32, bf16, sem = jnp.float32, jnp.bfloat16, pltpu.SemaphoreType.DMA
    wq = jax.ShapeDtypeStruct((8 * tall, cols), f32)
    narrow = jax.ShapeDtypeStruct((tall // 2, 8 * tall), f32)
    narrow_in = jax.ShapeDtypeStruct((tall // 2, tokens), bf16)
    sides = 2 if last else 1
    scratch = [
        pltpu.VMEM((4, sides, 2 * tall, across // 2), bf16),
        pltpu.VMEM((4 * tokens, cols), bf16),
        pltpu.VMEM((4, 2 * tall, cols), f32),
    ]
    if last:
        scratch += [pltpu.VMEM((across, tall), bf16)]
    scratch += [sem((4, sides, 2)), sem((4,))]
    if last:
        scratch += [sem((4,)), sem((2, 4))]
    scratch += [sem((4,))]
    return pl.pallas_call(
        functools.partial(weight_kernel, last),
        out_shape=(wq, narrow, narrow, narrow_in, narrow_in) if last else wq,
        in_specs=[smem, [hbm] * 4, [hbm] * 4, [hbm] * 4] + ([hbm, [hbm] * 4] if last else []),
        out_specs=(hbm, vmem, vmem, vmem, vmem) if last else hbm,
        scratch_shapes=scratch,
        compiler_params=pltpu.CompilerParams(vmem_limit_bytes=VMEM_BYTES),
        cost_estimate=pl.CostEstimate(
            flops=8 * tokens * cols * 8 * tall, bytes_accessed=10 * 1024 * 1024, transcendentals=0
        ),
    )(place, list(own), list(other), list(grads), *((total, list(shared)) if last else ()))


def local(layer_input, queries, key_vectors, value_vectors, grad_output, positions):
    group = lax.axis_index("dp")
    member, head, z = group % 2, group // 2, group // 4
    here = lax.axis_index("ctx")
    y, x_hi = here // 2, here % 2
    count = queries.shape[0]
    width = layer_input.shape[1] // 8
    slab = width // 8
    first = member == 0
    place = jnp.stack([member, z]).astype(jnp.int32)

    key_local = lax.dynamic_slice_in_dim(key_vectors, head * HD, HD, 1)
    value_local = lax.dynamic_slice_in_dim(value_vectors, head * HD, HD, 1)
    runs_here = (positions[::RUN] // RUN).astype(jnp.bfloat16)
    tail = jnp.broadcast_to(jnp.pad(runs_here, (0, HD - 2))[None], (16, HD))
    own = jnp.concatenate([jnp.where(first, key_local, value_local), tail], axis=0)
    column = jnp.stack([own] + by_source(*to_all_y(own)))
    start = (2 * z + member) * slab

    def block(dy, dx):
        target = ((y + dy) % 4) * 2 + (x_hi + dx) % 2
        return lax.dynamic_slice(layer_input, (0, target * width + start), (count, slab))

    from_x = swap_x(jnp.stack([block(dy, 1) for dy in range(4)]))
    partner_column = swap_x(column)
    column_other = swap_cores(column)
    pairs = [jnp.stack([block(dy, 0), from_x[dy]]) for dy in range(4)]
    pairs = [pairs[0]] + [along_y(pairs[dy], dy) for dy in range(1, 4)]
    partner_other = swap_cores(partner_column)
    info = jnp.concatenate(
        [
            column[:, count, :2].reshape(8).astype(jnp.int32),
            partner_column[:, count, :2].reshape(8).astype(jnp.int32),
            member.astype(jnp.int32)[None],
        ]
    )
    slab_own = turn(pairs)
    slab_back, slab_ahead = along_z(slab_own, 1), along_z(slab_own, 3)
    slab_far = along_z(slab_own, 2)
    own_other = swap_cores(slab_own)

    grad_query, keep, give = attention(
        info, queries, grad_output, [column, partner_column], [column_other, partner_other]
    )
    grad_query, keep, give, slab_back, slab_ahead, own_other = lax.optimization_barrier(
        (grad_query, keep, give, slab_back, slab_ahead, own_other)
    )

    give = swap_cores(give)
    back_other, ahead_other = swap_cores(slab_back), swap_cores(slab_ahead)
    summed = (keep.astype(jnp.float32) + give.astype(jnp.float32)).astype(jnp.bfloat16)
    summed = summed.reshape(2, 4, count, HD)
    from_partner = swap_x(grad_query)
    from_1, from_3 = along_y(grad_query, 1), along_y(grad_query, 3)
    rows_y = summed[:, 0].astype(jnp.float32)
    for dy in (1, 3, 2):
        rows_y = rows_y + along_y(summed[:, dy], -dy).astype(jnp.float32)
    rows_y = rows_y.astype(jnp.bfloat16)
    rows_y, from_partner, from_1, from_3, slab_far, back_other, ahead_other = lax.optimization_barrier(
        (rows_y, from_partner, from_1, from_3, slab_far, back_other, ahead_other)
    )
    both = (rows_y.astype(jnp.float32) + swap_x(rows_y).astype(jnp.float32)[::-1]).astype(jnp.bfloat16)
    far_other = swap_cores(slab_far)
    from_2 = along_y(grad_query, 2)
    other_1, other_3 = swap_x(from_1), swap_x(from_3)
    other_2 = along_y(from_partner, 2)
    shared = [both] + by_source(*to_all_y(both))

    slabs = [slab_own, slab_ahead, slab_far, slab_back]
    slabs_other = [own_other, ahead_other, far_other, back_other]
    partial = weights(place, slabs, slabs_other, [grad_query, from_1, from_2, from_3])
    grad_wq, grad_wk, grad_wv, grad_key, grad_value = weights(
        place, slabs, slabs_other, [from_partner, other_1, other_2, other_3], partial, shared
    )
    return grad_query, grad_key.T, grad_value.T, grad_wq, grad_wk.T, grad_wv.T


def solution(mesh):
    in_specs = (
        P("ctx", None),
        P("ctx", "dp"),
        P("ctx", None),
        P("ctx", None),
        P("ctx", "dp"),
        P("ctx"),
    )
    out_specs = (P("ctx", "dp"),) * 6
    return jax.shard_map(local, mesh=mesh, in_specs=in_specs, out_specs=out_specs, check_vma=False)
```

```python
import functools
import math

import jax
import jax.numpy as jnp
from jax import lax
from jax.experimental import pallas as pl
from jax.experimental.pallas import tpu as pltpu
from jax.sharding import PartitionSpec as P

HD = 128
QH = 64
KVH = 8
RUN = 256
LOW = -1e30
LOG2E = 1.4426950408889634
VMEM_BYTES = 60 * 1024 * 1024


def contract(left, right, left_dim, right_dim):
    return lax.dot_general(
        left, right, (((left_dim,), (right_dim,)), ((), ())), preferred_element_type=jnp.float32
    )


def along_y(value, step):
    return lax.ppermute(value, "ctx", [(i, (i + 2 * step) % 8) for i in range(8)])


def swap_x(value):
    return lax.ppermute(value, "ctx", [(i, i ^ 1) for i in range(8)])


def along_z(value, step):
    return lax.ppermute(value, "dp", [(i, (i + 4 * step) % 16) for i in range(16)])


def swap_cores(value):
    return lax.ppermute(value, "dp", [(i, i ^ 1) for i in range(16)])


def to_all_y(value):
    return [along_y(value, step) for step in (1, 3, 2)]


def by_source(one, three, two):
    return [one, two, three]


def attention_kernel(
    heads, info_ref, q_ref, g_ref, mine_refs, other_refs, dq_ref, dqh_ref, keep_ref, give_ref,
    ks, vs, kt, scores, grads, dka, dva, qh, gh, dqt,
):
    per_ref = mine_refs[0].shape[0]
    slots = per_ref * len(mine_refs)
    runs_per_slot = 2
    scale = 1.0 / math.sqrt(HD)
    core = info_ref[2 * slots]
    for b in range(slots * runs_per_slot):
        slot, part = b // runs_per_slot, b % runs_per_slot
        rows = slice(part * RUN, (part + 1) * RUN)
        at = pl.multiple_of(info_ref[b] * RUN, RUN)
        first = mine_refs[slot // per_ref][slot % per_ref, rows, :]
        second = other_refs[slot // per_ref][slot % per_ref, rows, :]
        key_block = jnp.where(core == 0, first, second)
        ks[pl.ds(at, RUN), :] = key_block
        kt[:, pl.ds(at, RUN)] = key_block.T
        vs[pl.ds(at, RUN), :] = jnp.where(core == 0, second, first)
    dka[...] = jnp.zeros_like(dka)
    dva[...] = jnp.zeros_like(dva)
    for half in range(2):
        run = info_ref[half]
        rows = slice(half * RUN, (half + 1) * RUN)
        for h in range(heads):
            qh[h * RUN : (h + 1) * RUN, :] = q_ref[rows, h * HD : (h + 1) * HD]
            gh[h * RUN : (h + 1) * RUN, :] = g_ref[rows, h * HD : (h + 1) * HD]

        def stat_step(j, state, diagonal):
            at = pl.multiple_of(j * RUN, RUN)
            key_block = ks[pl.ds(at, RUN), :]
            value_block = vs[pl.ds(at, RUN), :]
            new_state = []
            for h in range(heads):
                row_max, denom, weighted = state[h]
                cols = slice(h * RUN, (h + 1) * RUN)
                s = contract(key_block, qh[cols, :], 1, 1) * (scale * LOG2E)
                if diagonal:
                    key_at = lax.broadcasted_iota(jnp.int32, (RUN, RUN), 0)
                    query_at = lax.broadcasted_iota(jnp.int32, (RUN, RUN), 1)
                    s = jnp.where(key_at <= query_at, s, LOW)
                scores[pl.ds(at, RUN), cols] = s
                dp = contract(value_block, gh[cols, :], 1, 1)
                grads[pl.ds(at, RUN), cols] = dp
                s3 = s.reshape(RUN // 8, 8, RUN)
                dp3 = dp.reshape(RUN // 8, 8, RUN)
                new_max = jnp.maximum(row_max, jnp.max(s3, axis=0))
                fade = jnp.exp2(row_max - new_max)
                expo = jnp.exp2(s3 - new_max[None])
                if diagonal:
                    expo = jnp.where(s3 > 0.5 * LOW, expo, 0.0)
                new_state.append(
                    (
                        new_max,
                        denom * fade + jnp.sum(expo, axis=0),
                        weighted * fade + jnp.sum(expo * dp3, axis=0),
                    )
                )
            return tuple(new_state)

        zeros = jnp.zeros((8, RUN), jnp.float32)
        state = tuple((jnp.full((8, RUN), LOW, jnp.float32), zeros, zeros) for _ in range(heads))
        state = lax.fori_loop(0, run, lambda j, st: stat_step(j, st, False), state)
        state = stat_step(run, state, True)
        lse, dots = [], []
        for h in range(heads):
            row_max, denom, weighted = state[h]
            top = jnp.max(row_max, axis=0, keepdims=True)
            fade = jnp.exp2(row_max - top)
            total = jnp.sum(denom * fade, axis=0, keepdims=True)
            lse.append(top + jnp.log2(total))
            dots.append(jnp.sum(weighted * fade, axis=0, keepdims=True) / total)
        dqt[...] = jnp.zeros_like(dqt)

        def grad_step(j, carry):
            at = pl.multiple_of(j * RUN, RUN)
            key_cols = kt[:, pl.ds(at, RUN)]
            dk, dv = 0.0, 0.0
            for h in range(heads):
                cols = slice(h * RUN, (h + 1) * RUN)
                p = jnp.exp2(scores[pl.ds(at, RUN), cols] - lse[h])
                ds = (p * (grads[pl.ds(at, RUN), cols] - dots[h])).astype(jnp.bfloat16)
                dv += contract(p.astype(jnp.bfloat16), gh[cols, :], 1, 0)
                dk += contract(ds, qh[cols, :], 1, 0)
                dqt[:, cols] += contract(key_cols, ds, 1, 0)
            dka[pl.ds(at, RUN), :] += dk
            dva[pl.ds(at, RUN), :] += dv
            return carry

        lax.fori_loop(0, run + 1, grad_step, 0)
        for h in range(heads):
            cols = slice(h * RUN, (h + 1) * RUN)
            dq = (dqt[:, cols] * scale).T.astype(jnp.bfloat16)
            dq_ref[rows, h * HD : (h + 1) * HD] = dq
            dqh_ref[h, rows, :] = dq
    half_head = HD // 2
    for b in range(slots * runs_per_slot):
        slot, part = b // runs_per_slot, b % runs_per_slot
        rows = slice(part * RUN, (part + 1) * RUN)
        at = pl.multiple_of(info_ref[b] * RUN, RUN)
        dk = dka[pl.ds(at, RUN), :] * scale
        dv = dva[pl.ds(at, RUN), :]
        low = jnp.concatenate([dk[:, :half_head], dv[:, :half_head]], axis=1)
        high = jnp.concatenate([dk[:, half_head:], dv[:, half_head:]], axis=1)
        keep_ref[slot, rows, :] = jnp.where(core == 0, low, high).astype(jnp.bfloat16)
        give_ref[slot, rows, :] = jnp.where(core == 0, high, low).astype(jnp.bfloat16)


def attention(info, queries, grad_output, mine, other):
    slots = mine[0].shape[0] * len(mine)
    count = slots * 2 * RUN
    heads = queries.shape[1] // HD
    wide = heads * RUN
    smem = pl.BlockSpec(memory_space=pltpu.SMEM)
    vmem = pl.BlockSpec(memory_space=pltpu.VMEM)
    shared = jax.ShapeDtypeStruct((slots, 2 * RUN, HD), jnp.bfloat16)
    pairs = heads * 2 * RUN * count // 2
    return pl.pallas_call(
        functools.partial(attention_kernel, heads),
        out_shape=(
            jax.ShapeDtypeStruct(queries.shape, jnp.bfloat16),
            jax.ShapeDtypeStruct((heads, 2 * RUN, HD), jnp.bfloat16),
            shared,
            shared,
        ),
        in_specs=[smem, vmem, vmem, [vmem] * len(mine), [vmem] * len(other)],
        out_specs=(vmem, vmem, vmem, vmem),
        scratch_shapes=[
            pltpu.VMEM((count, HD), jnp.bfloat16),
            pltpu.VMEM((count, HD), jnp.bfloat16),
            pltpu.VMEM((HD, count), jnp.bfloat16),
            pltpu.VMEM((count, wide), jnp.float32),
            pltpu.VMEM((count, wide), jnp.float32),
            pltpu.VMEM((count, HD), jnp.float32),
            pltpu.VMEM((count, HD), jnp.float32),
            pltpu.VMEM((wide, HD), jnp.bfloat16),
            pltpu.VMEM((wide, HD), jnp.bfloat16),
            pltpu.VMEM((HD, wide), jnp.float32),
        ],
        compiler_params=pltpu.CompilerParams(vmem_limit_bytes=VMEM_BYTES),
        cost_estimate=pl.CostEstimate(
            flops=5 * 4 * pairs * HD, bytes_accessed=8 * 1024 * 1024, transcendentals=2 * pairs
        ),
    )(info, queries, grad_output, mine, other)


def turn_kernel(in_refs, out_ref):
    for dy, ref in enumerate(in_refs):
        for dx in range(2):
            tokens = ref.shape[1]
            at = (dx * len(in_refs) + dy) * tokens
            out_ref[:, at : at + tokens] = ref[dx].T


def turn(pieces):
    vmem = pl.BlockSpec(memory_space=pltpu.VMEM)
    sides, tokens, lanes = pieces[0].shape
    return pl.pallas_call(
        turn_kernel,
        out_shape=jax.ShapeDtypeStruct((lanes, len(pieces) * sides * tokens), jnp.bfloat16),
        in_specs=[[vmem] * len(pieces)],
        out_specs=vmem,
        compiler_params=pltpu.CompilerParams(vmem_limit_bytes=VMEM_BYTES),
        cost_estimate=pl.CostEstimate(flops=0, bytes_accessed=2 * 1024 * 1024, transcendentals=0),
    )(list(pieces))


EARLY = (0, 1, 3, 4)
LATE = (2, 5, 6, 7)


def consecutive(slots):
    spans = []
    for at, slot in enumerate(slots):
        if spans and spans[-1][1] + spans[-1][2] == slot:
            spans[-1][2] += 1
        else:
            spans.append([at, slot, 1])
    return spans


def weight_kernel(last, starts, place_ref, own_refs, other_refs, grad_refs, *rest):
    if last:
        (sum_ref, shared_refs, wq_ref, wk_ref, wv_ref, k_ref, v_ref,
         inputs, grads, sums, shared, in_sems, grad_sems, sum_sems, shared_sems, out_sems) = rest
    else:
        wq_ref, inputs, grads, sums, in_sems, grad_sems, out_sems = rest
    core, z = place_ref[0], place_ref[1]
    tall = own_refs[0].shape[0]
    tokens, wide = grad_refs[0].shape[1:]
    heads = grads.shape[1] // wide
    half = len(EARLY) * tokens
    order = LATE + EARLY if last else EARLY
    spans = consecutive(order)
    first_spans = sum(1 for at, _, _ in spans if at < len(EARLY))
    grad_copies = [
        pltpu.make_async_copy(
            ref.at[start + h],
            grads.at[pl.ds(i * tokens, tokens), pl.ds(h * wide, wide)],
            grad_sems.at[i, h],
        )
        for i, (ref, start) in enumerate(zip(grad_refs, starts))
        for h in range(heads)
    ]
    for copy in grad_copies:
        copy.start()
    row = [pl.multiple_of(lax.rem(z + away, 4) * 2 * tall, 2 * tall) for away in range(4)]
    in_copies, sum_copies, shared_copies, out_copies = {}, [], [], []
    if last:
        shared_copies = [
            pltpu.make_async_copy(
                shared_refs[slot % 4].at[slot // 4],
                shared.at[pl.ds(i * tokens, tokens)],
                shared_sems.at[i],
            )
            for i, slot in enumerate(order)
        ]
    for away in range(4):
        for n, (at, slot, many) in enumerate(spans):
            for which, ref in enumerate((own_refs[away], other_refs[away])):
                down = pl.multiple_of((core if which == 0 else 1 - core) * tall, tall)
                in_copies[away, n, which] = pltpu.make_async_copy(
                    ref.at[:, pl.ds(slot * tokens, many * tokens)],
                    inputs.at[away, pl.ds(down, tall), pl.ds(at * tokens, many * tokens)],
                    in_sems.at[away, n, which],
                )
                in_copies[away, n, which].start()
        if last:
            sum_copies.append(
                pltpu.make_async_copy(
                    sum_ref.at[pl.ds(row[away], 2 * tall)], sums.at[away], sum_sems.at[away]
                )
            )
            sum_copies[away].start()
            if away == 0:
                for copy in shared_copies:
                    copy.start()
    for copy in grad_copies:
        copy.wait()
    norm = 1.0 / math.sqrt(8 * tokens)
    for away in range(4):
        for n in range(first_spans):
            for which in range(2):
                in_copies[away, n, which].wait()
        total = contract(inputs[away, :, :half], grads[...], 1, 0)
        if last:
            sum_copies[away].wait()
            total = (total + sums[away]) * norm
        sums[away] = total
        out_copies.append(
            pltpu.make_async_copy(
                sums.at[away], wq_ref.at[pl.ds(row[away], 2 * tall)], out_sems.at[away]
            )
        )
        out_copies[away].start()
        if last:
            if away == 0:
                for copy in shared_copies:
                    copy.wait()
            for n in range(first_spans, len(spans)):
                for which in range(2):
                    in_copies[away, n, which].wait()
            part = (contract(inputs[away], shared[...], 1, 0) * norm).T
            wk_ref[:, pl.ds(row[away], 2 * tall)] = part[: tall // 2]
            wv_ref[:, pl.ds(row[away], 2 * tall)] = part[tall // 2 :]
    if last:
        at = order.index(0) * tokens
        here = shared[at : at + tokens].T
        k_ref[...] = here[: here.shape[0] // 2]
        v_ref[...] = here[here.shape[0] // 2 :]
    for copy in out_copies:
        copy.wait()


def weights(place, own, other, grads, heads, total=None, shared=None):
    last = total is not None
    smem = pl.BlockSpec(memory_space=pltpu.SMEM)
    vmem = pl.BlockSpec(memory_space=pltpu.VMEM)
    hbm = pl.BlockSpec(memory_space=pl.ANY)
    tall, across = own[0].shape
    tokens, wide = grads[0][0].shape[1:]
    cols = heads * wide
    f32, bf16, sem = jnp.float32, jnp.bfloat16, pltpu.SemaphoreType.DMA
    wq = jax.ShapeDtypeStruct((8 * tall, cols), f32)
    narrow = jax.ShapeDtypeStruct((tall // 2, 8 * tall), f32)
    narrow_in = jax.ShapeDtypeStruct((tall // 2, tokens), bf16)
    order = LATE + EARLY if last else EARLY
    scratch = [
        pltpu.VMEM((4, 2 * tall, len(order) * tokens), bf16),
        pltpu.VMEM((len(grads) * tokens, cols), bf16),
        pltpu.VMEM((4, 2 * tall, cols), f32),
    ]
    if last:
        scratch += [pltpu.VMEM((across, tall), bf16)]
    scratch += [sem((4, len(consecutive(order)), 2)), sem((len(grads), heads))]
    if last:
        scratch += [sem((4,)), sem((len(order),))]
    scratch += [sem((4,))]
    return pl.pallas_call(
        functools.partial(weight_kernel, last, tuple(start for _, start in grads)),
        out_shape=(wq, narrow, narrow, narrow_in, narrow_in) if last else wq,
        in_specs=[smem, [hbm] * 4, [hbm] * 4, [hbm] * 4] + ([hbm, [hbm] * 4] if last else []),
        out_specs=(hbm, vmem, vmem, vmem, vmem) if last else hbm,
        scratch_shapes=scratch,
        compiler_params=pltpu.CompilerParams(vmem_limit_bytes=VMEM_BYTES),
        cost_estimate=pl.CostEstimate(
            flops=8 * tokens * cols * 8 * tall, bytes_accessed=10 * 1024 * 1024, transcendentals=0
        ),
    )(
        place,
        list(own),
        list(other),
        [array for array, _ in grads],
        *((total, list(shared)) if last else ()),
    )


def local(layer_input, queries, key_vectors, value_vectors, grad_output, positions):
    group = lax.axis_index("dp")
    member, head, z = group % 2, group // 2, group // 4
    here = lax.axis_index("ctx")
    y, x_hi = here // 2, here % 2
    count = queries.shape[0]
    width = layer_input.shape[1] // 8
    slab = width // 8
    first = member == 0
    place = jnp.stack([member, z]).astype(jnp.int32)

    key_local = lax.dynamic_slice_in_dim(key_vectors, head * HD, HD, 1)
    value_local = lax.dynamic_slice_in_dim(value_vectors, head * HD, HD, 1)
    runs_here = (positions[::RUN] // RUN).astype(jnp.bfloat16)
    tail = jnp.broadcast_to(jnp.pad(runs_here, (0, HD - 2))[None], (16, HD))
    own = jnp.concatenate([jnp.where(first, key_local, value_local), tail], axis=0)
    column = jnp.stack([own] + by_source(*to_all_y(own)))
    start = (2 * z + member) * slab

    def block(dy, dx):
        target = ((y + dy) % 4) * 2 + (x_hi + dx) % 2
        return lax.dynamic_slice(layer_input, (0, target * width + start), (count, slab))

    from_x = swap_x(jnp.stack([block(dy, 1) for dy in range(4)]))
    partner_column = swap_x(column)
    column_other = swap_cores(column)
    pairs = [jnp.stack([block(dy, 0), from_x[dy]]) for dy in range(4)]
    moved = [along_y(pairs[dy], dy) for dy in range(1, 4)]
    partner_column, *moved = lax.optimization_barrier((partner_column, *moved))
    pairs = [pairs[0]] + moved
    partner_other = swap_cores(partner_column)
    info = jnp.concatenate(
        [
            column[:, count, :2].reshape(8).astype(jnp.int32),
            partner_column[:, count, :2].reshape(8).astype(jnp.int32),
            member.astype(jnp.int32)[None],
        ]
    )
    slab_own = turn(pairs)
    slab_back, slab_ahead = along_z(slab_own, 1), along_z(slab_own, 3)
    own_other = swap_cores(slab_own)

    grad_query, grad_heads, keep, give = attention(
        info, queries, grad_output, [column, partner_column], [column_other, partner_other]
    )
    heads = grad_heads.shape[0]
    grad_heads, keep, give, slab_own, slab_back, slab_ahead, own_other = lax.optimization_barrier(
        (grad_heads, keep, give, slab_own, slab_back, slab_ahead, own_other)
    )

    give, back_other = lax.optimization_barrier((swap_cores(give), swap_cores(slab_back)))
    summed = (keep.astype(jnp.float32) + give.astype(jnp.float32)).astype(jnp.bfloat16)
    summed = summed.reshape(2, 4, count, HD)
    from_1 = along_y(jnp.concatenate([grad_heads, summed[:, 3]]), 1)
    from_3 = along_y(jnp.concatenate([grad_heads, summed[:, 1]]), 3)
    rows_2 = along_y(summed[:, 2], 2)
    from_x = swap_x(grad_heads)
    slab_far = along_z(slab_own, 2)
    from_1, from_3, rows_2, from_x, slab_far = lax.optimization_barrier(
        (from_1, from_3, rows_2, from_x, slab_far)
    )
    rows_y = summed[:, 0].astype(jnp.float32)
    for term in (from_1[heads:], from_3[heads:], rows_2):
        rows_y = rows_y + term.astype(jnp.float32)
    rows_y = rows_y.astype(jnp.bfloat16)
    rows_x = swap_x(rows_y)
    from_x13 = swap_x(jnp.concatenate([from_1[:heads], from_3[:heads]]))
    from_2 = along_y(jnp.concatenate([grad_heads, from_x]), 2)
    far_other, ahead_other = swap_cores(slab_far), swap_cores(slab_ahead)
    rows_x, far_other, ahead_other = lax.optimization_barrier((rows_x, far_other, ahead_other))
    both = (rows_y.astype(jnp.float32) + rows_x.astype(jnp.float32)[::-1]).astype(jnp.bfloat16)
    shared = [both] + by_source(*to_all_y(both))

    slabs = [slab_own, slab_ahead, slab_far, slab_back]
    slabs_other = [own_other, ahead_other, far_other, back_other]
    early = [(grad_heads, 0), (from_1, 0), (from_3, 0), (from_x, 0)]
    late = [(from_2, 0), (from_x13, 0), (from_2, heads), (from_x13, heads)]
    partial = weights(place, slabs, slabs_other, early, heads)
    grad_wq, grad_wk, grad_wv, grad_key, grad_value = weights(
        place, slabs, slabs_other, late, heads, partial, shared
    )
    return grad_query, grad_key.T, grad_value.T, grad_wq, grad_wk.T, grad_wv.T


def solution(mesh):
    in_specs = (
        P("ctx", None),
        P("ctx", "dp"),
        P("ctx", None),
        P("ctx", None),
        P("ctx", "dp"),
        P("ctx"),
    )
    out_specs = (P("ctx", "dp"),) * 6
    return jax.shard_map(local, mesh=mesh, in_specs=in_specs, out_specs=out_specs, check_vma=False)
```

```python
import functools
import math

import jax
import jax.numpy as jnp
from jax import lax
from jax.experimental import pallas as pl
from jax.experimental.pallas import tpu as pltpu
from jax.sharding import PartitionSpec as P

HD = 128
QH = 64
KVH = 8
RUN = 256
LOW = -1e30
LOG2E = 1.4426950408889634
VMEM_BYTES = 60 * 1024 * 1024


def contract(left, right, left_dim, right_dim):
    return lax.dot_general(
        left, right, (((left_dim,), (right_dim,)), ((), ())), preferred_element_type=jnp.float32
    )


def along_y(value, step):
    return lax.ppermute(value, "ctx", [(i, (i + 2 * step) % 8) for i in range(8)])


def swap_x(value):
    return lax.ppermute(value, "ctx", [(i, i ^ 1) for i in range(8)])


def along_z(value, step):
    return lax.ppermute(value, "dp", [(i, (i + 4 * step) % 16) for i in range(16)])


def swap_cores(value):
    return lax.ppermute(value, "dp", [(i, i ^ 1) for i in range(16)])


def to_all_y(value):
    return [along_y(value, step) for step in (1, 3, 2)]


def by_source(one, three, two):
    return [one, two, three]


def attention_kernel(
    heads, info_ref, q_ref, g_ref, mine_refs, other_refs, dq_ref, dqh_ref, keep_ref, give_ref,
    ks, vs, kt, scores, grads, dka, dva, qh, gh, dqt,
):
    per_ref = mine_refs[0].shape[0]
    slots = per_ref * len(mine_refs)
    runs_per_slot = 2
    scale = 1.0 / math.sqrt(HD)
    core = info_ref[2 * slots]
    for b in range(slots * runs_per_slot):
        slot, part = b // runs_per_slot, b % runs_per_slot
        rows = slice(part * RUN, (part + 1) * RUN)
        at = pl.multiple_of(info_ref[b] * RUN, RUN)
        first = mine_refs[slot // per_ref][slot % per_ref, rows, :]
        second = other_refs[slot // per_ref][slot % per_ref, rows, :]
        key_block = jnp.where(core == 0, first, second)
        ks[pl.ds(at, RUN), :] = key_block
        kt[:, pl.ds(at, RUN)] = key_block.T
        vs[pl.ds(at, RUN), :] = jnp.where(core == 0, second, first)
    dka[...] = jnp.zeros_like(dka)
    dva[...] = jnp.zeros_like(dva)
    for half in range(2):
        run = info_ref[half]
        rows = slice(half * RUN, (half + 1) * RUN)
        for h in range(heads):
            qh[h * RUN : (h + 1) * RUN, :] = q_ref[rows, h * HD : (h + 1) * HD]
            gh[h * RUN : (h + 1) * RUN, :] = g_ref[rows, h * HD : (h + 1) * HD]

        def stat_step(j, state, diagonal):
            at = pl.multiple_of(j * RUN, RUN)
            key_block = ks[pl.ds(at, RUN), :]
            value_block = vs[pl.ds(at, RUN), :]
            new_state = []
            for h in range(heads):
                row_max, denom, weighted = state[h]
                cols = slice(h * RUN, (h + 1) * RUN)
                s = contract(key_block, qh[cols, :], 1, 1) * (scale * LOG2E)
                if diagonal:
                    key_at = lax.broadcasted_iota(jnp.int32, (RUN, RUN), 0)
                    query_at = lax.broadcasted_iota(jnp.int32, (RUN, RUN), 1)
                    s = jnp.where(key_at <= query_at, s, LOW)
                scores[pl.ds(at, RUN), cols] = s
                dp = contract(value_block, gh[cols, :], 1, 1)
                grads[pl.ds(at, RUN), cols] = dp
                s3 = s.reshape(RUN // 8, 8, RUN)
                dp3 = dp.reshape(RUN // 8, 8, RUN)
                new_max = jnp.maximum(row_max, jnp.max(s3, axis=0))
                fade = jnp.exp2(row_max - new_max)
                expo = jnp.exp2(s3 - new_max[None])
                if diagonal:
                    expo = jnp.where(s3 > 0.5 * LOW, expo, 0.0)
                new_state.append(
                    (
                        new_max,
                        denom * fade + jnp.sum(expo, axis=0),
                        weighted * fade + jnp.sum(expo * dp3, axis=0),
                    )
                )
            return tuple(new_state)

        zeros = jnp.zeros((8, RUN), jnp.float32)
        state = tuple((jnp.full((8, RUN), LOW, jnp.float32), zeros, zeros) for _ in range(heads))
        state = lax.fori_loop(0, run, lambda j, st: stat_step(j, st, False), state)
        state = stat_step(run, state, True)
        lse, dots = [], []
        for h in range(heads):
            row_max, denom, weighted = state[h]
            top = jnp.max(row_max, axis=0, keepdims=True)
            fade = jnp.exp2(row_max - top)
            total = jnp.sum(denom * fade, axis=0, keepdims=True)
            lse.append(top + jnp.log2(total))
            dots.append(jnp.sum(weighted * fade, axis=0, keepdims=True) / total)
        dqt[...] = jnp.zeros_like(dqt)

        def grad_step(j, carry):
            at = pl.multiple_of(j * RUN, RUN)
            key_cols = kt[:, pl.ds(at, RUN)]
            dk, dv = 0.0, 0.0
            for h in range(heads):
                cols = slice(h * RUN, (h + 1) * RUN)
                p = jnp.exp2(scores[pl.ds(at, RUN), cols] - lse[h])
                ds = (p * (grads[pl.ds(at, RUN), cols] - dots[h])).astype(jnp.bfloat16)
                dv += contract(p.astype(jnp.bfloat16), gh[cols, :], 1, 0)
                dk += contract(ds, qh[cols, :], 1, 0)
                dqt[:, cols] += contract(key_cols, ds, 1, 0)
            dka[pl.ds(at, RUN), :] += dk
            dva[pl.ds(at, RUN), :] += dv
            return carry

        lax.fori_loop(0, run + 1, grad_step, 0)
        for h in range(heads):
            cols = slice(h * RUN, (h + 1) * RUN)
            dq = (dqt[:, cols] * scale).T.astype(jnp.bfloat16)
            dq_ref[rows, h * HD : (h + 1) * HD] = dq
            dqh_ref[h, rows, :] = dq
    half_head = HD // 2
    for b in range(slots * runs_per_slot):
        slot, part = b // runs_per_slot, b % runs_per_slot
        rows = slice(part * RUN, (part + 1) * RUN)
        at = pl.multiple_of(info_ref[b] * RUN, RUN)
        dk = dka[pl.ds(at, RUN), :] * scale
        dv = dva[pl.ds(at, RUN), :]
        low = jnp.concatenate([dk[:, :half_head], dv[:, :half_head]], axis=1)
        high = jnp.concatenate([dk[:, half_head:], dv[:, half_head:]], axis=1)
        keep_ref[slot, rows, :] = jnp.where(core == 0, low, high).astype(jnp.bfloat16)
        give_ref[slot, rows, :] = jnp.where(core == 0, high, low).astype(jnp.bfloat16)


def attention(info, queries, grad_output, mine, other):
    slots = mine[0].shape[0] * len(mine)
    count = slots * 2 * RUN
    heads = queries.shape[1] // HD
    wide = heads * RUN
    smem = pl.BlockSpec(memory_space=pltpu.SMEM)
    vmem = pl.BlockSpec(memory_space=pltpu.VMEM)
    shared = jax.ShapeDtypeStruct((slots, 2 * RUN, HD), jnp.bfloat16)
    pairs = heads * 2 * RUN * count // 2
    return pl.pallas_call(
        functools.partial(attention_kernel, heads),
        out_shape=(
            jax.ShapeDtypeStruct(queries.shape, jnp.bfloat16),
            jax.ShapeDtypeStruct((heads, 2 * RUN, HD), jnp.bfloat16),
            shared,
            shared,
        ),
        in_specs=[smem, vmem, vmem, [vmem] * len(mine), [vmem] * len(other)],
        out_specs=(vmem, vmem, vmem, vmem),
        scratch_shapes=[
            pltpu.VMEM((count, HD), jnp.bfloat16),
            pltpu.VMEM((count, HD), jnp.bfloat16),
            pltpu.VMEM((HD, count), jnp.bfloat16),
            pltpu.VMEM((count, wide), jnp.float32),
            pltpu.VMEM((count, wide), jnp.float32),
            pltpu.VMEM((count, HD), jnp.float32),
            pltpu.VMEM((count, HD), jnp.float32),
            pltpu.VMEM((wide, HD), jnp.bfloat16),
            pltpu.VMEM((wide, HD), jnp.bfloat16),
            pltpu.VMEM((HD, wide), jnp.float32),
        ],
        compiler_params=pltpu.CompilerParams(vmem_limit_bytes=VMEM_BYTES),
        cost_estimate=pl.CostEstimate(
            flops=5 * 4 * pairs * HD, bytes_accessed=8 * 1024 * 1024, transcendentals=2 * pairs
        ),
    )(info, queries, grad_output, mine, other)


def turn_kernel(in_refs, out_ref):
    for dy, ref in enumerate(in_refs):
        for dx in range(2):
            tokens = ref.shape[1]
            at = (dx * len(in_refs) + dy) * tokens
            out_ref[:, at : at + tokens] = ref[dx].T


def turn(pieces):
    vmem = pl.BlockSpec(memory_space=pltpu.VMEM)
    sides, tokens, lanes = pieces[0].shape
    return pl.pallas_call(
        turn_kernel,
        out_shape=jax.ShapeDtypeStruct((lanes, len(pieces) * sides * tokens), jnp.bfloat16),
        in_specs=[[vmem] * len(pieces)],
        out_specs=vmem,
        compiler_params=pltpu.CompilerParams(vmem_limit_bytes=VMEM_BYTES),
        cost_estimate=pl.CostEstimate(flops=0, bytes_accessed=2 * 1024 * 1024, transcendentals=0),
    )(list(pieces))


EARLY = (0, 1, 3, 4)
LATE = (2, 5, 6, 7)


def consecutive(slots):
    spans = []
    for at, slot in enumerate(slots):
        if spans and spans[-1][1] + spans[-1][2] == slot:
            spans[-1][2] += 1
        else:
            spans.append([at, slot, 1])
    return spans


def weight_kernel(last, starts, place_ref, own_refs, other_refs, grad_refs, *rest):
    if last:
        (sum_ref, shared_refs, wq_ref, wk_ref, wv_ref, k_ref, v_ref,
         inputs, grads, sums, shared, in_sems, grad_sems, sum_sems, shared_sems, out_sems) = rest
    else:
        wq_ref, inputs, grads, sums, in_sems, grad_sems, out_sems = rest
    core, z = place_ref[0], place_ref[1]
    tall = own_refs[0].shape[0]
    tokens, wide = grad_refs[0].shape[1:]
    heads = grads.shape[1] // wide
    half = len(EARLY) * tokens
    order = LATE + EARLY if last else EARLY
    spans = consecutive(order)
    first_spans = sum(1 for at, _, _ in spans if at < len(EARLY))
    grad_copies = [
        pltpu.make_async_copy(
            ref.at[start + h],
            grads.at[pl.ds(i * tokens, tokens), pl.ds(h * wide, wide)],
            grad_sems.at[i, h],
        )
        for i, (ref, start) in enumerate(zip(grad_refs, starts))
        for h in range(heads)
    ]
    for copy in grad_copies:
        copy.start()
    row = [pl.multiple_of(lax.rem(z + away, 4) * 2 * tall, 2 * tall) for away in range(4)]
    in_copies, sum_copies, shared_copies, out_copies = {}, [], [], []
    if last:
        shared_copies = [
            pltpu.make_async_copy(
                shared_refs[slot % 4].at[slot // 4],
                shared.at[pl.ds(i * tokens, tokens)],
                shared_sems.at[i],
            )
            for i, slot in enumerate(order)
        ]
    for away in range(4):
        for n, (at, slot, many) in enumerate(spans):
            for which, ref in enumerate((own_refs[away], other_refs[away])):
                down = pl.multiple_of((core if which == 0 else 1 - core) * tall, tall)
                in_copies[away, n, which] = pltpu.make_async_copy(
                    ref.at[:, pl.ds(slot * tokens, many * tokens)],
                    inputs.at[away, pl.ds(down, tall), pl.ds(at * tokens, many * tokens)],
                    in_sems.at[away, n, which],
                )
                in_copies[away, n, which].start()
        if last:
            sum_copies.append(
                pltpu.make_async_copy(
                    sum_ref.at[pl.ds(row[away], 2 * tall)], sums.at[away], sum_sems.at[away]
                )
            )
            sum_copies[away].start()
            if away == 0:
                for copy in shared_copies:
                    copy.start()
    for copy in grad_copies:
        copy.wait()
    norm = 1.0 / math.sqrt(8 * tokens)
    for away in range(4):
        for n in range(first_spans):
            for which in range(2):
                in_copies[away, n, which].wait()
        total = contract(inputs[away, :, :half], grads[...], 1, 0)
        if last:
            sum_copies[away].wait()
            total = (total + sums[away]) * norm
        sums[away] = total
        out_copies.append(
            pltpu.make_async_copy(
                sums.at[away], wq_ref.at[pl.ds(row[away], 2 * tall)], out_sems.at[away]
            )
        )
        out_copies[away].start()
        if last:
            if away == 0:
                for copy in shared_copies:
                    copy.wait()
            for n in range(first_spans, len(spans)):
                for which in range(2):
                    in_copies[away, n, which].wait()
            part = (contract(inputs[away], shared[...], 1, 0) * norm).T
            wk_ref[:, pl.ds(row[away], 2 * tall)] = part[: tall // 2]
            wv_ref[:, pl.ds(row[away], 2 * tall)] = part[tall // 2 :]
    if last:
        at = order.index(0) * tokens
        here = shared[at : at + tokens].T
        k_ref[...] = here[: here.shape[0] // 2]
        v_ref[...] = here[here.shape[0] // 2 :]
    for copy in out_copies:
        copy.wait()


def weights(place, own, other, grads, heads, total=None, shared=None):
    last = total is not None
    smem = pl.BlockSpec(memory_space=pltpu.SMEM)
    vmem = pl.BlockSpec(memory_space=pltpu.VMEM)
    hbm = pl.BlockSpec(memory_space=pl.ANY)
    tall, across = own[0].shape
    tokens, wide = grads[0][0].shape[1:]
    cols = heads * wide
    f32, bf16, sem = jnp.float32, jnp.bfloat16, pltpu.SemaphoreType.DMA
    wq = jax.ShapeDtypeStruct((8 * tall, cols), f32)
    narrow = jax.ShapeDtypeStruct((tall // 2, 8 * tall), f32)
    narrow_in = jax.ShapeDtypeStruct((tall // 2, tokens), bf16)
    order = LATE + EARLY if last else EARLY
    scratch = [
        pltpu.VMEM((4, 2 * tall, len(order) * tokens), bf16),
        pltpu.VMEM((len(grads) * tokens, cols), bf16),
        pltpu.VMEM((4, 2 * tall, cols), f32),
    ]
    if last:
        scratch += [pltpu.VMEM((across, tall), bf16)]
    scratch += [sem((4, len(consecutive(order)), 2)), sem((len(grads), heads))]
    if last:
        scratch += [sem((4,)), sem((len(order),))]
    scratch += [sem((4,))]
    return pl.pallas_call(
        functools.partial(weight_kernel, last, tuple(start for _, start in grads)),
        out_shape=(wq, narrow, narrow, narrow_in, narrow_in) if last else wq,
        in_specs=[smem, [hbm] * 4, [hbm] * 4, [hbm] * 4] + ([hbm, [hbm] * 4] if last else []),
        out_specs=(hbm, vmem, vmem, vmem, vmem) if last else hbm,
        scratch_shapes=scratch,
        compiler_params=pltpu.CompilerParams(vmem_limit_bytes=VMEM_BYTES),
        cost_estimate=pl.CostEstimate(
            flops=8 * tokens * cols * 8 * tall, bytes_accessed=10 * 1024 * 1024, transcendentals=0
        ),
    )(
        place,
        list(own),
        list(other),
        [array for array, _ in grads],
        *((total, list(shared)) if last else ()),
    )


def local(layer_input, queries, key_vectors, value_vectors, grad_output, positions):
    group = lax.axis_index("dp")
    member, head, z = group % 2, group // 2, group // 4
    here = lax.axis_index("ctx")
    y, x_hi = here // 2, here % 2
    count = queries.shape[0]
    width = layer_input.shape[1] // 8
    slab = width // 8
    first = member == 0
    place = jnp.stack([member, z]).astype(jnp.int32)

    key_local = lax.dynamic_slice_in_dim(key_vectors, head * HD, HD, 1)
    value_local = lax.dynamic_slice_in_dim(value_vectors, head * HD, HD, 1)
    runs_here = (positions[::RUN] // RUN).astype(jnp.bfloat16)
    tail = jnp.broadcast_to(jnp.pad(runs_here, (0, HD - 2))[None], (16, HD))
    own = jnp.concatenate([jnp.where(first, key_local, value_local), tail], axis=0)
    column = jnp.stack([own] + by_source(*to_all_y(own)))
    start = (2 * z + member) * slab

    def block(dy, dx):
        target = ((y + dy) % 4) * 2 + (x_hi + dx) % 2
        return lax.dynamic_slice(layer_input, (0, target * width + start), (count, slab))

    from_x = swap_x(jnp.stack([block(dy, 1) for dy in range(4)]))
    partner_column = swap_x(column)
    column_other = swap_cores(column)
    pairs = [jnp.stack([block(dy, 0), from_x[dy]]) for dy in range(4)]
    moved = [along_y(pairs[dy], dy) for dy in range(1, 4)]
    info = column[:, count, :2].reshape(8).astype(jnp.int32)
    partner_column, info, place, kept, *moved = lax.optimization_barrier(
        (partner_column, info, place, pairs[0], *moved)
    )
    pairs = [kept] + moved
    partner_other = swap_cores(partner_column)
    partner_info = partner_column[:, count, :2].reshape(8).astype(jnp.int32)
    info = jnp.concatenate([info, partner_info, place[:1]])
    slab_own = turn(pairs)
    slab_back, slab_ahead = along_z(slab_own, 1), along_z(slab_own, 3)
    own_other = swap_cores(slab_own)

    grad_query, grad_heads, keep, give = attention(
        info, queries, grad_output, [column, partner_column], [column_other, partner_other]
    )
    heads = grad_heads.shape[0]
    grad_heads, keep, give, slab_own, slab_back, slab_ahead, own_other = lax.optimization_barrier(
        (grad_heads, keep, give, slab_own, slab_back, slab_ahead, own_other)
    )

    give, back_other = lax.optimization_barrier((swap_cores(give), swap_cores(slab_back)))
    summed = (keep.astype(jnp.float32) + give.astype(jnp.float32)).astype(jnp.bfloat16)
    summed = summed.reshape(2, 4, count, HD)
    from_1 = along_y(jnp.concatenate([grad_heads, summed[:, 3]]), 1)
    from_3 = along_y(jnp.concatenate([grad_heads, summed[:, 1]]), 3)
    rows_2 = along_y(summed[:, 2], 2)
    from_x = swap_x(grad_heads)
    slab_far = along_z(slab_own, 2)
    from_1, from_3, rows_2, from_x, slab_far = lax.optimization_barrier(
        (from_1, from_3, rows_2, from_x, slab_far)
    )
    rows_y = summed[:, 0].astype(jnp.float32)
    for term in (from_1[heads:], from_3[heads:], rows_2):
        rows_y = rows_y + term.astype(jnp.float32)
    rows_y = rows_y.astype(jnp.bfloat16)
    rows_x = swap_x(rows_y)
    from_2 = along_y(jnp.concatenate([grad_heads, from_x]), 2)
    far_other, ahead_other = swap_cores(slab_far), swap_cores(slab_ahead)
    to_x = jnp.concatenate([from_1[:heads], from_3[:heads]])
    rows_x, far_other, ahead_other, to_x = lax.optimization_barrier(
        (rows_x, far_other, ahead_other, to_x)
    )
    from_x13 = swap_x(to_x)
    both = (rows_y.astype(jnp.float32) + rows_x.astype(jnp.float32)[::-1]).astype(jnp.bfloat16)
    shared = [both] + by_source(*to_all_y(both))

    slabs = [slab_own, slab_ahead, slab_far, slab_back]
    slabs_other = [own_other, ahead_other, far_other, back_other]
    early = [(grad_heads, 0), (from_1, 0), (from_3, 0), (from_x, 0)]
    late = [(from_2, 0), (from_x13, 0), (from_2, heads), (from_x13, heads)]
    partial = weights(place, slabs, slabs_other, early, heads)
    grad_wq, grad_wk, grad_wv, grad_key, grad_value = weights(
        place, slabs, slabs_other, late, heads, partial, shared
    )
    return grad_query, grad_key.T, grad_value.T, grad_wq, grad_wk.T, grad_wv.T


def solution(mesh):
    in_specs = (
        P("ctx", None),
        P("ctx", "dp"),
        P("ctx", None),
        P("ctx", None),
        P("ctx", "dp"),
        P("ctx"),
    )
    out_specs = (P("ctx", "dp"),) * 6
    return jax.shard_map(local, mesh=mesh, in_specs=in_specs, out_specs=out_specs, check_vma=False)
```

```python
import functools
import math

import jax
import jax.numpy as jnp
from jax import lax
from jax.experimental import pallas as pl
from jax.experimental.pallas import tpu as pltpu
from jax.sharding import PartitionSpec as P

HD = 128
QH = 64
KVH = 8
RUN = 256
LOW = -1e30
LOG2E = 1.4426950408889634
VMEM_BYTES = 60 * 1024 * 1024


def contract(left, right, left_dim, right_dim):
    return lax.dot_general(
        left, right, (((left_dim,), (right_dim,)), ((), ())), preferred_element_type=jnp.float32
    )


def along_y(value, step):
    return lax.ppermute(value, "ctx", [(i, (i + 2 * step) % 8) for i in range(8)])


def swap_x(value):
    return lax.ppermute(value, "ctx", [(i, i ^ 1) for i in range(8)])


def along_z(value, step):
    return lax.ppermute(value, "dp", [(i, (i + 4 * step) % 16) for i in range(16)])


def swap_cores(value):
    return lax.ppermute(value, "dp", [(i, i ^ 1) for i in range(16)])


def to_all_y(value):
    return [along_y(value, step) for step in (1, 3, 2)]


def by_source(one, three, two):
    return [one, two, three]


def in_strides(count, step, state):
    done = 0
    for stride in (4, 2, 1):

        def several(j, state, done=done, stride=stride):
            for i in range(stride):
                state = step(done + j * stride + i, state)
            return state

        times = (count - done) // stride
        state = lax.fori_loop(0, times, several, state)
        done = done + times * stride
    return state


def attention_kernel(
    heads, info_ref, q_ref, g_ref, mine_refs, other_refs, dq_ref, dqh_ref, keep_ref, give_ref,
    ks, vs, kt, scores, grads, dka, dva, qh, gh, dqt,
):
    per_ref = mine_refs[0].shape[0]
    slots = per_ref * len(mine_refs)
    runs_per_slot = 2
    scale = 1.0 / math.sqrt(HD)
    core = info_ref[2 * slots]
    for b in range(slots * runs_per_slot):
        slot, part = b // runs_per_slot, b % runs_per_slot
        rows = slice(part * RUN, (part + 1) * RUN)
        at = pl.multiple_of(info_ref[b] * RUN, RUN)
        first = mine_refs[slot // per_ref][slot % per_ref, rows, :]
        second = other_refs[slot // per_ref][slot % per_ref, rows, :]
        key_block = jnp.where(core == 0, first, second)
        ks[pl.ds(at, RUN), :] = key_block
        kt[:, pl.ds(at, RUN)] = key_block.T
        vs[pl.ds(at, RUN), :] = jnp.where(core == 0, second, first)
    dka[...] = jnp.zeros_like(dka)
    dva[...] = jnp.zeros_like(dva)
    for half in range(2):
        run = info_ref[half]
        rows = slice(half * RUN, (half + 1) * RUN)
        for h in range(heads):
            qh[h * RUN : (h + 1) * RUN, :] = q_ref[rows, h * HD : (h + 1) * HD]
            gh[h * RUN : (h + 1) * RUN, :] = g_ref[rows, h * HD : (h + 1) * HD]

        def stat_step(j, state, diagonal):
            at = pl.multiple_of(j * RUN, RUN)
            key_block = ks[pl.ds(at, RUN), :]
            value_block = vs[pl.ds(at, RUN), :]
            new_state = []
            s_all = contract(key_block, qh[...], 1, 1) * (scale * LOG2E)
            dp_all = contract(value_block, gh[...], 1, 1)
            if diagonal:
                key_at = lax.broadcasted_iota(jnp.int32, (RUN, RUN), 0)
                query_at = lax.broadcasted_iota(jnp.int32, (RUN, RUN), 1)
                visible = jnp.concatenate([key_at <= query_at] * heads, axis=1)
                s_all = jnp.where(visible, s_all, LOW)
            scores[pl.ds(at, RUN), :] = s_all
            grads[pl.ds(at, RUN), :] = dp_all
            for h in range(heads):
                row_max, denom, weighted = state[h]
                cols = slice(h * RUN, (h + 1) * RUN)
                s3 = s_all[:, cols].reshape(RUN // 8, 8, RUN)
                dp3 = dp_all[:, cols].reshape(RUN // 8, 8, RUN)
                new_max = jnp.maximum(row_max, jnp.max(s3, axis=0))
                fade = jnp.exp2(row_max - new_max)
                expo = jnp.exp2(s3 - new_max[None])
                if diagonal:
                    expo = jnp.where(s3 > 0.5 * LOW, expo, 0.0)
                new_state.append(
                    (
                        new_max,
                        denom * fade + jnp.sum(expo, axis=0),
                        weighted * fade + jnp.sum(expo * dp3, axis=0),
                    )
                )
            return tuple(new_state)

        zeros = jnp.zeros((8, RUN), jnp.float32)
        state = tuple((jnp.full((8, RUN), LOW, jnp.float32), zeros, zeros) for _ in range(heads))
        state = in_strides(run, lambda j, st: stat_step(j, st, False), state)
        state = stat_step(run, state, True)
        lse, dots = [], []
        for h in range(heads):
            row_max, denom, weighted = state[h]
            top = jnp.max(row_max, axis=0, keepdims=True)
            fade = jnp.exp2(row_max - top)
            total = jnp.sum(denom * fade, axis=0, keepdims=True)
            lse.append(top + jnp.log2(total))
            dots.append(jnp.sum(weighted * fade, axis=0, keepdims=True) / total)
        dqt[...] = jnp.zeros_like(dqt)

        def grad_step(j, carry):
            at = pl.multiple_of(j * RUN, RUN)
            key_cols = kt[:, pl.ds(at, RUN)]
            probs_low, grad_scores = [], []
            for h in range(heads):
                cols = slice(h * RUN, (h + 1) * RUN)
                p = jnp.exp2(scores[pl.ds(at, RUN), cols] - lse[h])
                ds = p * (grads[pl.ds(at, RUN), cols] - dots[h])
                probs_low.append(p.astype(jnp.bfloat16))
                grad_scores.append(ds.astype(jnp.bfloat16))
            ds_all = jnp.concatenate(grad_scores, axis=1)
            dv = contract(jnp.concatenate(probs_low, axis=1), gh[...], 1, 0)
            dk = contract(ds_all, qh[...], 1, 0)
            dqt[...] += contract(key_cols, ds_all, 1, 0)
            dka[pl.ds(at, RUN), :] += dk
            dva[pl.ds(at, RUN), :] += dv
            return carry

        in_strides(run + 1, grad_step, 0)
        for h in range(heads):
            cols = slice(h * RUN, (h + 1) * RUN)
            dq = (dqt[:, cols] * scale).T.astype(jnp.bfloat16)
            dq_ref[rows, h * HD : (h + 1) * HD] = dq
            dqh_ref[h, rows, :] = dq
    half_head = HD // 2
    for b in range(slots * runs_per_slot):
        slot, part = b // runs_per_slot, b % runs_per_slot
        rows = slice(part * RUN, (part + 1) * RUN)
        at = pl.multiple_of(info_ref[b] * RUN, RUN)
        dk = dka[pl.ds(at, RUN), :] * scale
        dv = dva[pl.ds(at, RUN), :]
        low = jnp.concatenate([dk[:, :half_head], dv[:, :half_head]], axis=1)
        high = jnp.concatenate([dk[:, half_head:], dv[:, half_head:]], axis=1)
        keep_ref[slot, rows, :] = jnp.where(core == 0, low, high).astype(jnp.bfloat16)
        give_ref[slot, rows, :] = jnp.where(core == 0, high, low).astype(jnp.bfloat16)


def attention(info, queries, grad_output, mine, other):
    slots = mine[0].shape[0] * len(mine)
    count = slots * 2 * RUN
    heads = queries.shape[1] // HD
    wide = heads * RUN
    smem = pl.BlockSpec(memory_space=pltpu.SMEM)
    vmem = pl.BlockSpec(memory_space=pltpu.VMEM)
    shared = jax.ShapeDtypeStruct((slots, 2 * RUN, HD), jnp.bfloat16)
    pairs = heads * 2 * RUN * count // 2
    return pl.pallas_call(
        functools.partial(attention_kernel, heads),
        out_shape=(
            jax.ShapeDtypeStruct(queries.shape, jnp.bfloat16),
            jax.ShapeDtypeStruct((heads, 2 * RUN, HD), jnp.bfloat16),
            shared,
            shared,
        ),
        in_specs=[smem, vmem, vmem, [vmem] * len(mine), [vmem] * len(other)],
        out_specs=(vmem, vmem, vmem, vmem),
        scratch_shapes=[
            pltpu.VMEM((count, HD), jnp.bfloat16),
            pltpu.VMEM((count, HD), jnp.bfloat16),
            pltpu.VMEM((HD, count), jnp.bfloat16),
            pltpu.VMEM((count, wide), jnp.float32),
            pltpu.VMEM((count, wide), jnp.float32),
            pltpu.VMEM((count, HD), jnp.float32),
            pltpu.VMEM((count, HD), jnp.float32),
            pltpu.VMEM((wide, HD), jnp.bfloat16),
            pltpu.VMEM((wide, HD), jnp.bfloat16),
            pltpu.VMEM((HD, wide), jnp.float32),
        ],
        compiler_params=pltpu.CompilerParams(vmem_limit_bytes=VMEM_BYTES),
        cost_estimate=pl.CostEstimate(
            flops=5 * 4 * pairs * HD, bytes_accessed=8 * 1024 * 1024, transcendentals=2 * pairs
        ),
    )(info, queries, grad_output, mine, other)


def turn_kernel(in_refs, out_ref):
    for dy, ref in enumerate(in_refs):
        for dx in range(2):
            tokens = ref.shape[1]
            at = (dx * len(in_refs) + dy) * tokens
            out_ref[:, at : at + tokens] = ref[dx].T


def turn(pieces):
    vmem = pl.BlockSpec(memory_space=pltpu.VMEM)
    sides, tokens, lanes = pieces[0].shape
    return pl.pallas_call(
        turn_kernel,
        out_shape=jax.ShapeDtypeStruct((lanes, len(pieces) * sides * tokens), jnp.bfloat16),
        in_specs=[[vmem] * len(pieces)],
        out_specs=vmem,
        compiler_params=pltpu.CompilerParams(vmem_limit_bytes=VMEM_BYTES),
        cost_estimate=pl.CostEstimate(flops=0, bytes_accessed=2 * 1024 * 1024, transcendentals=0),
    )(list(pieces))


EARLY = (0, 1, 3, 4)
LATE = (2, 5, 6, 7)


def consecutive(slots):
    spans = []
    for at, slot in enumerate(slots):
        if spans and spans[-1][1] + spans[-1][2] == slot:
            spans[-1][2] += 1
        else:
            spans.append([at, slot, 1])
    return spans


def weight_kernel(last, starts, place_ref, own_refs, other_refs, grad_refs, *rest):
    if last:
        (sum_ref, shared_refs, wq_ref, wk_ref, wv_ref, k_ref, v_ref,
         inputs, grads, sums, shared, in_sems, grad_sems, sum_sems, shared_sems, out_sems) = rest
    else:
        wq_ref, inputs, grads, sums, in_sems, grad_sems, out_sems = rest
    core, z = place_ref[0], place_ref[1]
    tall = own_refs[0].shape[0]
    tokens, wide = grad_refs[0].shape[1:]
    heads = grads.shape[1] // wide
    slots = LATE if last else EARLY
    spans = [[0, 0, 8]] if last else consecutive(EARLY)
    grad_copies = [
        pltpu.make_async_copy(
            ref.at[start + h],
            grads.at[pl.ds(i * tokens, tokens), pl.ds(h * wide, wide)],
            grad_sems.at[i, h],
        )
        for i, (ref, start) in enumerate(zip(grad_refs, starts))
        for h in range(heads)
    ]
    for copy in grad_copies:
        copy.start()
    row = [pl.multiple_of(lax.rem(z + away, 4) * 2 * tall, 2 * tall) for away in range(4)]
    in_copies, sum_copies, shared_copies, out_copies = {}, [], [], []
    if last:
        shared_copies = [
            pltpu.make_async_copy(
                shared_refs[slot % 4].at[slot // 4],
                shared.at[pl.ds(slot * tokens, tokens)],
                shared_sems.at[slot],
            )
            for slot in range(8)
        ]
    for away in range(4):
        for n, (at, slot, many) in enumerate(spans):
            for which, ref in enumerate((own_refs[away], other_refs[away])):
                down = pl.multiple_of((core if which == 0 else 1 - core) * tall, tall)
                in_copies[away, n, which] = pltpu.make_async_copy(
                    ref.at[:, pl.ds(slot * tokens, many * tokens)],
                    inputs.at[away, pl.ds(down, tall), pl.ds(at * tokens, many * tokens)],
                    in_sems.at[away, n, which],
                )
        if last:
            sum_copies.append(
                pltpu.make_async_copy(
                    sum_ref.at[pl.ds(row[away], 2 * tall)], sums.at[away], sum_sems.at[away]
                )
            )

    def fetch(away):
        for n in range(len(spans)):
            for which in range(2):
                in_copies[away, n, which].start()
        if last:
            sum_copies[away].start()

    fetch(0)
    for copy in shared_copies:
        copy.start()
    fetch(1)
    for copy in grad_copies:
        copy.wait()
    norm = 1.0 / math.sqrt(8 * tokens)
    for away in range(4):
        for n in range(len(spans)):
            for which in range(2):
                in_copies[away, n, which].wait()
        if away + 2 < 4:
            fetch(away + 2)
        if last:
            total = sum(
                contract(
                    inputs[away, :, slot * tokens : (slot + many) * tokens],
                    grads[at * tokens : (at + many) * tokens],
                    1,
                    0,
                )
                for at, slot, many in consecutive(slots)
            )
        else:
            total = contract(inputs[away], grads[...], 1, 0)
        if last:
            sum_copies[away].wait()
            total = (total + sums[away]) * norm
        sums[away] = total
        out_copies.append(
            pltpu.make_async_copy(
                sums.at[away], wq_ref.at[pl.ds(row[away], 2 * tall)], out_sems.at[away]
            )
        )
        out_copies[away].start()
        if last:
            if away == 0:
                for copy in shared_copies:
                    copy.wait()
            part = (contract(inputs[away], shared[...], 1, 0) * norm).T
            wk_ref[:, pl.ds(row[away], 2 * tall)] = part[: tall // 2]
            wv_ref[:, pl.ds(row[away], 2 * tall)] = part[tall // 2 :]
    if last:
        here = shared[:tokens].T
        k_ref[...] = here[: here.shape[0] // 2]
        v_ref[...] = here[here.shape[0] // 2 :]
    for copy in out_copies:
        copy.wait()


def weights(place, own, other, grads, heads, total=None, shared=None):
    last = total is not None
    smem = pl.BlockSpec(memory_space=pltpu.SMEM)
    vmem = pl.BlockSpec(memory_space=pltpu.VMEM)
    hbm = pl.BlockSpec(memory_space=pl.ANY)
    tall, across = own[0].shape
    tokens, wide = grads[0][0].shape[1:]
    cols = heads * wide
    f32, bf16, sem = jnp.float32, jnp.bfloat16, pltpu.SemaphoreType.DMA
    wq = jax.ShapeDtypeStruct((8 * tall, cols), f32)
    narrow = jax.ShapeDtypeStruct((tall // 2, 8 * tall), f32)
    narrow_in = jax.ShapeDtypeStruct((tall // 2, tokens), bf16)
    spans = 1 if last else len(consecutive(EARLY))
    scratch = [
        pltpu.VMEM((4, 2 * tall, (8 if last else len(EARLY)) * tokens), bf16),
        pltpu.VMEM((len(grads) * tokens, cols), bf16),
        pltpu.VMEM((4, 2 * tall, cols), f32),
    ]
    if last:
        scratch += [pltpu.VMEM((across, tall), bf16)]
    scratch += [sem((4, spans, 2)), sem((len(grads), heads))]
    if last:
        scratch += [sem((4,)), sem((8,))]
    scratch += [sem((4,))]
    return pl.pallas_call(
        functools.partial(weight_kernel, last, tuple(start for _, start in grads)),
        out_shape=(wq, narrow, narrow, narrow_in, narrow_in) if last else wq,
        in_specs=[smem, [hbm] * 4, [hbm] * 4, [hbm] * 4] + ([hbm, [hbm] * 4] if last else []),
        out_specs=(hbm, vmem, vmem, vmem, vmem) if last else hbm,
        scratch_shapes=scratch,
        compiler_params=pltpu.CompilerParams(vmem_limit_bytes=VMEM_BYTES),
        cost_estimate=pl.CostEstimate(
            flops=8 * tokens * cols * 8 * tall, bytes_accessed=10 * 1024 * 1024, transcendentals=0
        ),
    )(
        place,
        list(own),
        list(other),
        [array for array, _ in grads],
        *((total, list(shared)) if last else ()),
    )


def local(layer_input, queries, key_vectors, value_vectors, grad_output, positions):
    group = lax.axis_index("dp")
    member, head, z = group % 2, group // 2, group // 4
    here = lax.axis_index("ctx")
    y, x_hi = here // 2, here % 2
    count = queries.shape[0]
    width = layer_input.shape[1] // 8
    slab = width // 8
    first = member == 0
    place = jnp.stack([member, z]).astype(jnp.int32)

    key_local = lax.dynamic_slice_in_dim(key_vectors, head * HD, HD, 1)
    value_local = lax.dynamic_slice_in_dim(value_vectors, head * HD, HD, 1)
    runs_here = (positions[::RUN] // RUN).astype(jnp.bfloat16)
    tail = jnp.broadcast_to(jnp.pad(runs_here, (0, HD - 2))[None], (16, HD))
    own = jnp.concatenate([jnp.where(first, key_local, value_local), tail], axis=0)
    column = jnp.stack([own] + by_source(*to_all_y(own)))
    start = (2 * z + member) * slab

    def block(dy, dx):
        target = ((y + dy) % 4) * 2 + (x_hi + dx) % 2
        return lax.dynamic_slice(layer_input, (0, target * width + start), (count, slab))

    from_x = swap_x(jnp.stack([block(dy, 1) for dy in range(4)]))
    partner_column = swap_x(column)
    column_other = swap_cores(column)
    pairs = [jnp.stack([block(dy, 0), from_x[dy]]) for dy in range(4)]
    moved = [along_y(pairs[dy], dy) for dy in range(1, 4)]
    info = column[:, count, :2].reshape(8).astype(jnp.int32)
    partner_column, info, place, kept, *moved = lax.optimization_barrier(
        (partner_column, info, place, pairs[0], *moved)
    )
    pairs = [kept] + moved
    partner_other = swap_cores(partner_column)
    partner_info = partner_column[:, count, :2].reshape(8).astype(jnp.int32)
    info = jnp.concatenate([info, partner_info, place[:1]])
    slab_own = turn(pairs)
    slab_back, slab_ahead = along_z(slab_own, 1), along_z(slab_own, 3)
    own_other = swap_cores(slab_own)

    grad_query, grad_heads, keep, give = attention(
        info, queries, grad_output, [column, partner_column], [column_other, partner_other]
    )
    heads = grad_heads.shape[0]
    grad_heads, keep, give, slab_own, slab_back, slab_ahead, own_other = lax.optimization_barrier(
        (grad_heads, keep, give, slab_own, slab_back, slab_ahead, own_other)
    )

    give, back_other = lax.optimization_barrier((swap_cores(give), swap_cores(slab_back)))
    summed = (keep.astype(jnp.float32) + give.astype(jnp.float32)).astype(jnp.bfloat16)
    summed = summed.reshape(2, 4, count, HD)
    from_1 = along_y(jnp.concatenate([grad_heads, summed[:, 3]]), 1)
    from_3 = along_y(jnp.concatenate([grad_heads, summed[:, 1]]), 3)
    rows_2 = along_y(summed[:, 2], 2)
    from_x = swap_x(grad_heads)
    slab_far = along_z(slab_own, 2)
    from_1, from_3, rows_2, from_x, slab_far = lax.optimization_barrier(
        (from_1, from_3, rows_2, from_x, slab_far)
    )
    rows_y = summed[:, 0].astype(jnp.float32)
    for term in (from_1[heads:], from_3[heads:], rows_2):
        rows_y = rows_y + term.astype(jnp.float32)
    rows_y = rows_y.astype(jnp.bfloat16)
    rows_x = swap_x(rows_y)
    from_2 = along_y(jnp.concatenate([grad_heads, from_x]), 2)
    far_other, ahead_other = swap_cores(slab_far), swap_cores(slab_ahead)
    to_x = jnp.concatenate([from_1[:heads], from_3[:heads]])
    rows_x, far_other, ahead_other, to_x = lax.optimization_barrier(
        (rows_x, far_other, ahead_other, to_x)
    )
    from_x13 = swap_x(to_x)
    both = (rows_y.astype(jnp.float32) + rows_x.astype(jnp.float32)[::-1]).astype(jnp.bfloat16)
    shared = [both] + by_source(*to_all_y(both))

    slabs = [slab_own, slab_ahead, slab_far, slab_back]
    slabs_other = [own_other, ahead_other, far_other, back_other]
    early = [(grad_heads, 0), (from_1, 0), (from_3, 0), (from_x, 0)]
    late = [(from_2, 0), (from_x13, 0), (from_2, heads), (from_x13, heads)]
    partial = weights(place, slabs, slabs_other, early, heads)
    grad_wq, grad_wk, grad_wv, grad_key, grad_value = weights(
        place, slabs, slabs_other, late, heads, partial, shared
    )
    return grad_query, grad_key.T, grad_value.T, grad_wq, grad_wk.T, grad_wv.T


def solution(mesh):
    in_specs = (
        P("ctx", None),
        P("ctx", "dp"),
        P("ctx", None),
        P("ctx", None),
        P("ctx", "dp"),
        P("ctx"),
    )
    out_specs = (P("ctx", "dp"),) * 6
    return jax.shard_map(local, mesh=mesh, in_specs=in_specs, out_specs=out_specs, check_vma=False)
```

```python
import functools
import math

import jax
import jax.numpy as jnp
from jax import lax
from jax.experimental import pallas as pl
from jax.experimental.pallas import tpu as pltpu
from jax.sharding import PartitionSpec as P

HD = 128
QH = 64
KVH = 8
RUN = 256
LOW = -1e30
LOG2E = 1.4426950408889634
VMEM_BYTES = 60 * 1024 * 1024


def contract(left, right, left_dim, right_dim):
    return lax.dot_general(
        left, right, (((left_dim,), (right_dim,)), ((), ())), preferred_element_type=jnp.float32
    )


def along_y(value, step):
    return lax.ppermute(value, "ctx", [(i, (i + 2 * step) % 8) for i in range(8)])


def swap_x(value):
    return lax.ppermute(value, "ctx", [(i, i ^ 1) for i in range(8)])


def along_z(value, step):
    return lax.ppermute(value, "dp", [(i, (i + 4 * step) % 16) for i in range(16)])


def swap_cores(value):
    return lax.ppermute(value, "dp", [(i, i ^ 1) for i in range(16)])


def to_all_y(value):
    return [along_y(value, step) for step in (1, 3, 2)]


def by_source(one, three, two):
    return [one, two, three]


def in_strides(count, step, state):
    done = 0
    for stride in (4, 2, 1):

        def several(j, state, done=done, stride=stride):
            for i in range(stride):
                state = step(done + j * stride + i, state)
            return state

        times = (count - done) // stride
        state = lax.fori_loop(0, times, several, state)
        done = done + times * stride
    return state


def attention_kernel(
    heads, info_ref, q_ref, g_ref, mine_refs, other_refs, dq_ref, dqh_ref, keep_ref, give_ref,
    ks, vs, kt, scores, grads, dka, dva, qh, gh, dqt,
):
    per_ref = mine_refs[0].shape[0]
    slots = per_ref * len(mine_refs)
    runs_per_slot = 2
    scale = 1.0 / math.sqrt(HD)
    core = info_ref[2 * slots]
    for b in range(slots * runs_per_slot):
        slot, part = b // runs_per_slot, b % runs_per_slot
        rows = slice(part * RUN, (part + 1) * RUN)
        at = pl.multiple_of(info_ref[b] * RUN, RUN)
        first = mine_refs[slot // per_ref][slot % per_ref, rows, :]
        second = other_refs[slot // per_ref][slot % per_ref, rows, :]
        key_block = jnp.where(core == 0, first, second)
        ks[pl.ds(at, RUN), :] = key_block
        kt[:, pl.ds(at, RUN)] = key_block.T
        vs[pl.ds(at, RUN), :] = jnp.where(core == 0, second, first)
    dka[...] = jnp.zeros_like(dka)
    dva[...] = jnp.zeros_like(dva)
    for half in range(2):
        run = info_ref[half]
        rows = slice(half * RUN, (half + 1) * RUN)
        for h in range(heads):
            qh[h * RUN : (h + 1) * RUN, :] = q_ref[rows, h * HD : (h + 1) * HD]
            gh[h * RUN : (h + 1) * RUN, :] = g_ref[rows, h * HD : (h + 1) * HD]

        def stat_step(j, state, diagonal):
            at = pl.multiple_of(j * RUN, RUN)
            key_block = ks[pl.ds(at, RUN), :]
            value_block = vs[pl.ds(at, RUN), :]
            new_state = []
            s_all = contract(key_block, qh[...], 1, 1) * (scale * LOG2E)
            dp_all = contract(value_block, gh[...], 1, 1)
            if diagonal:
                key_at = lax.broadcasted_iota(jnp.int32, (RUN, RUN), 0)
                query_at = lax.broadcasted_iota(jnp.int32, (RUN, RUN), 1)
                visible = jnp.concatenate([key_at <= query_at] * heads, axis=1)
                s_all = jnp.where(visible, s_all, LOW)
            scores[pl.ds(at, RUN), :] = s_all
            grads[pl.ds(at, RUN), :] = dp_all
            for h in range(heads):
                row_max, denom, weighted = state[h]
                cols = slice(h * RUN, (h + 1) * RUN)
                s3 = s_all[:, cols].reshape(RUN // 8, 8, RUN)
                dp3 = dp_all[:, cols].reshape(RUN // 8, 8, RUN)
                new_max = jnp.maximum(row_max, jnp.max(s3, axis=0))
                fade = jnp.exp2(row_max - new_max)
                expo = jnp.exp2(s3 - new_max[None])
                if diagonal:
                    expo = jnp.where(s3 > 0.5 * LOW, expo, 0.0)
                new_state.append(
                    (
                        new_max,
                        denom * fade + jnp.sum(expo, axis=0),
                        weighted * fade + jnp.sum(expo * dp3, axis=0),
                    )
                )
            return tuple(new_state)

        zeros = jnp.zeros((8, RUN), jnp.float32)
        state = tuple((jnp.full((8, RUN), LOW, jnp.float32), zeros, zeros) for _ in range(heads))
        state = in_strides(run, lambda j, st: stat_step(j, st, False), state)
        state = stat_step(run, state, True)
        lse, dots = [], []
        for h in range(heads):
            row_max, denom, weighted = state[h]
            top = jnp.max(row_max, axis=0, keepdims=True)
            fade = jnp.exp2(row_max - top)
            total = jnp.sum(denom * fade, axis=0, keepdims=True)
            lse.append(top + jnp.log2(total))
            dots.append(jnp.sum(weighted * fade, axis=0, keepdims=True) / total)
        dqt[...] = jnp.zeros_like(dqt)

        def grad_step(j, carry):
            at = pl.multiple_of(j * RUN, RUN)
            key_cols = kt[:, pl.ds(at, RUN)]
            probs_low, grad_scores = [], []
            for h in range(heads):
                cols = slice(h * RUN, (h + 1) * RUN)
                p = jnp.exp2(scores[pl.ds(at, RUN), cols] - lse[h])
                ds = p * (grads[pl.ds(at, RUN), cols] - dots[h])
                probs_low.append(p.astype(jnp.bfloat16))
                grad_scores.append(ds.astype(jnp.bfloat16))
            ds_all = jnp.concatenate(grad_scores, axis=1)
            dv = contract(jnp.concatenate(probs_low, axis=1), gh[...], 1, 0)
            dk = contract(ds_all, qh[...], 1, 0)
            dqt[...] += contract(key_cols, ds_all, 1, 0)
            dka[pl.ds(at, RUN), :] += dk
            dva[pl.ds(at, RUN), :] += dv
            return carry

        in_strides(run + 1, grad_step, 0)
        for h in range(heads):
            cols = slice(h * RUN, (h + 1) * RUN)
            dq = (dqt[:, cols] * scale).T.astype(jnp.bfloat16)
            dq_ref[rows, h * HD : (h + 1) * HD] = dq
            dqh_ref[h, rows, :] = dq
    half_head = HD // 2
    for b in range(slots * runs_per_slot):
        slot, part = b // runs_per_slot, b % runs_per_slot
        rows = slice(part * RUN, (part + 1) * RUN)
        at = pl.multiple_of(info_ref[b] * RUN, RUN)
        dk = dka[pl.ds(at, RUN), :] * scale
        dv = dva[pl.ds(at, RUN), :]
        low = jnp.concatenate([dk[:, :half_head], dv[:, :half_head]], axis=1)
        high = jnp.concatenate([dk[:, half_head:], dv[:, half_head:]], axis=1)
        keep_ref[slot, rows, :] = jnp.where(core == 0, low, high).astype(jnp.bfloat16)
        give_ref[slot, rows, :] = jnp.where(core == 0, high, low).astype(jnp.bfloat16)


def attention(info, queries, grad_output, mine, other):
    slots = mine[0].shape[0] * len(mine)
    count = slots * 2 * RUN
    heads = queries.shape[1] // HD
    wide = heads * RUN
    smem = pl.BlockSpec(memory_space=pltpu.SMEM)
    vmem = pl.BlockSpec(memory_space=pltpu.VMEM)
    shared = jax.ShapeDtypeStruct((slots, 2 * RUN, HD), jnp.bfloat16)
    pairs = heads * 2 * RUN * count // 2
    return pl.pallas_call(
        functools.partial(attention_kernel, heads),
        out_shape=(
            jax.ShapeDtypeStruct(queries.shape, jnp.bfloat16),
            jax.ShapeDtypeStruct((heads, 2 * RUN, HD), jnp.bfloat16),
            shared,
            shared,
        ),
        in_specs=[smem, vmem, vmem, [vmem] * len(mine), [vmem] * len(other)],
        out_specs=(vmem, vmem, vmem, vmem),
        scratch_shapes=[
            pltpu.VMEM((count, HD), jnp.bfloat16),
            pltpu.VMEM((count, HD), jnp.bfloat16),
            pltpu.VMEM((HD, count), jnp.bfloat16),
            pltpu.VMEM((count, wide), jnp.float32),
            pltpu.VMEM((count, wide), jnp.float32),
            pltpu.VMEM((count, HD), jnp.float32),
            pltpu.VMEM((count, HD), jnp.float32),
            pltpu.VMEM((wide, HD), jnp.bfloat16),
            pltpu.VMEM((wide, HD), jnp.bfloat16),
            pltpu.VMEM((HD, wide), jnp.float32),
        ],
        compiler_params=pltpu.CompilerParams(vmem_limit_bytes=VMEM_BYTES),
        cost_estimate=pl.CostEstimate(
            flops=5 * 4 * pairs * HD, bytes_accessed=8 * 1024 * 1024, transcendentals=2 * pairs
        ),
    )(info, queries, grad_output, mine, other)


def turn_kernel(in_refs, out_ref):
    for dy, ref in enumerate(in_refs):
        for dx in range(2):
            tokens = ref.shape[1]
            at = (dx * len(in_refs) + dy) * tokens
            out_ref[:, at : at + tokens] = ref[dx].T


def turn(pieces):
    vmem = pl.BlockSpec(memory_space=pltpu.VMEM)
    sides, tokens, lanes = pieces[0].shape
    return pl.pallas_call(
        turn_kernel,
        out_shape=jax.ShapeDtypeStruct((lanes, len(pieces) * sides * tokens), jnp.bfloat16),
        in_specs=[[vmem] * len(pieces)],
        out_specs=vmem,
        compiler_params=pltpu.CompilerParams(vmem_limit_bytes=VMEM_BYTES),
        cost_estimate=pl.CostEstimate(flops=0, bytes_accessed=2 * 1024 * 1024, transcendentals=0),
    )(list(pieces))


EARLY = (0, 1, 3, 4)
LATE = (2, 5, 6, 7)


def consecutive(slots):
    spans = []
    for at, slot in enumerate(slots):
        if spans and spans[-1][1] + spans[-1][2] == slot:
            spans[-1][2] += 1
        else:
            spans.append([at, slot, 1])
    return spans


def weight_kernel(last, starts, place_ref, own_refs, other_refs, grad_refs, *rest):
    if last:
        (sum_ref, shared_refs, wq_ref, wk_ref, wv_ref, k_ref, v_ref,
         inputs, grads, sums, shared, in_sems, grad_sems, sum_sems, shared_sems, out_sems) = rest
    else:
        wq_ref, inputs, grads, sums, in_sems, grad_sems, out_sems = rest
    core, z = place_ref[0], place_ref[1]
    tall = own_refs[0].shape[0]
    tokens, wide = grad_refs[0].shape[1:]
    heads = grads.shape[1] // wide
    slots = LATE if last else EARLY
    spans = [[0, 0, 8]] if last else consecutive(EARLY)
    grad_copies = [
        pltpu.make_async_copy(
            ref.at[start + h],
            grads.at[pl.ds(i * tokens, tokens), pl.ds(h * wide, wide)],
            grad_sems.at[i, h],
        )
        for i, (ref, start) in enumerate(zip(grad_refs, starts))
        for h in range(heads)
    ]
    for copy in grad_copies:
        copy.start()
    row = [pl.multiple_of(lax.rem(z + away, 4) * 2 * tall, 2 * tall) for away in range(4)]
    in_copies, sum_copies, shared_copies, out_copies = {}, [], [], []
    if last:
        shared_copies = [
            pltpu.make_async_copy(
                shared_refs[slot % 4].at[slot // 4],
                shared.at[pl.ds(slot * tokens, tokens)],
                shared_sems.at[slot],
            )
            for slot in range(8)
        ]
    for away in range(4):
        for n, (at, slot, many) in enumerate(spans):
            for which, ref in enumerate((own_refs[away], other_refs[away])):
                down = pl.multiple_of((core if which == 0 else 1 - core) * tall, tall)
                in_copies[away, n, which] = pltpu.make_async_copy(
                    ref.at[:, pl.ds(slot * tokens, many * tokens)],
                    inputs.at[away, pl.ds(down, tall), pl.ds(at * tokens, many * tokens)],
                    in_sems.at[away, n, which],
                )
        if last:
            sum_copies.append(
                pltpu.make_async_copy(
                    sum_ref.at[pl.ds(row[away], 2 * tall)], sums.at[away], sum_sems.at[away]
                )
            )

    def fetch(away):
        for n in range(len(spans)):
            for which in range(2):
                in_copies[away, n, which].start()
        if last:
            sum_copies[away].start()

    fetch(0)
    for copy in shared_copies:
        copy.start()
    fetch(1)
    for copy in grad_copies:
        copy.wait()
    norm = 1.0 / math.sqrt(8 * tokens)
    for away in range(4):
        for n in range(len(spans)):
            for which in range(2):
                in_copies[away, n, which].wait()
        if away + 2 < 4:
            fetch(away + 2)
        if last:
            total = sum(
                contract(
                    inputs[away, :, slot * tokens : (slot + many) * tokens],
                    grads[at * tokens : (at + many) * tokens],
                    1,
                    0,
                )
                for at, slot, many in consecutive(slots)
            )
        else:
            total = contract(inputs[away], grads[...], 1, 0)
        if last:
            sum_copies[away].wait()
            total = (total + sums[away]) * norm
        sums[away] = total
        out_copies.append(
            pltpu.make_async_copy(
                sums.at[away], wq_ref.at[pl.ds(row[away], 2 * tall)], out_sems.at[away]
            )
        )
        out_copies[away].start()
        if last:
            if away == 0:
                for copy in shared_copies:
                    copy.wait()
            part = (contract(inputs[away], shared[...], 1, 0) * norm).T
            wk_ref[:, pl.ds(row[away], 2 * tall)] = part[: tall // 2]
            wv_ref[:, pl.ds(row[away], 2 * tall)] = part[tall // 2 :]
    if last:
        here = shared[:tokens].T
        k_ref[...] = here[: here.shape[0] // 2]
        v_ref[...] = here[here.shape[0] // 2 :]
    for copy in out_copies:
        copy.wait()


def weights(place, own, other, grads, heads, total=None, shared=None):
    last = total is not None
    smem = pl.BlockSpec(memory_space=pltpu.SMEM)
    vmem = pl.BlockSpec(memory_space=pltpu.VMEM)
    hbm = pl.BlockSpec(memory_space=pl.ANY)
    tall, across = own[0].shape
    tokens, wide = grads[0][0].shape[1:]
    cols = heads * wide
    f32, bf16, sem = jnp.float32, jnp.bfloat16, pltpu.SemaphoreType.DMA
    wq = jax.ShapeDtypeStruct((8 * tall, cols), f32)
    narrow = jax.ShapeDtypeStruct((tall // 2, 8 * tall), f32)
    narrow_in = jax.ShapeDtypeStruct((tall // 2, tokens), bf16)
    spans = 1 if last else len(consecutive(EARLY))
    scratch = [
        pltpu.VMEM((4, 2 * tall, (8 if last else len(EARLY)) * tokens), bf16),
        pltpu.VMEM((len(grads) * tokens, cols), bf16),
        pltpu.VMEM((4, 2 * tall, cols), f32),
    ]
    if last:
        scratch += [pltpu.VMEM((across, tall), bf16)]
    scratch += [sem((4, spans, 2)), sem((len(grads), heads))]
    if last:
        scratch += [sem((4,)), sem((8,))]
    scratch += [sem((4,))]
    return pl.pallas_call(
        functools.partial(weight_kernel, last, tuple(start for _, start in grads)),
        out_shape=(wq, narrow, narrow, narrow_in, narrow_in) if last else wq,
        in_specs=[smem, [hbm] * 4, [hbm] * 4, [hbm] * 4] + ([hbm, [hbm] * 4] if last else []),
        out_specs=(hbm, vmem, vmem, vmem, vmem) if last else hbm,
        scratch_shapes=scratch,
        compiler_params=pltpu.CompilerParams(vmem_limit_bytes=VMEM_BYTES),
        cost_estimate=pl.CostEstimate(
            flops=8 * tokens * cols * 8 * tall, bytes_accessed=10 * 1024 * 1024, transcendentals=0
        ),
    )(
        place,
        list(own),
        list(other),
        [array for array, _ in grads],
        *((total, list(shared)) if last else ()),
    )


def local(layer_input, queries, key_vectors, value_vectors, grad_output, positions):
    group = lax.axis_index("dp")
    member, head, z = group % 2, group // 2, group // 4
    here = lax.axis_index("ctx")
    y, x_hi = here // 2, here % 2
    count = queries.shape[0]
    width = layer_input.shape[1] // 8
    slab = width // 8
    first = member == 0
    place = jnp.stack([member, z]).astype(jnp.int32)

    key_local = lax.dynamic_slice_in_dim(key_vectors, head * HD, HD, 1)
    value_local = lax.dynamic_slice_in_dim(value_vectors, head * HD, HD, 1)
    runs_here = (positions[::RUN] // RUN).astype(jnp.bfloat16)
    tail = jnp.broadcast_to(jnp.pad(runs_here, (0, HD - 2))[None], (16, HD))
    own = jnp.concatenate([jnp.where(first, key_local, value_local), tail], axis=0)
    column = jnp.stack([own] + by_source(*to_all_y(own)))
    start = (2 * z + member) * slab

    def block(dy, dx):
        target = ((y + dy) % 4) * 2 + (x_hi + dx) % 2
        return lax.dynamic_slice(layer_input, (0, target * width + start), (count, slab))

    from_x = swap_x(jnp.stack([block(dy, 1) for dy in range(4)]))
    partner_column = swap_x(column)
    column_other = swap_cores(column)
    pairs = [jnp.stack([block(dy, 0), from_x[dy]]) for dy in range(4)]
    moved = [along_y(pairs[dy], dy) for dy in range(1, 4)]
    info = column[:, count, :2].reshape(8).astype(jnp.int32)
    partner_column, info, place, kept, *moved = lax.optimization_barrier(
        (partner_column, info, place, pairs[0], *moved)
    )
    pairs = [kept] + moved
    partner_other = swap_cores(partner_column)
    partner_info = partner_column[:, count, :2].reshape(8).astype(jnp.int32)
    info = jnp.concatenate([info, partner_info, place[:1]])
    slab_own = turn(pairs)
    slab_back, slab_ahead = along_z(slab_own, 1), along_z(slab_own, 3)
    own_other = swap_cores(slab_own)

    grad_query, grad_heads, keep, give = attention(
        info, queries, grad_output, [column, partner_column], [column_other, partner_other]
    )
    heads = grad_heads.shape[0]
    grad_heads, keep, give, slab_own, slab_back, slab_ahead, own_other = lax.optimization_barrier(
        (grad_heads, keep, give, slab_own, slab_back, slab_ahead, own_other)
    )

    from_1, from_3 = along_y(grad_heads, 1), along_y(grad_heads, 3)
    from_x = swap_x(grad_heads)
    summed = (keep.astype(jnp.float32) + swap_cores(give).astype(jnp.float32)).astype(jnp.bfloat16)
    summed = summed.reshape(2, 4, count, HD)
    rows_1, rows_3 = along_y(summed[:, 3], 1), along_y(summed[:, 1], 3)
    from_1, from_3, from_x, to_2, slab_own = lax.optimization_barrier(
        (from_1, from_3, from_x, summed[:, 2], slab_own)
    )
    rows_2 = along_y(to_2, 2)
    from_x13 = swap_x(jnp.concatenate([from_1, from_3]))
    slab_far = along_z(slab_own, 2)
    rows_y = summed[:, 0].astype(jnp.float32)
    for term in (rows_1, rows_3, rows_2):
        rows_y = rows_y + term.astype(jnp.float32)
    rows_y = rows_y.astype(jnp.bfloat16)
    to_2 = jnp.concatenate([grad_heads, from_x])
    rows_y, to_2, slab_back = lax.optimization_barrier((rows_y, to_2, slab_back))
    rows_x = swap_x(rows_y)
    from_2 = along_y(to_2, 2)
    back_other = swap_cores(slab_back)
    rows_x, slab_far, back_other, slab_ahead, from_x13 = lax.optimization_barrier(
        (rows_x, slab_far, back_other, slab_ahead, from_x13)
    )
    both = (rows_y.astype(jnp.float32) + rows_x.astype(jnp.float32)[::-1]).astype(jnp.bfloat16)
    shared = [both] + by_source(*to_all_y(both))

    ahead_other = swap_cores(slab_ahead)
    ahead_other, slab_far = lax.optimization_barrier((ahead_other, slab_far))
    far_other = swap_cores(slab_far)

    slabs = [slab_own, slab_ahead, slab_far, slab_back]
    slabs_other = [own_other, ahead_other, far_other, back_other]
    early = [(grad_heads, 0), (from_1, 0), (from_3, 0), (from_x, 0)]
    late = [(from_2, 0), (from_x13, 0), (from_2, heads), (from_x13, heads)]
    partial = weights(place, slabs, slabs_other, early, heads)
    grad_wq, grad_wk, grad_wv, grad_key, grad_value = weights(
        place, slabs, slabs_other, late, heads, partial, shared
    )
    return grad_query, grad_key.T, grad_value.T, grad_wq, grad_wk.T, grad_wv.T


def solution(mesh):
    in_specs = (
        P("ctx", None),
        P("ctx", "dp"),
        P("ctx", None),
        P("ctx", None),
        P("ctx", "dp"),
        P("ctx"),
    )
    out_specs = (P("ctx", "dp"),) * 6
    return jax.shard_map(local, mesh=mesh, in_specs=in_specs, out_specs=out_specs, check_vma=False)
```

```python
import functools
import math

import jax
import jax.numpy as jnp
from jax import lax
from jax.experimental import pallas as pl
from jax.experimental.pallas import tpu as pltpu
from jax.sharding import PartitionSpec as P

HD = 128
QH = 64
KVH = 8
RUN = 256
LOW = -1e30
LOG2E = 1.4426950408889634
VMEM_BYTES = 60 * 1024 * 1024


def contract(left, right, left_dim, right_dim):
    return lax.dot_general(
        left, right, (((left_dim,), (right_dim,)), ((), ())), preferred_element_type=jnp.float32
    )


def along_y(value, step):
    return lax.ppermute(value, "ctx", [(i, (i + 2 * step) % 8) for i in range(8)])


def swap_x(value):
    return lax.ppermute(value, "ctx", [(i, i ^ 1) for i in range(8)])


def along_z(value, step):
    return lax.ppermute(value, "dp", [(i, (i + 4 * step) % 16) for i in range(16)])


def swap_cores(value):
    return lax.ppermute(value, "dp", [(i, i ^ 1) for i in range(16)])


def to_all_y(value):
    return [along_y(value, step) for step in (1, 3, 2)]


def by_source(one, three, two):
    return [one, two, three]


def in_strides(count, step, state):
    done = 0
    for stride in (4, 2, 1):

        def several(j, state, done=done, stride=stride):
            for i in range(stride):
                state = step(done + j * stride + i, state)
            return state

        times = (count - done) // stride
        state = lax.fori_loop(0, times, several, state)
        done = done + times * stride
    return state


def attention_kernel(
    heads, info_ref, q_ref, g_ref, mine_refs, other_refs, dq_ref, dqh_ref, keep_ref, give_ref,
    ks, vs, kt, scores, grads, dka, dva, qh, gh, dqt,
):
    per_ref = mine_refs[0].shape[0]
    slots = per_ref * len(mine_refs)
    runs_per_slot = 2
    scale = 1.0 / math.sqrt(HD)
    core = info_ref[2 * slots]
    for b in range(slots * runs_per_slot):
        slot, part = b // runs_per_slot, b % runs_per_slot
        rows = slice(part * RUN, (part + 1) * RUN)
        at = pl.multiple_of(info_ref[b] * RUN, RUN)
        first = mine_refs[slot // per_ref][slot % per_ref, rows, :]
        second = other_refs[slot // per_ref][slot % per_ref, rows, :]
        key_block = jnp.where(core == 0, first, second)
        ks[pl.ds(at, RUN), :] = key_block
        kt[:, pl.ds(at, RUN)] = key_block.T
        vs[pl.ds(at, RUN), :] = jnp.where(core == 0, second, first)
    dka[...] = jnp.zeros_like(dka)
    dva[...] = jnp.zeros_like(dva)
    for half in range(2):
        run = info_ref[half]
        rows = slice(half * RUN, (half + 1) * RUN)
        for h in range(heads):
            qh[h * RUN : (h + 1) * RUN, :] = q_ref[rows, h * HD : (h + 1) * HD]
            gh[h * RUN : (h + 1) * RUN, :] = g_ref[rows, h * HD : (h + 1) * HD]

        def stat_step(j, state, diagonal):
            at = pl.multiple_of(j * RUN, RUN)
            key_block = ks[pl.ds(at, RUN), :]
            value_block = vs[pl.ds(at, RUN), :]
            new_state = []
            s_all = contract(key_block, qh[...], 1, 1) * (scale * LOG2E)
            dp_all = contract(value_block, gh[...], 1, 1)
            if diagonal:
                key_at = lax.broadcasted_iota(jnp.int32, (RUN, RUN), 0)
                query_at = lax.broadcasted_iota(jnp.int32, (RUN, RUN), 1)
                visible = jnp.concatenate([key_at <= query_at] * heads, axis=1)
                s_all = jnp.where(visible, s_all, LOW)
            scores[pl.ds(at, RUN), :] = s_all
            grads[pl.ds(at, RUN), :] = dp_all
            for h in range(heads):
                row_max, denom, weighted = state[h]
                cols = slice(h * RUN, (h + 1) * RUN)
                s3 = s_all[:, cols].reshape(RUN // 8, 8, RUN)
                dp3 = dp_all[:, cols].reshape(RUN // 8, 8, RUN)
                new_max = jnp.maximum(row_max, jnp.max(s3, axis=0))
                fade = jnp.exp2(row_max - new_max)
                expo = jnp.exp2(s3 - new_max[None])
                if diagonal:
                    expo = jnp.where(s3 > 0.5 * LOW, expo, 0.0)
                new_state.append(
                    (
                        new_max,
                        denom * fade + jnp.sum(expo, axis=0),
                        weighted * fade + jnp.sum(expo * dp3, axis=0),
                    )
                )
            return tuple(new_state)

        zeros = jnp.zeros((8, RUN), jnp.float32)
        state = tuple((jnp.full((8, RUN), LOW, jnp.float32), zeros, zeros) for _ in range(heads))
        state = in_strides(run, lambda j, st: stat_step(j, st, False), state)
        state = stat_step(run, state, True)
        lse, dots = [], []
        for h in range(heads):
            row_max, denom, weighted = state[h]
            top = jnp.max(row_max, axis=0, keepdims=True)
            fade = jnp.exp2(row_max - top)
            total = jnp.sum(denom * fade, axis=0, keepdims=True)
            lse.append(top + jnp.log2(total))
            dots.append(jnp.sum(weighted * fade, axis=0, keepdims=True) / total)
        dqt[...] = jnp.zeros_like(dqt)

        def grad_step(j, carry):
            at = pl.multiple_of(j * RUN, RUN)
            key_cols = kt[:, pl.ds(at, RUN)]
            probs_low, grad_scores = [], []
            for h in range(heads):
                cols = slice(h * RUN, (h + 1) * RUN)
                p = jnp.exp2(scores[pl.ds(at, RUN), cols] - lse[h])
                ds = p * (grads[pl.ds(at, RUN), cols] - dots[h])
                probs_low.append(p.astype(jnp.bfloat16))
                grad_scores.append(ds.astype(jnp.bfloat16))
            ds_all = jnp.concatenate(grad_scores, axis=1)
            dv = contract(jnp.concatenate(probs_low, axis=1), gh[...], 1, 0)
            dk = contract(ds_all, qh[...], 1, 0)
            dqt[...] += contract(key_cols, ds_all, 1, 0)
            dka[pl.ds(at, RUN), :] += dk
            dva[pl.ds(at, RUN), :] += dv
            return carry

        in_strides(run + 1, grad_step, 0)
        for h in range(heads):
            cols = slice(h * RUN, (h + 1) * RUN)
            dq = (dqt[:, cols] * scale).T.astype(jnp.bfloat16)
            dq_ref[rows, h * HD : (h + 1) * HD] = dq
            dqh_ref[h, rows, :] = dq
    half_head = HD // 2
    for b in range(slots * runs_per_slot):
        slot, part = b // runs_per_slot, b % runs_per_slot
        rows = slice(part * RUN, (part + 1) * RUN)
        at = pl.multiple_of(info_ref[b] * RUN, RUN)
        dk = dka[pl.ds(at, RUN), :] * scale
        dv = dva[pl.ds(at, RUN), :]
        low = jnp.concatenate([dk[:, :half_head], dv[:, :half_head]], axis=1)
        high = jnp.concatenate([dk[:, half_head:], dv[:, half_head:]], axis=1)
        keep_ref[slot, rows, :] = jnp.where(core == 0, low, high).astype(jnp.bfloat16)
        give_ref[slot, rows, :] = jnp.where(core == 0, high, low).astype(jnp.bfloat16)


def attention(info, queries, grad_output, mine, other):
    slots = mine[0].shape[0] * len(mine)
    count = slots * 2 * RUN
    heads = queries.shape[1] // HD
    wide = heads * RUN
    smem = pl.BlockSpec(memory_space=pltpu.SMEM)
    vmem = pl.BlockSpec(memory_space=pltpu.VMEM)
    shared = jax.ShapeDtypeStruct((slots, 2 * RUN, HD), jnp.bfloat16)
    pairs = heads * 2 * RUN * count // 2
    return pl.pallas_call(
        functools.partial(attention_kernel, heads),
        out_shape=(
            jax.ShapeDtypeStruct(queries.shape, jnp.bfloat16),
            jax.ShapeDtypeStruct((heads, 2 * RUN, HD), jnp.bfloat16),
            shared,
            shared,
        ),
        in_specs=[smem, vmem, vmem, [vmem] * len(mine), [vmem] * len(other)],
        out_specs=(vmem, vmem, vmem, vmem),
        scratch_shapes=[
            pltpu.VMEM((count, HD), jnp.bfloat16),
            pltpu.VMEM((count, HD), jnp.bfloat16),
            pltpu.VMEM((HD, count), jnp.bfloat16),
            pltpu.VMEM((count, wide), jnp.float32),
            pltpu.VMEM((count, wide), jnp.float32),
            pltpu.VMEM((count, HD), jnp.float32),
            pltpu.VMEM((count, HD), jnp.float32),
            pltpu.VMEM((wide, HD), jnp.bfloat16),
            pltpu.VMEM((wide, HD), jnp.bfloat16),
            pltpu.VMEM((HD, wide), jnp.float32),
        ],
        compiler_params=pltpu.CompilerParams(vmem_limit_bytes=VMEM_BYTES),
        cost_estimate=pl.CostEstimate(
            flops=5 * 4 * pairs * HD, bytes_accessed=8 * 1024 * 1024, transcendentals=2 * pairs
        ),
    )(info, queries, grad_output, mine, other)


def turn_kernel(in_refs, out_ref):
    for dy, ref in enumerate(in_refs):
        for dx in range(2):
            tokens = ref.shape[1]
            at = (dx * len(in_refs) + dy) * tokens
            out_ref[:, at : at + tokens] = ref[dx].T


def turn(pieces):
    vmem = pl.BlockSpec(memory_space=pltpu.VMEM)
    sides, tokens, lanes = pieces[0].shape
    return pl.pallas_call(
        turn_kernel,
        out_shape=jax.ShapeDtypeStruct((lanes, len(pieces) * sides * tokens), jnp.bfloat16),
        in_specs=[[vmem] * len(pieces)],
        out_specs=vmem,
        compiler_params=pltpu.CompilerParams(vmem_limit_bytes=VMEM_BYTES),
        cost_estimate=pl.CostEstimate(flops=0, bytes_accessed=2 * 1024 * 1024, transcendentals=0),
    )(list(pieces))


EARLY = (0, 1, 3, 4)
LATE = (2, 5, 6, 7)


def consecutive(slots):
    spans = []
    for at, slot in enumerate(slots):
        if spans and spans[-1][1] + spans[-1][2] == slot:
            spans[-1][2] += 1
        else:
            spans.append([at, slot, 1])
    return spans


def weight_kernel(last, starts, place_ref, own_refs, other_refs, grad_refs, *rest):
    if last:
        (sum_ref, shared_refs, wq_ref, wk_ref, wv_ref, k_ref, v_ref,
         inputs, grads, sums, shared, in_sems, grad_sems, sum_sems, shared_sems, out_sems) = rest
    else:
        wq_ref, inputs, grads, sums, in_sems, grad_sems, out_sems = rest
    core, z = place_ref[0], place_ref[1]
    tall = own_refs[0].shape[0]
    tokens, wide = grad_refs[0].shape[1:]
    heads = grads.shape[1] // wide
    slots = LATE if last else EARLY
    spans = [[0, 0, 8]] if last else consecutive(EARLY)
    grad_copies = [
        pltpu.make_async_copy(
            ref.at[start + h],
            grads.at[pl.ds(i * tokens, tokens), pl.ds(h * wide, wide)],
            grad_sems.at[i, h],
        )
        for i, (ref, start) in enumerate(zip(grad_refs, starts))
        for h in range(heads)
    ]
    for copy in grad_copies:
        copy.start()
    row = [pl.multiple_of(lax.rem(z + away, 4) * 2 * tall, 2 * tall) for away in range(4)]
    in_copies, sum_copies, shared_copies, out_copies = {}, [], [], []
    if last:
        shared_copies = [
            pltpu.make_async_copy(
                shared_refs[slot % 4].at[slot // 4],
                shared.at[pl.ds(slot * tokens, tokens)],
                shared_sems.at[slot],
            )
            for slot in range(8)
        ]
    for away in range(4):
        for n, (at, slot, many) in enumerate(spans):
            for which, ref in enumerate((own_refs[away], other_refs[away])):
                down = pl.multiple_of((core if which == 0 else 1 - core) * tall, tall)
                in_copies[away, n, which] = pltpu.make_async_copy(
                    ref.at[:, pl.ds(slot * tokens, many * tokens)],
                    inputs.at[away, pl.ds(down, tall), pl.ds(at * tokens, many * tokens)],
                    in_sems.at[away, n, which],
                )
        if last:
            sum_copies.append(
                pltpu.make_async_copy(
                    sum_ref.at[pl.ds(row[away], 2 * tall)], sums.at[away], sum_sems.at[away]
                )
            )

    def fetch(away):
        for n in range(len(spans)):
            for which in range(2):
                in_copies[away, n, which].start()
        if last:
            sum_copies[away].start()

    fetch(0)
    for copy in shared_copies:
        copy.start()
    fetch(1)
    for copy in grad_copies:
        copy.wait()
    norm = 1.0 / math.sqrt(8 * tokens)
    for away in range(4):
        for n in range(len(spans)):
            for which in range(2):
                in_copies[away, n, which].wait()
        if away + 2 < 4:
            fetch(away + 2)
        if last:
            total = sum(
                contract(
                    inputs[away, :, slot * tokens : (slot + many) * tokens],
                    grads[at * tokens : (at + many) * tokens],
                    1,
                    0,
                )
                for at, slot, many in consecutive(slots)
            )
        else:
            total = contract(inputs[away], grads[...], 1, 0)
        if last:
            sum_copies[away].wait()
            total = (total + sums[away]) * norm
        sums[away] = total
        out_copies.append(
            pltpu.make_async_copy(
                sums.at[away], wq_ref.at[pl.ds(row[away], 2 * tall)], out_sems.at[away]
            )
        )
        out_copies[away].start()
        if last:
            if away == 0:
                for copy in shared_copies:
                    copy.wait()
            part = (contract(inputs[away], shared[...], 1, 0) * norm).T
            wk_ref[:, pl.ds(row[away], 2 * tall)] = part[: tall // 2]
            wv_ref[:, pl.ds(row[away], 2 * tall)] = part[tall // 2 :]
    if last:
        here = shared[:tokens].T
        k_ref[...] = here[: here.shape[0] // 2]
        v_ref[...] = here[here.shape[0] // 2 :]
    for copy in out_copies:
        copy.wait()


def weights(place, own, other, grads, heads, total=None, shared=None):
    last = total is not None
    smem = pl.BlockSpec(memory_space=pltpu.SMEM)
    vmem = pl.BlockSpec(memory_space=pltpu.VMEM)
    hbm = pl.BlockSpec(memory_space=pl.ANY)
    tall, across = own[0].shape
    tokens, wide = grads[0][0].shape[1:]
    cols = heads * wide
    f32, bf16, sem = jnp.float32, jnp.bfloat16, pltpu.SemaphoreType.DMA
    wq = jax.ShapeDtypeStruct((8 * tall, cols), f32)
    narrow = jax.ShapeDtypeStruct((tall // 2, 8 * tall), f32)
    narrow_in = jax.ShapeDtypeStruct((tall // 2, tokens), bf16)
    spans = 1 if last else len(consecutive(EARLY))
    scratch = [
        pltpu.VMEM((4, 2 * tall, (8 if last else len(EARLY)) * tokens), bf16),
        pltpu.VMEM((len(grads) * tokens, cols), bf16),
        pltpu.VMEM((4, 2 * tall, cols), f32),
    ]
    if last:
        scratch += [pltpu.VMEM((across, tall), bf16)]
    scratch += [sem((4, spans, 2)), sem((len(grads), heads))]
    if last:
        scratch += [sem((4,)), sem((8,))]
    scratch += [sem((4,))]
    return pl.pallas_call(
        functools.partial(weight_kernel, last, tuple(start for _, start in grads)),
        out_shape=(wq, narrow, narrow, narrow_in, narrow_in) if last else wq,
        in_specs=[smem, [hbm] * 4, [hbm] * 4, [hbm] * 4] + ([hbm, [hbm] * 4] if last else []),
        out_specs=(hbm, vmem, vmem, vmem, vmem) if last else hbm,
        scratch_shapes=scratch,
        compiler_params=pltpu.CompilerParams(vmem_limit_bytes=VMEM_BYTES),
        cost_estimate=pl.CostEstimate(
            flops=8 * tokens * cols * 8 * tall, bytes_accessed=10 * 1024 * 1024, transcendentals=0
        ),
    )(
        place,
        list(own),
        list(other),
        [array for array, _ in grads],
        *((total, list(shared)) if last else ()),
    )


def local(layer_input, queries, key_vectors, value_vectors, grad_output, positions):
    group = lax.axis_index("dp")
    member, head, z = group % 2, group // 2, group // 4
    here = lax.axis_index("ctx")
    y, x_hi = here // 2, here % 2
    count = queries.shape[0]
    width = layer_input.shape[1] // 8
    slab = width // 8
    first = member == 0
    place = jnp.stack([member, z]).astype(jnp.int32)

    key_local = lax.dynamic_slice_in_dim(key_vectors, head * HD, HD, 1)
    value_local = lax.dynamic_slice_in_dim(value_vectors, head * HD, HD, 1)
    runs_here = (positions[::RUN] // RUN).astype(jnp.bfloat16)
    tail = jnp.broadcast_to(jnp.pad(runs_here, (0, HD - 2))[None], (16, HD))
    own = jnp.concatenate([jnp.where(first, key_local, value_local), tail], axis=0)
    column = jnp.stack([own] + by_source(*to_all_y(own)))
    start = (2 * z + member) * slab

    def block(dy, dx):
        target = ((y + dy) % 4) * 2 + (x_hi + dx) % 2
        return lax.dynamic_slice(layer_input, (0, target * width + start), (count, slab))

    from_x = swap_x(jnp.stack([block(dy, 1) for dy in range(4)]))
    partner_column = swap_x(column)
    column_other = swap_cores(column)
    pairs = [jnp.stack([block(dy, 0), from_x[dy]]) for dy in range(4)]
    moved = [along_y(pairs[dy], dy) for dy in range(1, 4)]
    info = column[:, count, :2].reshape(8).astype(jnp.int32)
    partner_column, info, place, kept, *moved = lax.optimization_barrier(
        (partner_column, info, place, pairs[0], *moved)
    )
    pairs = [kept] + moved
    partner_other = swap_cores(partner_column)
    partner_info = partner_column[:, count, :2].reshape(8).astype(jnp.int32)
    info = jnp.concatenate([info, partner_info, place[:1]])
    slab_own = turn(pairs)
    slab_back, slab_ahead = along_z(slab_own, 1), along_z(slab_own, 3)
    own_other = swap_cores(slab_own)

    grad_query, grad_heads, keep, give = attention(
        info, queries, grad_output, [column, partner_column], [column_other, partner_other]
    )
    heads = grad_heads.shape[0]
    grad_heads, keep, give, slab_own, slab_back, slab_ahead, own_other = lax.optimization_barrier(
        (grad_heads, keep, give, slab_own, slab_back, slab_ahead, own_other)
    )

    from_1, from_3 = along_y(grad_heads, 1), along_y(grad_heads, 3)
    from_x = swap_x(grad_heads)
    summed = (keep.astype(jnp.float32) + swap_cores(give).astype(jnp.float32)).astype(jnp.bfloat16)
    summed = summed.reshape(2, 4, count, HD)
    rows_1, rows_3 = along_y(summed[:, 3], 1), along_y(summed[:, 1], 3)
    from_x, to_2 = lax.optimization_barrier((from_x, summed[:, 2]))
    rows_2 = along_y(to_2, 2)
    from_1, from_3, rows_1, rows_3, rows_2, slab_own, slab_back, slab_ahead = lax.optimization_barrier(
        (from_1, from_3, rows_1, rows_3, rows_2, slab_own, slab_back, slab_ahead)
    )
    slab_far = along_z(slab_own, 2)
    rows_y = summed[:, 0].astype(jnp.float32)
    for term in (rows_1, rows_3, rows_2):
        rows_y = rows_y + term.astype(jnp.float32)
    rows_y = rows_y.astype(jnp.bfloat16)
    rows_x = swap_x(rows_y)
    from_2 = along_y(jnp.concatenate([grad_heads, from_x]), 2)
    back_other, ahead_other = swap_cores(slab_back), swap_cores(slab_ahead)
    to_x = jnp.concatenate([from_1, from_3])
    rows_x, back_other, ahead_other, to_x = lax.optimization_barrier(
        (rows_x, back_other, ahead_other, to_x)
    )
    from_x13 = swap_x(to_x)
    both = (rows_y.astype(jnp.float32) + rows_x.astype(jnp.float32)[::-1]).astype(jnp.bfloat16)
    shared = [both] + by_source(*to_all_y(both))

    far_other = swap_cores(slab_far)

    slabs = [slab_own, slab_ahead, slab_far, slab_back]
    slabs_other = [own_other, ahead_other, far_other, back_other]
    early = [(grad_heads, 0), (from_1, 0), (from_3, 0), (from_x, 0)]
    late = [(from_2, 0), (from_x13, 0), (from_2, heads), (from_x13, heads)]
    partial = weights(place, slabs, slabs_other, early, heads)
    grad_wq, grad_wk, grad_wv, grad_key, grad_value = weights(
        place, slabs, slabs_other, late, heads, partial, shared
    )
    return grad_query, grad_key.T, grad_value.T, grad_wq, grad_wk.T, grad_wv.T


def solution(mesh):
    in_specs = (
        P("ctx", None),
        P("ctx", "dp"),
        P("ctx", None),
        P("ctx", None),
        P("ctx", "dp"),
        P("ctx"),
    )
    out_specs = (P("ctx", "dp"),) * 6
    return jax.shard_map(local, mesh=mesh, in_specs=in_specs, out_specs=out_specs, check_vma=False)
```

```python
import functools
import math

import jax
import jax.numpy as jnp
from jax import lax
from jax.experimental import pallas as pl
from jax.experimental.pallas import tpu as pltpu
from jax.sharding import PartitionSpec as P

HD = 128
QH = 64
KVH = 8
RUN = 256
LOW = -1e30
LOG2E = 1.4426950408889634
VMEM_BYTES = 60 * 1024 * 1024


def contract(left, right, left_dim, right_dim):
    return lax.dot_general(
        left, right, (((left_dim,), (right_dim,)), ((), ())), preferred_element_type=jnp.float32
    )


def along_y(value, step):
    return lax.ppermute(value, "ctx", [(i, (i + 2 * step) % 8) for i in range(8)])


def swap_x(value):
    return lax.ppermute(value, "ctx", [(i, i ^ 1) for i in range(8)])


def along_z(value, step):
    return lax.ppermute(value, "dp", [(i, (i + 4 * step) % 16) for i in range(16)])


def swap_cores(value):
    return lax.ppermute(value, "dp", [(i, i ^ 1) for i in range(16)])


def to_all_y(value):
    return [along_y(value, step) for step in (1, 3, 2)]


def by_source(one, three, two):
    return [one, two, three]


def in_strides(count, step, state):
    done = 0
    for stride in (4, 2, 1):

        def several(j, state, done=done, stride=stride):
            for i in range(stride):
                state = step(done + j * stride + i, state)
            return state

        times = (count - done) // stride
        state = lax.fori_loop(0, times, several, state)
        done = done + times * stride
    return state


def attention_kernel(
    heads, place_ref, here_ref, there_ref, q_ref, g_ref, mine_refs, other_refs, dq_ref, dqh_ref, keep_ref, give_ref,
    ks, vs, kt, scores, grads, dka, dva, qh, gh, dqt,
):
    per_ref = mine_refs[0].shape[0]
    slots = per_ref * len(mine_refs)
    runs_per_slot = 2
    scale = 1.0 / math.sqrt(HD)
    core = place_ref[0]
    runs = [ref[i] for ref in (here_ref, there_ref) for i in range(slots)]
    for b in range(slots * runs_per_slot):
        slot, part = b // runs_per_slot, b % runs_per_slot
        rows = slice(part * RUN, (part + 1) * RUN)
        at = pl.multiple_of(runs[b] * RUN, RUN)
        first = mine_refs[slot // per_ref][slot % per_ref, rows, :]
        second = other_refs[slot // per_ref][slot % per_ref, rows, :]
        key_block = jnp.where(core == 0, first, second)
        ks[pl.ds(at, RUN), :] = key_block
        kt[:, pl.ds(at, RUN)] = key_block.T
        vs[pl.ds(at, RUN), :] = jnp.where(core == 0, second, first)
    dka[...] = jnp.zeros_like(dka)
    dva[...] = jnp.zeros_like(dva)
    for half in range(2):
        run = runs[half]
        rows = slice(half * RUN, (half + 1) * RUN)
        for h in range(heads):
            qh[h * RUN : (h + 1) * RUN, :] = q_ref[rows, h * HD : (h + 1) * HD]
            gh[h * RUN : (h + 1) * RUN, :] = g_ref[rows, h * HD : (h + 1) * HD]

        def stat_step(j, state, diagonal):
            at = pl.multiple_of(j * RUN, RUN)
            key_block = ks[pl.ds(at, RUN), :]
            value_block = vs[pl.ds(at, RUN), :]
            new_state = []
            s_all = contract(key_block, qh[...], 1, 1) * (scale * LOG2E)
            dp_all = contract(value_block, gh[...], 1, 1)
            if diagonal:
                key_at = lax.broadcasted_iota(jnp.int32, (RUN, RUN), 0)
                query_at = lax.broadcasted_iota(jnp.int32, (RUN, RUN), 1)
                visible = jnp.concatenate([key_at <= query_at] * heads, axis=1)
                s_all = jnp.where(visible, s_all, LOW)
            scores[pl.ds(at, RUN), :] = s_all
            grads[pl.ds(at, RUN), :] = dp_all
            for h in range(heads):
                row_max, denom, weighted = state[h]
                cols = slice(h * RUN, (h + 1) * RUN)
                s3 = s_all[:, cols].reshape(RUN // 8, 8, RUN)
                dp3 = dp_all[:, cols].reshape(RUN // 8, 8, RUN)
                new_max = jnp.maximum(row_max, jnp.max(s3, axis=0))
                fade = jnp.exp2(row_max - new_max)
                expo = jnp.exp2(s3 - new_max[None])
                if diagonal:
                    expo = jnp.where(s3 > 0.5 * LOW, expo, 0.0)
                new_state.append(
                    (
                        new_max,
                        denom * fade + jnp.sum(expo, axis=0),
                        weighted * fade + jnp.sum(expo * dp3, axis=0),
                    )
                )
            return tuple(new_state)

        zeros = jnp.zeros((8, RUN), jnp.float32)
        state = tuple((jnp.full((8, RUN), LOW, jnp.float32), zeros, zeros) for _ in range(heads))
        state = in_strides(run, lambda j, st: stat_step(j, st, False), state)
        state = stat_step(run, state, True)
        lse, dots = [], []
        for h in range(heads):
            row_max, denom, weighted = state[h]
            top = jnp.max(row_max, axis=0, keepdims=True)
            fade = jnp.exp2(row_max - top)
            total = jnp.sum(denom * fade, axis=0, keepdims=True)
            lse.append(top + jnp.log2(total))
            dots.append(jnp.sum(weighted * fade, axis=0, keepdims=True) / total)
        dqt[...] = jnp.zeros_like(dqt)

        def grad_step(j, carry):
            at = pl.multiple_of(j * RUN, RUN)
            key_cols = kt[:, pl.ds(at, RUN)]
            probs_low, grad_scores = [], []
            for h in range(heads):
                cols = slice(h * RUN, (h + 1) * RUN)
                p = jnp.exp2(scores[pl.ds(at, RUN), cols] - lse[h])
                ds = p * (grads[pl.ds(at, RUN), cols] - dots[h])
                probs_low.append(p.astype(jnp.bfloat16))
                grad_scores.append(ds.astype(jnp.bfloat16))
            ds_all = jnp.concatenate(grad_scores, axis=1)
            dv = contract(jnp.concatenate(probs_low, axis=1), gh[...], 1, 0)
            dk = contract(ds_all, qh[...], 1, 0)
            dqt[...] += contract(key_cols, ds_all, 1, 0)
            dka[pl.ds(at, RUN), :] += dk
            dva[pl.ds(at, RUN), :] += dv
            return carry

        in_strides(run + 1, grad_step, 0)
        for h in range(heads):
            cols = slice(h * RUN, (h + 1) * RUN)
            dq = (dqt[:, cols] * scale).T.astype(jnp.bfloat16)
            dq_ref[rows, h * HD : (h + 1) * HD] = dq
            dqh_ref[h, rows, :] = dq
    half_head = HD // 2
    for b in range(slots * runs_per_slot):
        slot, part = b // runs_per_slot, b % runs_per_slot
        rows = slice(part * RUN, (part + 1) * RUN)
        at = pl.multiple_of(runs[b] * RUN, RUN)
        dk = dka[pl.ds(at, RUN), :] * scale
        dv = dva[pl.ds(at, RUN), :]
        low = jnp.concatenate([dk[:, :half_head], dv[:, :half_head]], axis=1)
        high = jnp.concatenate([dk[:, half_head:], dv[:, half_head:]], axis=1)
        keep_ref[slot, rows, :] = jnp.where(core == 0, low, high).astype(jnp.bfloat16)
        give_ref[slot, rows, :] = jnp.where(core == 0, high, low).astype(jnp.bfloat16)


def attention(place, here, there, queries, grad_output, mine, other):
    slots = mine[0].shape[0] * len(mine)
    count = slots * 2 * RUN
    heads = queries.shape[1] // HD
    wide = heads * RUN
    smem = pl.BlockSpec(memory_space=pltpu.SMEM)
    vmem = pl.BlockSpec(memory_space=pltpu.VMEM)
    shared = jax.ShapeDtypeStruct((slots, 2 * RUN, HD), jnp.bfloat16)
    pairs = heads * 2 * RUN * count // 2
    return pl.pallas_call(
        functools.partial(attention_kernel, heads),
        out_shape=(
            jax.ShapeDtypeStruct(queries.shape, jnp.bfloat16),
            jax.ShapeDtypeStruct((heads, 2 * RUN, HD), jnp.bfloat16),
            shared,
            shared,
        ),
        in_specs=[smem, smem, smem, vmem, vmem, [vmem] * len(mine), [vmem] * len(other)],
        out_specs=(vmem, vmem, vmem, vmem),
        scratch_shapes=[
            pltpu.VMEM((count, HD), jnp.bfloat16),
            pltpu.VMEM((count, HD), jnp.bfloat16),
            pltpu.VMEM((HD, count), jnp.bfloat16),
            pltpu.VMEM((count, wide), jnp.float32),
            pltpu.VMEM((count, wide), jnp.float32),
            pltpu.VMEM((count, HD), jnp.float32),
            pltpu.VMEM((count, HD), jnp.float32),
            pltpu.VMEM((wide, HD), jnp.bfloat16),
            pltpu.VMEM((wide, HD), jnp.bfloat16),
            pltpu.VMEM((HD, wide), jnp.float32),
        ],
        compiler_params=pltpu.CompilerParams(vmem_limit_bytes=VMEM_BYTES),
        cost_estimate=pl.CostEstimate(
            flops=5 * 4 * pairs * HD, bytes_accessed=8 * 1024 * 1024, transcendentals=2 * pairs
        ),
    )(place, here, there, queries, grad_output, mine, other)


def turn_kernel(in_refs, out_ref):
    for dy, ref in enumerate(in_refs):
        for dx in range(2):
            tokens = ref.shape[1]
            at = (dx * len(in_refs) + dy) * tokens
            out_ref[:, at : at + tokens] = ref[dx].T


def turn(pieces):
    vmem = pl.BlockSpec(memory_space=pltpu.VMEM)
    sides, tokens, lanes = pieces[0].shape
    return pl.pallas_call(
        turn_kernel,
        out_shape=jax.ShapeDtypeStruct((lanes, len(pieces) * sides * tokens), jnp.bfloat16),
        in_specs=[[vmem] * len(pieces)],
        out_specs=vmem,
        compiler_params=pltpu.CompilerParams(vmem_limit_bytes=VMEM_BYTES),
        cost_estimate=pl.CostEstimate(flops=0, bytes_accessed=2 * 1024 * 1024, transcendentals=0),
    )(list(pieces))


EARLY = (0, 1, 3, 4)
LATE = (2, 5, 6, 7)


def consecutive(slots):
    spans = []
    for at, slot in enumerate(slots):
        if spans and spans[-1][1] + spans[-1][2] == slot:
            spans[-1][2] += 1
        else:
            spans.append([at, slot, 1])
    return spans


def slab_copies(core, own_refs, other_refs, inputs, sems, spans, tokens):
    tall = own_refs[0].shape[0]
    copies = []
    for away in range(4):
        copies.append([])
        for n, (at, slot, many) in enumerate(spans):
            for which, ref in enumerate((own_refs[away], other_refs[away])):
                down = pl.multiple_of((core if which == 0 else 1 - core) * tall, tall)
                copies[away].append(
                    pltpu.make_async_copy(
                        ref.at[:, pl.ds(slot * tokens, many * tokens)],
                        inputs.at[away, pl.ds(down, tall), pl.ds(at * tokens, many * tokens)],
                        sems.at[away, n, which],
                    )
                )
    return copies


def pair_rows(z, tall):
    return [pl.multiple_of(lax.rem(z + away, 4) * 2 * tall, 2 * tall) for away in range(4)]


def query_weight_kernel(last, starts, place_ref, own_refs, other_refs, grad_refs, *rest):
    if last:
        sum_ref, out_ref, inputs, grads, sums, in_sems, grad_sems, out_sems, sum_sems = rest
    else:
        out_ref, inputs, grads, sums, in_sems, grad_sems, out_sems = rest
    tall = own_refs[0].shape[0]
    tokens, wide = grad_refs[0].shape[1:]
    spans = consecutive(LATE if last else EARLY)
    grad_copies = [
        pltpu.make_async_copy(
            ref.at[start + h],
            grads.at[pl.ds(i * tokens, tokens), pl.ds(h * wide, wide)],
            grad_sems.at[i, h],
        )
        for i, (ref, start) in enumerate(zip(grad_refs, starts))
        for h in range(grads.shape[1] // wide)
    ]
    for copy in grad_copies:
        copy.start()
    row = pair_rows(place_ref[1], tall)
    in_copies = slab_copies(place_ref[0], own_refs, other_refs, inputs, in_sems, spans, tokens)
    out_copies = []
    for away in range(4):
        if last:
            in_copies[away].append(
                pltpu.make_async_copy(
                    sum_ref.at[pl.ds(row[away], 2 * tall)], sums.at[away], sum_sems.at[away]
                )
            )
        out_copies.append(
            pltpu.make_async_copy(
                sums.at[away], out_ref.at[pl.ds(row[away], 2 * tall)], out_sems.at[away]
            )
        )
    for away in range(2):
        for copy in in_copies[away]:
            copy.start()
    for copy in grad_copies:
        copy.wait()
    for away in range(4):
        for copy in in_copies[away]:
            copy.wait()
        if away + 2 < 4:
            for copy in in_copies[away + 2]:
                copy.start()
        total = contract(inputs[away], grads[...], 1, 0)
        if last:
            total = (total + sums[away]) * (1.0 / math.sqrt(8 * tokens))
        sums[away] = total
        out_copies[away].start()
    for copy in out_copies:
        copy.wait()


def query_weights(place, own, other, grads, heads, total=None):
    last = total is not None
    smem = pl.BlockSpec(memory_space=pltpu.SMEM)
    hbm = pl.BlockSpec(memory_space=pl.ANY)
    tall = own[0].shape[0]
    tokens, wide = grads[0][0].shape[1:]
    cols = heads * wide
    f32, bf16, sem = jnp.float32, jnp.bfloat16, pltpu.SemaphoreType.DMA
    spans = len(consecutive(LATE if last else EARLY))
    return pl.pallas_call(
        functools.partial(query_weight_kernel, last, tuple(start for _, start in grads)),
        out_shape=jax.ShapeDtypeStruct((8 * tall, cols), f32),
        in_specs=[smem, [hbm] * 4, [hbm] * 4, [hbm] * 4] + ([hbm] if last else []),
        out_specs=hbm,
        scratch_shapes=[
            pltpu.VMEM((4, 2 * tall, len(grads) * tokens), bf16),
            pltpu.VMEM((len(grads) * tokens, cols), bf16),
            pltpu.VMEM((4, 2 * tall, cols), f32),
            sem((4, spans, 2)),
            sem((len(grads), heads)),
            sem((4,)),
        ]
        + ([sem((4,))] if last else []),
        compiler_params=pltpu.CompilerParams(vmem_limit_bytes=VMEM_BYTES),
        cost_estimate=pl.CostEstimate(
            flops=8 * tokens * cols * 8 * tall, bytes_accessed=10 * 1024 * 1024, transcendentals=0
        ),
    )(
        place,
        list(own),
        list(other),
        [array for array, _ in grads],
        *((total,) if last else ()),
    )


def shared_weight_kernel(
    place_ref, own_refs, other_refs, shared_refs, wk_ref, wv_ref, k_ref, v_ref,
    inputs, shared, in_sems, shared_sems,
):
    tall = own_refs[0].shape[0]
    tokens = shared_refs[0].shape[1]
    half = tall // 2
    shared_copies = [
        pltpu.make_async_copy(
            shared_refs[slot % 4].at[slot // 4],
            shared.at[pl.ds(slot * tokens, tokens)],
            shared_sems.at[slot],
        )
        for slot in range(8)
    ]
    for copy in shared_copies:
        copy.start()
    row = pair_rows(place_ref[1], tall)
    in_copies = slab_copies(
        place_ref[0], own_refs, other_refs, inputs, in_sems, [[0, 0, 8]], tokens
    )
    for away in range(2):
        for copy in in_copies[away]:
            copy.start()
    for copy in shared_copies:
        copy.wait()
    here = shared[:tokens].T
    k_ref[...] = here[:half]
    v_ref[...] = here[half:]
    for away in range(4):
        for copy in in_copies[away]:
            copy.wait()
        if away + 2 < 4:
            for copy in in_copies[away + 2]:
                copy.start()
        part = contract(inputs[away], shared[...], 1, 0) * (1.0 / math.sqrt(8 * tokens))
        part = part.T
        wk_ref[:, pl.ds(row[away], 2 * tall)] = part[:half]
        wv_ref[:, pl.ds(row[away], 2 * tall)] = part[half:]


def shared_weights(place, own, other, shared):
    smem = pl.BlockSpec(memory_space=pltpu.SMEM)
    vmem = pl.BlockSpec(memory_space=pltpu.VMEM)
    hbm = pl.BlockSpec(memory_space=pl.ANY)
    tall, across = own[0].shape
    tokens = shared[0].shape[1]
    f32, bf16, sem = jnp.float32, jnp.bfloat16, pltpu.SemaphoreType.DMA
    narrow = jax.ShapeDtypeStruct((tall // 2, 8 * tall), f32)
    narrow_in = jax.ShapeDtypeStruct((tall // 2, tokens), bf16)
    return pl.pallas_call(
        shared_weight_kernel,
        out_shape=(narrow, narrow, narrow_in, narrow_in),
        in_specs=[smem, [hbm] * 4, [hbm] * 4, [hbm] * 4],
        out_specs=(vmem, vmem, vmem, vmem),
        scratch_shapes=[
            pltpu.VMEM((4, 2 * tall, across), bf16),
            pltpu.VMEM((across, tall), bf16),
            sem((4, 1, 2)),
            sem((8,)),
        ],
        compiler_params=pltpu.CompilerParams(vmem_limit_bytes=VMEM_BYTES),
        cost_estimate=pl.CostEstimate(
            flops=2 * across * tall * 8 * tall, bytes_accessed=10 * 1024 * 1024, transcendentals=0
        ),
    )(place, list(own), list(other), list(shared))


def local(layer_input, queries, key_vectors, value_vectors, grad_output, positions):
    group = lax.axis_index("dp")
    member, head, z = group % 2, group // 2, group // 4
    here = lax.axis_index("ctx")
    y, x_hi = here // 2, here % 2
    count = queries.shape[0]
    width = layer_input.shape[1] // 8
    slab = width // 8
    first = member == 0
    place = jnp.stack([member, z]).astype(jnp.int32)

    key_local = lax.dynamic_slice_in_dim(key_vectors, head * HD, HD, 1)
    value_local = lax.dynamic_slice_in_dim(value_vectors, head * HD, HD, 1)
    runs_here = (positions[::RUN] // RUN).astype(jnp.bfloat16)
    tail = jnp.broadcast_to(jnp.pad(runs_here, (0, HD - 2))[None], (16, HD))
    own = jnp.concatenate([jnp.where(first, key_local, value_local), tail], axis=0)
    column = jnp.stack([own] + by_source(*to_all_y(own)))
    start = (2 * z + member) * slab

    def block(dy, dx):
        target = ((y + dy) % 4) * 2 + (x_hi + dx) % 2
        return lax.dynamic_slice(layer_input, (0, target * width + start), (count, slab))

    from_x = swap_x(jnp.stack([block(dy, 1) for dy in range(4)]))
    partner_column = swap_x(column)
    column_other = swap_cores(column)
    pairs = [jnp.stack([block(dy, 0), from_x[dy]]) for dy in range(4)]
    moved = [along_y(pairs[dy], dy) for dy in range(1, 4)]
    slab_own = turn([pairs[0]] + moved)
    info = column[:, count, :2].reshape(8).astype(jnp.int32)
    partner_column, info, place, slab_own = lax.optimization_barrier(
        (partner_column, info, place, slab_own)
    )
    partner_other = swap_cores(partner_column)
    partner_info = partner_column[:, count, :2].reshape(8).astype(jnp.int32)
    slab_back, slab_ahead = along_z(slab_own, 1), along_z(slab_own, 3)
    own_other = swap_cores(slab_own)

    grad_query, grad_heads, keep, give = attention(
        place,
        info,
        partner_info,
        queries,
        grad_output,
        [column, partner_column],
        [column_other, partner_other],
    )
    heads = grad_heads.shape[0]
    grad_heads, keep, give, slab_own, slab_back, slab_ahead, own_other = lax.optimization_barrier(
        (grad_heads, keep, give, slab_own, slab_back, slab_ahead, own_other)
    )

    give, back_other = lax.optimization_barrier((swap_cores(give), swap_cores(slab_back)))
    summed = (keep.astype(jnp.float32) + give.astype(jnp.float32)).astype(jnp.bfloat16)
    summed = summed.reshape(2, 4, count, HD)
    from_1 = along_y(jnp.concatenate([grad_heads, summed[:, 3]]), 1)
    from_3 = along_y(jnp.concatenate([grad_heads, summed[:, 1]]), 3)
    rows_2 = along_y(summed[:, 2], 2)
    from_x = swap_x(grad_heads)
    slab_far = along_z(slab_own, 2)
    from_1, from_3, rows_2, from_x, slab_far = lax.optimization_barrier(
        (from_1, from_3, rows_2, from_x, slab_far)
    )
    rows_y = summed[:, 0].astype(jnp.float32)
    for term in (from_1[heads:], from_3[heads:], rows_2):
        rows_y = rows_y + term.astype(jnp.float32)
    rows_y = rows_y.astype(jnp.bfloat16)
    rows_x = swap_x(rows_y)
    from_2 = along_y(jnp.concatenate([grad_heads, from_x]), 2)
    far_other, ahead_other = swap_cores(slab_far), swap_cores(slab_ahead)
    to_x = jnp.concatenate([from_1[:heads], from_3[:heads]])
    rows_x, far_other, ahead_other, to_x = lax.optimization_barrier(
        (rows_x, far_other, ahead_other, to_x)
    )
    from_x13 = swap_x(to_x)
    both = (rows_y.astype(jnp.float32) + rows_x.astype(jnp.float32)[::-1]).astype(jnp.bfloat16)
    shared = [both] + by_source(*to_all_y(both))

    slabs = [slab_own, slab_ahead, slab_far, slab_back]
    slabs_other = [own_other, ahead_other, far_other, back_other]
    early = [(grad_heads, 0), (from_1, 0), (from_3, 0), (from_x, 0)]
    late = [(from_2, 0), (from_x13, 0), (from_2, heads), (from_x13, heads)]
    partial = query_weights(place, slabs, slabs_other, early, heads)
    grad_wq = query_weights(place, slabs, slabs_other, late, heads, partial)
    grad_wk, grad_wv, grad_key, grad_value = shared_weights(place, slabs, slabs_other, shared)
    return grad_query, grad_key.T, grad_value.T, grad_wq, grad_wk.T, grad_wv.T


def solution(mesh):
    in_specs = (
        P("ctx", None),
        P("ctx", "dp"),
        P("ctx", None),
        P("ctx", None),
        P("ctx", "dp"),
        P("ctx"),
    )
    out_specs = (P("ctx", "dp"),) * 6
    return jax.shard_map(local, mesh=mesh, in_specs=in_specs, out_specs=out_specs, check_vma=False)
```

```python
import functools
import math

import jax
import jax.numpy as jnp
from jax import lax
from jax.experimental import pallas as pl
from jax.experimental.pallas import tpu as pltpu
from jax.sharding import PartitionSpec as P

HD = 128
QH = 64
KVH = 8
RUN = 256
LOW = -1e30
LOG2E = 1.4426950408889634
VMEM_BYTES = 60 * 1024 * 1024


def contract(left, right, left_dim, right_dim):
    return lax.dot_general(
        left, right, (((left_dim,), (right_dim,)), ((), ())), preferred_element_type=jnp.float32
    )


def along_y(value, step):
    return lax.ppermute(value, "ctx", [(i, (i + 2 * step) % 8) for i in range(8)])


def swap_x(value):
    return lax.ppermute(value, "ctx", [(i, i ^ 1) for i in range(8)])


def along_z(value, step):
    return lax.ppermute(value, "dp", [(i, (i + 4 * step) % 16) for i in range(16)])


def swap_cores(value):
    return lax.ppermute(value, "dp", [(i, i ^ 1) for i in range(16)])


def to_all_y(value):
    return [along_y(value, step) for step in (1, 3, 2)]


def by_source(one, three, two):
    return [one, two, three]


def in_strides(count, step, state):
    done = 0
    for stride in (4, 2, 1):

        def several(j, state, done=done, stride=stride):
            for i in range(stride):
                state = step(done + j * stride + i, state)
            return state

        times = (count - done) // stride
        state = lax.fori_loop(0, times, several, state)
        done = done + times * stride
    return state


def attention_kernel(
    heads, place_ref, here_ref, there_ref, q_ref, g_ref, mine_refs, other_refs, dq_ref, dqh_ref, keep_ref, give_ref,
    ks, vs, kt, scores, grads, dka, dva, qh, gh, dqt,
):
    per_ref = mine_refs[0].shape[0]
    slots = per_ref * len(mine_refs)
    runs_per_slot = 2
    scale = 1.0 / math.sqrt(HD)
    core = place_ref[0]
    runs = [ref[i, j] for ref in (here_ref, there_ref) for i in range(per_ref) for j in range(2)]
    for b in range(slots * runs_per_slot):
        slot, part = b // runs_per_slot, b % runs_per_slot
        rows = slice(part * RUN, (part + 1) * RUN)
        at = pl.multiple_of(runs[b] * RUN, RUN)
        first = mine_refs[slot // per_ref][slot % per_ref, rows, :]
        second = other_refs[slot // per_ref][slot % per_ref, rows, :]
        key_block = jnp.where(core == 0, first, second)
        ks[pl.ds(at, RUN), :] = key_block
        kt[:, pl.ds(at, RUN)] = key_block.T
        vs[pl.ds(at, RUN), :] = jnp.where(core == 0, second, first)
    dka[...] = jnp.zeros_like(dka)
    dva[...] = jnp.zeros_like(dva)
    for half in range(2):
        run = runs[half]
        rows = slice(half * RUN, (half + 1) * RUN)
        for h in range(heads):
            qh[h * RUN : (h + 1) * RUN, :] = q_ref[rows, h * HD : (h + 1) * HD]
            gh[h * RUN : (h + 1) * RUN, :] = g_ref[rows, h * HD : (h + 1) * HD]

        def stat_step(j, state, diagonal):
            at = pl.multiple_of(j * RUN, RUN)
            key_block = ks[pl.ds(at, RUN), :]
            value_block = vs[pl.ds(at, RUN), :]
            new_state = []
            s_all = contract(key_block, qh[...], 1, 1) * (scale * LOG2E)
            dp_all = contract(value_block, gh[...], 1, 1)
            if diagonal:
                key_at = lax.broadcasted_iota(jnp.int32, (RUN, RUN), 0)
                query_at = lax.broadcasted_iota(jnp.int32, (RUN, RUN), 1)
                visible = jnp.concatenate([key_at <= query_at] * heads, axis=1)
                s_all = jnp.where(visible, s_all, LOW)
            scores[pl.ds(at, RUN), :] = s_all
            grads[pl.ds(at, RUN), :] = dp_all
            for h in range(heads):
                row_max, denom, weighted = state[h]
                cols = slice(h * RUN, (h + 1) * RUN)
                s3 = s_all[:, cols].reshape(RUN // 8, 8, RUN)
                dp3 = dp_all[:, cols].reshape(RUN // 8, 8, RUN)
                new_max = jnp.maximum(row_max, jnp.max(s3, axis=0))
                fade = jnp.exp2(row_max - new_max)
                expo = jnp.exp2(s3 - new_max[None])
                if diagonal:
                    expo = jnp.where(s3 > 0.5 * LOW, expo, 0.0)
                new_state.append(
                    (
                        new_max,
                        denom * fade + jnp.sum(expo, axis=0),
                        weighted * fade + jnp.sum(expo * dp3, axis=0),
                    )
                )
            return tuple(new_state)

        zeros = jnp.zeros((8, RUN), jnp.float32)
        state = tuple((jnp.full((8, RUN), LOW, jnp.float32), zeros, zeros) for _ in range(heads))
        state = in_strides(run, lambda j, st: stat_step(j, st, False), state)
        state = stat_step(run, state, True)
        lse, dots = [], []
        for h in range(heads):
            row_max, denom, weighted = state[h]
            top = jnp.max(row_max, axis=0, keepdims=True)
            fade = jnp.exp2(row_max - top)
            total = jnp.sum(denom * fade, axis=0, keepdims=True)
            lse.append(top + jnp.log2(total))
            dots.append(jnp.sum(weighted * fade, axis=0, keepdims=True) / total)
        dqt[...] = jnp.zeros_like(dqt)

        def grad_step(j, carry):
            at = pl.multiple_of(j * RUN, RUN)
            key_cols = kt[:, pl.ds(at, RUN)]
            probs_low, grad_scores = [], []
            for h in range(heads):
                cols = slice(h * RUN, (h + 1) * RUN)
                p = jnp.exp2(scores[pl.ds(at, RUN), cols] - lse[h])
                ds = p * (grads[pl.ds(at, RUN), cols] - dots[h])
                probs_low.append(p.astype(jnp.bfloat16))
                grad_scores.append(ds.astype(jnp.bfloat16))
            ds_all = jnp.concatenate(grad_scores, axis=1)
            dv = contract(jnp.concatenate(probs_low, axis=1), gh[...], 1, 0)
            dk = contract(ds_all, qh[...], 1, 0)
            dqt[...] += contract(key_cols, ds_all, 1, 0)
            dka[pl.ds(at, RUN), :] += dk
            dva[pl.ds(at, RUN), :] += dv
            return carry

        in_strides(run + 1, grad_step, 0)
        for h in range(heads):
            cols = slice(h * RUN, (h + 1) * RUN)
            dq = (dqt[:, cols] * scale).T.astype(jnp.bfloat16)
            dq_ref[rows, h * HD : (h + 1) * HD] = dq
            dqh_ref[h, rows, :] = dq
    half_head = HD // 2
    for b in range(slots * runs_per_slot):
        slot, part = b // runs_per_slot, b % runs_per_slot
        rows = slice(part * RUN, (part + 1) * RUN)
        at = pl.multiple_of(runs[b] * RUN, RUN)
        dk = dka[pl.ds(at, RUN), :] * scale
        dv = dva[pl.ds(at, RUN), :]
        low = jnp.concatenate([dk[:, :half_head], dv[:, :half_head]], axis=1)
        high = jnp.concatenate([dk[:, half_head:], dv[:, half_head:]], axis=1)
        keep_ref[slot, rows, :] = jnp.where(core == 0, low, high).astype(jnp.bfloat16)
        give_ref[slot, rows, :] = jnp.where(core == 0, high, low).astype(jnp.bfloat16)


def attention(place, here, there, queries, grad_output, mine, other):
    slots = mine[0].shape[0] * len(mine)
    count = slots * 2 * RUN
    heads = queries.shape[1] // HD
    wide = heads * RUN
    smem = pl.BlockSpec(memory_space=pltpu.SMEM)
    vmem = pl.BlockSpec(memory_space=pltpu.VMEM)
    shared = jax.ShapeDtypeStruct((slots, 2 * RUN, HD), jnp.bfloat16)
    pairs = heads * 2 * RUN * count // 2
    return pl.pallas_call(
        functools.partial(attention_kernel, heads),
        out_shape=(
            jax.ShapeDtypeStruct(queries.shape, jnp.bfloat16),
            jax.ShapeDtypeStruct((heads, 2 * RUN, HD), jnp.bfloat16),
            shared,
            shared,
        ),
        in_specs=[smem, smem, smem, vmem, vmem, [vmem] * len(mine), [vmem] * len(other)],
        out_specs=(vmem, vmem, vmem, vmem),
        scratch_shapes=[
            pltpu.VMEM((count, HD), jnp.bfloat16),
            pltpu.VMEM((count, HD), jnp.bfloat16),
            pltpu.VMEM((HD, count), jnp.bfloat16),
            pltpu.VMEM((count, wide), jnp.float32),
            pltpu.VMEM((count, wide), jnp.float32),
            pltpu.VMEM((count, HD), jnp.float32),
            pltpu.VMEM((count, HD), jnp.float32),
            pltpu.VMEM((wide, HD), jnp.bfloat16),
            pltpu.VMEM((wide, HD), jnp.bfloat16),
            pltpu.VMEM((HD, wide), jnp.float32),
        ],
        compiler_params=pltpu.CompilerParams(vmem_limit_bytes=VMEM_BYTES),
        cost_estimate=pl.CostEstimate(
            flops=5 * 4 * pairs * HD, bytes_accessed=8 * 1024 * 1024, transcendentals=2 * pairs
        ),
    )(place, here, there, queries, grad_output, mine, other)


def turn_kernel(in_refs, out_ref):
    for dy, ref in enumerate(in_refs):
        for dx in range(2):
            tokens = ref.shape[1]
            at = (dx * len(in_refs) + dy) * tokens
            out_ref[:, at : at + tokens] = ref[dx].T


def turn(pieces):
    vmem = pl.BlockSpec(memory_space=pltpu.VMEM)
    sides, tokens, lanes = pieces[0].shape
    return pl.pallas_call(
        turn_kernel,
        out_shape=jax.ShapeDtypeStruct((lanes, len(pieces) * sides * tokens), jnp.bfloat16),
        in_specs=[[vmem] * len(pieces)],
        out_specs=vmem,
        compiler_params=pltpu.CompilerParams(vmem_limit_bytes=VMEM_BYTES),
        cost_estimate=pl.CostEstimate(flops=0, bytes_accessed=2 * 1024 * 1024, transcendentals=0),
    )(list(pieces))


EARLY = (0, 1, 3, 4)
LATE = (2, 5, 6, 7)


def consecutive(slots):
    spans = []
    for at, slot in enumerate(slots):
        if spans and spans[-1][1] + spans[-1][2] == slot:
            spans[-1][2] += 1
        else:
            spans.append([at, slot, 1])
    return spans


def slab_copies(core, own_refs, other_refs, inputs, sems, spans, tokens):
    tall = own_refs[0].shape[0]
    copies = []
    for away in range(4):
        copies.append([])
        for n, (at, slot, many) in enumerate(spans):
            for which, ref in enumerate((own_refs[away], other_refs[away])):
                down = pl.multiple_of((core if which == 0 else 1 - core) * tall, tall)
                copies[away].append(
                    pltpu.make_async_copy(
                        ref.at[:, pl.ds(slot * tokens, many * tokens)],
                        inputs.at[away, pl.ds(down, tall), pl.ds(at * tokens, many * tokens)],
                        sems.at[away, n, which],
                    )
                )
    return copies


def pair_rows(z, tall):
    return [pl.multiple_of(lax.rem(z + away, 4) * 2 * tall, 2 * tall) for away in range(4)]


def query_weight_kernel(last, starts, place_ref, own_refs, other_refs, grad_refs, *rest):
    if last:
        sum_ref, out_ref, inputs, grads, sums, in_sems, grad_sems, out_sems, sum_sems = rest
    else:
        out_ref, inputs, grads, sums, in_sems, grad_sems, out_sems = rest
    tall = own_refs[0].shape[0]
    tokens, wide = grad_refs[0].shape[1:]
    spans = consecutive(LATE if last else EARLY)
    grad_copies = [
        pltpu.make_async_copy(
            ref.at[start + h],
            grads.at[pl.ds(i * tokens, tokens), pl.ds(h * wide, wide)],
            grad_sems.at[i, h],
        )
        for i, (ref, start) in enumerate(zip(grad_refs, starts))
        for h in range(grads.shape[1] // wide)
    ]
    for copy in grad_copies:
        copy.start()
    row = pair_rows(place_ref[1], tall)
    in_copies = slab_copies(place_ref[0], own_refs, other_refs, inputs, in_sems, spans, tokens)
    out_copies = []
    for away in range(4):
        if last:
            in_copies[away].append(
                pltpu.make_async_copy(
                    sum_ref.at[pl.ds(row[away], 2 * tall)], sums.at[away], sum_sems.at[away]
                )
            )
        out_copies.append(
            pltpu.make_async_copy(
                sums.at[away], out_ref.at[pl.ds(row[away], 2 * tall)], out_sems.at[away]
            )
        )
    for away in range(2):
        for copy in in_copies[away]:
            copy.start()
    for copy in grad_copies:
        copy.wait()
    for away in range(4):
        for copy in in_copies[away]:
            copy.wait()
        if away + 2 < 4:
            for copy in in_copies[away + 2]:
                copy.start()
        total = contract(inputs[away], grads[...], 1, 0)
        if last:
            total = (total + sums[away]) * (1.0 / math.sqrt(8 * tokens))
        sums[away] = total
        out_copies[away].start()
    for copy in out_copies:
        copy.wait()


def query_weights(place, own, other, grads, heads, total=None):
    last = total is not None
    smem = pl.BlockSpec(memory_space=pltpu.SMEM)
    hbm = pl.BlockSpec(memory_space=pl.ANY)
    tall = own[0].shape[0]
    tokens, wide = grads[0][0].shape[1:]
    cols = heads * wide
    f32, bf16, sem = jnp.float32, jnp.bfloat16, pltpu.SemaphoreType.DMA
    spans = len(consecutive(LATE if last else EARLY))
    return pl.pallas_call(
        functools.partial(query_weight_kernel, last, tuple(start for _, start in grads)),
        out_shape=jax.ShapeDtypeStruct((8 * tall, cols), f32),
        in_specs=[smem, [hbm] * 4, [hbm] * 4, [hbm] * 4] + ([hbm] if last else []),
        out_specs=hbm,
        scratch_shapes=[
            pltpu.VMEM((4, 2 * tall, len(grads) * tokens), bf16),
            pltpu.VMEM((len(grads) * tokens, cols), bf16),
            pltpu.VMEM((4, 2 * tall, cols), f32),
            sem((4, spans, 2)),
            sem((len(grads), heads)),
            sem((4,)),
        ]
        + ([sem((4,))] if last else []),
        compiler_params=pltpu.CompilerParams(vmem_limit_bytes=VMEM_BYTES),
        cost_estimate=pl.CostEstimate(
            flops=8 * tokens * cols * 8 * tall, bytes_accessed=10 * 1024 * 1024, transcendentals=0
        ),
    )(
        place,
        list(own),
        list(other),
        [array for array, _ in grads],
        *((total,) if last else ()),
    )


def shared_weight_kernel(
    place_ref, own_refs, other_refs, shared_refs, wk_ref, wv_ref, k_ref, v_ref,
    inputs, shared, in_sems, shared_sems,
):
    tall = own_refs[0].shape[0]
    tokens = shared_refs[0].shape[1]
    half = tall // 2
    shared_copies = [
        pltpu.make_async_copy(
            shared_refs[slot % 4].at[slot // 4],
            shared.at[pl.ds(slot * tokens, tokens)],
            shared_sems.at[slot],
        )
        for slot in range(8)
    ]
    for copy in shared_copies:
        copy.start()
    row = pair_rows(place_ref[1], tall)
    in_copies = slab_copies(
        place_ref[0], own_refs, other_refs, inputs, in_sems, [[0, 0, 8]], tokens
    )
    for away in range(2):
        for copy in in_copies[away]:
            copy.start()
    for copy in shared_copies:
        copy.wait()
    here = shared[:tokens].T
    k_ref[...] = here[:half]
    v_ref[...] = here[half:]
    for away in range(4):
        for copy in in_copies[away]:
            copy.wait()
        if away + 2 < 4:
            for copy in in_copies[away + 2]:
                copy.start()
        part = contract(inputs[away], shared[...], 1, 0) * (1.0 / math.sqrt(8 * tokens))
        part = part.T
        wk_ref[:, pl.ds(row[away], 2 * tall)] = part[:half]
        wv_ref[:, pl.ds(row[away], 2 * tall)] = part[half:]


def shared_weights(place, own, other, shared):
    smem = pl.BlockSpec(memory_space=pltpu.SMEM)
    vmem = pl.BlockSpec(memory_space=pltpu.VMEM)
    hbm = pl.BlockSpec(memory_space=pl.ANY)
    tall, across = own[0].shape
    tokens = shared[0].shape[1]
    f32, bf16, sem = jnp.float32, jnp.bfloat16, pltpu.SemaphoreType.DMA
    narrow = jax.ShapeDtypeStruct((tall // 2, 8 * tall), f32)
    narrow_in = jax.ShapeDtypeStruct((tall // 2, tokens), bf16)
    return pl.pallas_call(
        shared_weight_kernel,
        out_shape=(narrow, narrow, narrow_in, narrow_in),
        in_specs=[smem, [hbm] * 4, [hbm] * 4, [hbm] * 4],
        out_specs=(vmem, vmem, vmem, vmem),
        scratch_shapes=[
            pltpu.VMEM((4, 2 * tall, across), bf16),
            pltpu.VMEM((across, tall), bf16),
            sem((4, 1, 2)),
            sem((8,)),
        ],
        compiler_params=pltpu.CompilerParams(vmem_limit_bytes=VMEM_BYTES),
        cost_estimate=pl.CostEstimate(
            flops=2 * across * tall * 8 * tall, bytes_accessed=10 * 1024 * 1024, transcendentals=0
        ),
    )(place, list(own), list(other), list(shared))


def local(layer_input, queries, key_vectors, value_vectors, grad_output, positions):
    group = lax.axis_index("dp")
    member, head, z = group % 2, group // 2, group // 4
    here = lax.axis_index("ctx")
    y, x_hi = here // 2, here % 2
    count = queries.shape[0]
    width = layer_input.shape[1] // 8
    slab = width // 8
    first = member == 0
    place = jnp.stack([member, z]).astype(jnp.int32)

    key_local = lax.dynamic_slice_in_dim(key_vectors, head * HD, HD, 1)
    value_local = lax.dynamic_slice_in_dim(value_vectors, head * HD, HD, 1)
    runs_here = (positions[::RUN] // RUN).astype(jnp.bfloat16)
    tail = jnp.broadcast_to(jnp.pad(runs_here, (0, HD - 2))[None], (16, HD))
    own = jnp.concatenate([jnp.where(first, key_local, value_local), tail], axis=0)
    column = jnp.stack([own] + by_source(*to_all_y(own)))
    start = (2 * z + member) * slab

    def block(dy, dx):
        target = ((y + dy) % 4) * 2 + (x_hi + dx) % 2
        return lax.dynamic_slice(layer_input, (0, target * width + start), (count, slab))

    from_x = swap_x(jnp.stack([block(dy, 1) for dy in range(4)]))
    partner_column = swap_x(column)
    column_other = swap_cores(column)
    pairs = [jnp.stack([block(dy, 0), from_x[dy]]) for dy in range(4)]
    moved = [along_y(pairs[dy], dy) for dy in range(1, 4)]
    info = column[:, count, :2].astype(jnp.int32)
    partner_column, info, place, kept, *moved = lax.optimization_barrier(
        (partner_column, info, place, pairs[0], *moved)
    )
    partner_other = swap_cores(partner_column)
    partner_info = partner_column[:, count, :2].astype(jnp.int32)
    slab_own = turn([kept] + moved)
    slab_back, slab_ahead = along_z(slab_own, 1), along_z(slab_own, 3)
    own_other = swap_cores(slab_own)

    grad_query, grad_heads, keep, give = attention(
        place,
        info,
        partner_info,
        queries,
        grad_output,
        [column, partner_column],
        [column_other, partner_other],
    )
    heads = grad_heads.shape[0]
    grad_heads, keep, give, slab_own, slab_back, slab_ahead, own_other = lax.optimization_barrier(
        (grad_heads, keep, give, slab_own, slab_back, slab_ahead, own_other)
    )

    give, back_other = lax.optimization_barrier((swap_cores(give), swap_cores(slab_back)))
    summed = (keep.astype(jnp.float32) + give.astype(jnp.float32)).astype(jnp.bfloat16)
    summed = summed.reshape(2, 4, count, HD)
    from_1 = along_y(jnp.concatenate([grad_heads, summed[:, 3]]), 1)
    from_3 = along_y(jnp.concatenate([grad_heads, summed[:, 1]]), 3)
    rows_2 = along_y(summed[:, 2], 2)
    from_x = swap_x(grad_heads)
    slab_far = along_z(slab_own, 2)
    from_1, from_3, rows_2, from_x, slab_far = lax.optimization_barrier(
        (from_1, from_3, rows_2, from_x, slab_far)
    )
    rows_y = summed[:, 0].astype(jnp.float32)
    for term in (from_1[heads:], from_3[heads:], rows_2):
        rows_y = rows_y + term.astype(jnp.float32)
    rows_y = rows_y.astype(jnp.bfloat16)
    rows_x = swap_x(rows_y)
    from_2 = along_y(jnp.concatenate([grad_heads, from_x]), 2)
    far_other, ahead_other = swap_cores(slab_far), swap_cores(slab_ahead)
    to_x = jnp.concatenate([from_1[:heads], from_3[:heads]])
    rows_x, far_other, ahead_other, to_x = lax.optimization_barrier(
        (rows_x, far_other, ahead_other, to_x)
    )
    from_x13 = swap_x(to_x)
    both = (rows_y.astype(jnp.float32) + rows_x.astype(jnp.float32)[::-1]).astype(jnp.bfloat16)
    shared = [both] + by_source(*to_all_y(both))

    slabs = [slab_own, slab_ahead, slab_far, slab_back]
    slabs_other = [own_other, ahead_other, far_other, back_other]
    early = [(grad_heads, 0), (from_1, 0), (from_3, 0), (from_x, 0)]
    late = [(from_2, 0), (from_x13, 0), (from_2, heads), (from_x13, heads)]
    partial = query_weights(place, slabs, slabs_other, early, heads)
    grad_wq = query_weights(place, slabs, slabs_other, late, heads, partial)
    place, grad_wq = lax.optimization_barrier((place, grad_wq))
    grad_wk, grad_wv, grad_key, grad_value = shared_weights(place, slabs, slabs_other, shared)
    return grad_query, grad_key.T, grad_value.T, grad_wq, grad_wk.T, grad_wv.T


def solution(mesh):
    in_specs = (
        P("ctx", None),
        P("ctx", "dp"),
        P("ctx", None),
        P("ctx", None),
        P("ctx", "dp"),
        P("ctx"),
    )
    out_specs = (P("ctx", "dp"),) * 6
    return jax.shard_map(local, mesh=mesh, in_specs=in_specs, out_specs=out_specs, check_vma=False)
```

```python
import functools
import math

import jax
import jax.numpy as jnp
from jax import lax
from jax.experimental import pallas as pl
from jax.experimental.pallas import tpu as pltpu
from jax.sharding import PartitionSpec as P

HD = 128
QH = 64
KVH = 8
RUN = 256
LOW = -1e30
LOG2E = 1.4426950408889634
VMEM_BYTES = 60 * 1024 * 1024
WEIGHT_VMEM_BYTES = 20 * 1024 * 1024


def contract(left, right, left_dim, right_dim):
    return lax.dot_general(
        left, right, (((left_dim,), (right_dim,)), ((), ())), preferred_element_type=jnp.float32
    )


def along_y(value, step):
    return lax.ppermute(value, "ctx", [(i, (i + 2 * step) % 8) for i in range(8)])


def swap_x(value):
    return lax.ppermute(value, "ctx", [(i, i ^ 1) for i in range(8)])


def along_z(value, step):
    return lax.ppermute(value, "dp", [(i, (i + 4 * step) % 16) for i in range(16)])


def swap_cores(value):
    return lax.ppermute(value, "dp", [(i, i ^ 1) for i in range(16)])


def to_all_y(value):
    return [along_y(value, step) for step in (1, 3, 2)]


def by_source(one, three, two):
    return [one, two, three]


def in_strides(count, step, state):
    done = 0
    for stride in (4, 2, 1):

        def several(j, state, done=done, stride=stride):
            for i in range(stride):
                state = step(done + j * stride + i, state)
            return state

        times = (count - done) // stride
        state = lax.fori_loop(0, times, several, state)
        done = done + times * stride
    return state


def attention_kernel(
    heads, info_ref, q_ref, g_ref, mine_refs, other_refs, dq_ref, dqh_ref, keep_ref, give_ref,
    ks, vs, kt, scores, grads, dka, dva, qh, gh, dqt,
):
    per_ref = mine_refs[0].shape[0]
    slots = per_ref * len(mine_refs)
    runs_per_slot = 2
    scale = 1.0 / math.sqrt(HD)
    core = info_ref[2 * slots]
    for b in range(slots * runs_per_slot):
        slot, part = b // runs_per_slot, b % runs_per_slot
        rows = slice(part * RUN, (part + 1) * RUN)
        at = pl.multiple_of(info_ref[b] * RUN, RUN)
        first = mine_refs[slot // per_ref][slot % per_ref, rows, :]
        second = other_refs[slot // per_ref][slot % per_ref, rows, :]
        key_block = jnp.where(core == 0, first, second)
        ks[pl.ds(at, RUN), :] = key_block
        kt[:, pl.ds(at, RUN)] = key_block.T
        vs[pl.ds(at, RUN), :] = jnp.where(core == 0, second, first)
    dka[...] = jnp.zeros_like(dka)
    dva[...] = jnp.zeros_like(dva)
    for half in range(2):
        run = info_ref[half]
        rows = slice(half * RUN, (half + 1) * RUN)
        for h in range(heads):
            qh[h * RUN : (h + 1) * RUN, :] = q_ref[rows, h * HD : (h + 1) * HD]
            gh[h * RUN : (h + 1) * RUN, :] = g_ref[rows, h * HD : (h + 1) * HD]

        def stat_step(j, state, diagonal):
            at = pl.multiple_of(j * RUN, RUN)
            key_block = ks[pl.ds(at, RUN), :]
            value_block = vs[pl.ds(at, RUN), :]
            new_state = []
            s_all = contract(key_block, qh[...], 1, 1) * (scale * LOG2E)
            dp_all = contract(value_block, gh[...], 1, 1)
            if diagonal:
                key_at = lax.broadcasted_iota(jnp.int32, (RUN, RUN), 0)
                query_at = lax.broadcasted_iota(jnp.int32, (RUN, RUN), 1)
                visible = jnp.concatenate([key_at <= query_at] * heads, axis=1)
                s_all = jnp.where(visible, s_all, LOW)
            scores[pl.ds(at, RUN), :] = s_all
            grads[pl.ds(at, RUN), :] = dp_all
            for h in range(heads):
                row_max, denom, weighted = state[h]
                cols = slice(h * RUN, (h + 1) * RUN)
                s3 = s_all[:, cols].reshape(RUN // 8, 8, RUN)
                dp3 = dp_all[:, cols].reshape(RUN // 8, 8, RUN)
                new_max = jnp.maximum(row_max, jnp.max(s3, axis=0))
                fade = jnp.exp2(row_max - new_max)
                expo = jnp.exp2(s3 - new_max[None])
                if diagonal:
                    expo = jnp.where(s3 > 0.5 * LOW, expo, 0.0)
                new_state.append(
                    (
                        new_max,
                        denom * fade + jnp.sum(expo, axis=0),
                        weighted * fade + jnp.sum(expo * dp3, axis=0),
                    )
                )
            return tuple(new_state)

        zeros = jnp.zeros((8, RUN), jnp.float32)
        state = tuple((jnp.full((8, RUN), LOW, jnp.float32), zeros, zeros) for _ in range(heads))
        state = in_strides(run, lambda j, st: stat_step(j, st, False), state)
        state = stat_step(run, state, True)
        lse, dots = [], []
        for h in range(heads):
            row_max, denom, weighted = state[h]
            top = jnp.max(row_max, axis=0, keepdims=True)
            fade = jnp.exp2(row_max - top)
            total = jnp.sum(denom * fade, axis=0, keepdims=True)
            lse.append(top + jnp.log2(total))
            dots.append(jnp.sum(weighted * fade, axis=0, keepdims=True) / total)
        dqt[...] = jnp.zeros_like(dqt)

        def grad_step(j, carry):
            at = pl.multiple_of(j * RUN, RUN)
            key_cols = kt[:, pl.ds(at, RUN)]
            probs_low, grad_scores = [], []
            for h in range(heads):
                cols = slice(h * RUN, (h + 1) * RUN)
                p = jnp.exp2(scores[pl.ds(at, RUN), cols] - lse[h])
                ds = p * (grads[pl.ds(at, RUN), cols] - dots[h])
                probs_low.append(p.astype(jnp.bfloat16))
                grad_scores.append(ds.astype(jnp.bfloat16))
            ds_all = jnp.concatenate(grad_scores, axis=1)
            dv = contract(jnp.concatenate(probs_low, axis=1), gh[...], 1, 0)
            dk = contract(ds_all, qh[...], 1, 0)
            dqt[...] += contract(key_cols, ds_all, 1, 0)
            dka[pl.ds(at, RUN), :] += dk
            dva[pl.ds(at, RUN), :] += dv
            return carry

        in_strides(run + 1, grad_step, 0)
        for h in range(heads):
            cols = slice(h * RUN, (h + 1) * RUN)
            dq = (dqt[:, cols] * scale).T.astype(jnp.bfloat16)
            dq_ref[rows, h * HD : (h + 1) * HD] = dq
            dqh_ref[h, rows, :] = dq
    half_head = HD // 2
    for b in range(slots * runs_per_slot):
        slot, part = b // runs_per_slot, b % runs_per_slot
        rows = slice(part * RUN, (part + 1) * RUN)
        at = pl.multiple_of(info_ref[b] * RUN, RUN)
        dk = dka[pl.ds(at, RUN), :] * scale
        dv = dva[pl.ds(at, RUN), :]
        low = jnp.concatenate([dk[:, :half_head], dv[:, :half_head]], axis=1)
        high = jnp.concatenate([dk[:, half_head:], dv[:, half_head:]], axis=1)
        keep_ref[slot, rows, :] = jnp.where(core == 0, low, high).astype(jnp.bfloat16)
        give_ref[slot, rows, :] = jnp.where(core == 0, high, low).astype(jnp.bfloat16)


def attention(info, queries, grad_output, mine, other):
    slots = mine[0].shape[0] * len(mine)
    count = slots * 2 * RUN
    heads = queries.shape[1] // HD
    wide = heads * RUN
    smem = pl.BlockSpec(memory_space=pltpu.SMEM)
    vmem = pl.BlockSpec(memory_space=pltpu.VMEM)
    shared = jax.ShapeDtypeStruct((slots, 2 * RUN, HD), jnp.bfloat16)
    pairs = heads * 2 * RUN * count // 2
    return pl.pallas_call(
        functools.partial(attention_kernel, heads),
        out_shape=(
            jax.ShapeDtypeStruct(queries.shape, jnp.bfloat16),
            jax.ShapeDtypeStruct((heads, 2 * RUN, HD), jnp.bfloat16),
            shared,
            shared,
        ),
        in_specs=[smem, vmem, vmem, [vmem] * len(mine), [vmem] * len(other)],
        out_specs=(vmem, vmem, vmem, vmem),
        scratch_shapes=[
            pltpu.VMEM((count, HD), jnp.bfloat16),
            pltpu.VMEM((count, HD), jnp.bfloat16),
            pltpu.VMEM((HD, count), jnp.bfloat16),
            pltpu.VMEM((count, wide), jnp.float32),
            pltpu.VMEM((count, wide), jnp.float32),
            pltpu.VMEM((count, HD), jnp.float32),
            pltpu.VMEM((count, HD), jnp.float32),
            pltpu.VMEM((wide, HD), jnp.bfloat16),
            pltpu.VMEM((wide, HD), jnp.bfloat16),
            pltpu.VMEM((HD, wide), jnp.float32),
        ],
        compiler_params=pltpu.CompilerParams(vmem_limit_bytes=VMEM_BYTES),
        cost_estimate=pl.CostEstimate(
            flops=5 * 4 * pairs * HD, bytes_accessed=8 * 1024 * 1024, transcendentals=2 * pairs
        ),
    )(info, queries, grad_output, mine, other)


def turn_kernel(in_refs, out_ref):
    for dy, ref in enumerate(in_refs):
        for dx in range(2):
            tokens = ref.shape[1]
            at = (dx * len(in_refs) + dy) * tokens
            out_ref[:, at : at + tokens] = ref[dx].T


def turn(pieces):
    vmem = pl.BlockSpec(memory_space=pltpu.VMEM)
    sides, tokens, lanes = pieces[0].shape
    return pl.pallas_call(
        turn_kernel,
        out_shape=jax.ShapeDtypeStruct((lanes, len(pieces) * sides * tokens), jnp.bfloat16),
        in_specs=[[vmem] * len(pieces)],
        out_specs=vmem,
        compiler_params=pltpu.CompilerParams(vmem_limit_bytes=VMEM_BYTES),
        cost_estimate=pl.CostEstimate(flops=0, bytes_accessed=2 * 1024 * 1024, transcendentals=0),
    )(list(pieces))


EARLY = (0, 1, 3, 4)
LATE = (2, 5, 6, 7)


def consecutive(slots):
    spans = []
    for at, slot in enumerate(slots):
        if spans and spans[-1][1] + spans[-1][2] == slot:
            spans[-1][2] += 1
        else:
            spans.append([at, slot, 1])
    return spans


def weight_kernel(last, starts, place_ref, own_refs, other_refs, grad_refs, *rest):
    if last:
        (sum_ref, shared_refs, wq_ref, wk_ref, wv_ref, k_ref, v_ref,
         inputs, grads, sums, shared, in_sems, grad_sems, sum_sems, shared_sems, out_sems) = rest
    else:
        wq_ref, inputs, grads, sums, in_sems, grad_sems, out_sems = rest
    core, z = place_ref[0], place_ref[1]
    tall = own_refs[0].shape[0]
    tokens, wide = grad_refs[0].shape[1:]
    heads = grads.shape[1] // wide
    slots = LATE if last else EARLY
    spans = [[0, 0, 8]] if last else consecutive(EARLY)
    grad_copies = [
        pltpu.make_async_copy(
            ref.at[start + h],
            grads.at[pl.ds(i * tokens, tokens), pl.ds(h * wide, wide)],
            grad_sems.at[i, h],
        )
        for i, (ref, start) in enumerate(zip(grad_refs, starts))
        for h in range(heads)
    ]
    for copy in grad_copies:
        copy.start()
    row = [pl.multiple_of(lax.rem(z + away, 4) * 2 * tall, 2 * tall) for away in range(4)]
    in_copies, sum_copies, shared_copies, out_copies = {}, [], [], []
    if last:
        shared_copies = [
            pltpu.make_async_copy(
                shared_refs[slot % 4].at[slot // 4],
                shared.at[pl.ds(slot * tokens, tokens)],
                shared_sems.at[slot],
            )
            for slot in range(8)
        ]
    for away in range(4):
        for n, (at, slot, many) in enumerate(spans):
            for which, ref in enumerate((own_refs[away], other_refs[away])):
                down = pl.multiple_of((core if which == 0 else 1 - core) * tall, tall)
                in_copies[away, n, which] = pltpu.make_async_copy(
                    ref.at[:, pl.ds(slot * tokens, many * tokens)],
                    inputs.at[away, pl.ds(down, tall), pl.ds(at * tokens, many * tokens)],
                    in_sems.at[away, n, which],
                )
        if last:
            sum_copies.append(
                pltpu.make_async_copy(
                    sum_ref.at[pl.ds(row[away], 2 * tall)], sums.at[away], sum_sems.at[away]
                )
            )

    def fetch(away):
        for n in range(len(spans)):
            for which in range(2):
                in_copies[away, n, which].start()
        if last:
            sum_copies[away].start()

    fetch(0)
    for copy in shared_copies:
        copy.start()
    fetch(1)
    for copy in grad_copies:
        copy.wait()
    norm = 1.0 / math.sqrt(8 * tokens)
    for away in range(4):
        for n in range(len(spans)):
            for which in range(2):
                in_copies[away, n, which].wait()
        if away + 2 < 4:
            fetch(away + 2)
        if last:
            total = sum(
                contract(
                    inputs[away, :, slot * tokens : (slot + many) * tokens],
                    grads[at * tokens : (at + many) * tokens],
                    1,
                    0,
                )
                for at, slot, many in consecutive(slots)
            )
        else:
            total = contract(inputs[away], grads[...], 1, 0)
        if last:
            sum_copies[away].wait()
            total = (total + sums[away]) * norm
        sums[away] = total
        out_copies.append(
            pltpu.make_async_copy(
                sums.at[away], wq_ref.at[pl.ds(row[away], 2 * tall)], out_sems.at[away]
            )
        )
        out_copies[away].start()
        if last:
            if away == 0:
                for copy in shared_copies:
                    copy.wait()
            part = (contract(inputs[away], shared[...], 1, 0) * norm).T
            wk_ref[:, pl.ds(row[away], 2 * tall)] = part[: tall // 2]
            wv_ref[:, pl.ds(row[away], 2 * tall)] = part[tall // 2 :]
    if last:
        here = shared[:tokens].T
        k_ref[...] = here[: here.shape[0] // 2]
        v_ref[...] = here[here.shape[0] // 2 :]
    for copy in out_copies:
        copy.wait()


def weights(place, own, other, grads, heads, total=None, shared=None):
    last = total is not None
    smem = pl.BlockSpec(memory_space=pltpu.SMEM)
    vmem = pl.BlockSpec(memory_space=pltpu.VMEM)
    hbm = pl.BlockSpec(memory_space=pl.ANY)
    tall, across = own[0].shape
    tokens, wide = grads[0][0].shape[1:]
    cols = heads * wide
    f32, bf16, sem = jnp.float32, jnp.bfloat16, pltpu.SemaphoreType.DMA
    wq = jax.ShapeDtypeStruct((8 * tall, cols), f32)
    narrow = jax.ShapeDtypeStruct((tall // 2, 8 * tall), f32)
    narrow_in = jax.ShapeDtypeStruct((tall // 2, tokens), bf16)
    spans = 1 if last else len(consecutive(EARLY))
    scratch = [
        pltpu.VMEM((4, 2 * tall, (8 if last else len(EARLY)) * tokens), bf16),
        pltpu.VMEM((len(grads) * tokens, cols), bf16),
        pltpu.VMEM((4, 2 * tall, cols), f32),
    ]
    if last:
        scratch += [pltpu.VMEM((across, tall), bf16)]
    scratch += [sem((4, spans, 2)), sem((len(grads), heads))]
    if last:
        scratch += [sem((4,)), sem((8,))]
    scratch += [sem((4,))]
    return pl.pallas_call(
        functools.partial(weight_kernel, last, tuple(start for _, start in grads)),
        out_shape=(wq, narrow, narrow, narrow_in, narrow_in) if last else wq,
        in_specs=[smem, [hbm] * 4, [hbm] * 4, [hbm] * 4] + ([hbm, [hbm] * 4] if last else []),
        out_specs=(hbm, vmem, vmem, vmem, vmem) if last else hbm,
        scratch_shapes=scratch,
        compiler_params=pltpu.CompilerParams(vmem_limit_bytes=WEIGHT_VMEM_BYTES),
        cost_estimate=pl.CostEstimate(
            flops=8 * tokens * cols * 8 * tall, bytes_accessed=10 * 1024 * 1024, transcendentals=0
        ),
    )(
        place,
        list(own),
        list(other),
        [array for array, _ in grads],
        *((total, list(shared)) if last else ()),
    )


def local(layer_input, queries, key_vectors, value_vectors, grad_output, positions):
    group = lax.axis_index("dp")
    member, head, z = group % 2, group // 2, group // 4
    here = lax.axis_index("ctx")
    y, x_hi = here // 2, here % 2
    count = queries.shape[0]
    width = layer_input.shape[1] // 8
    slab = width // 8
    first = member == 0
    place = jnp.stack([member, z]).astype(jnp.int32)

    key_local = lax.dynamic_slice_in_dim(key_vectors, head * HD, HD, 1)
    value_local = lax.dynamic_slice_in_dim(value_vectors, head * HD, HD, 1)
    runs_here = (positions[::RUN] // RUN).astype(jnp.bfloat16)
    tail = jnp.broadcast_to(jnp.pad(runs_here, (0, HD - 2))[None], (16, HD))
    own = jnp.concatenate([jnp.where(first, key_local, value_local), tail], axis=0)
    column = jnp.stack([own] + by_source(*to_all_y(own)))
    start = (2 * z + member) * slab

    def block(dy, dx):
        target = ((y + dy) % 4) * 2 + (x_hi + dx) % 2
        return lax.dynamic_slice(layer_input, (0, target * width + start), (count, slab))

    from_x = swap_x(jnp.stack([block(dy, 1) for dy in range(4)]))
    partner_column = swap_x(column)
    column_other = swap_cores(column)
    pairs = [jnp.stack([block(dy, 0), from_x[dy]]) for dy in range(4)]
    moved = [along_y(pairs[dy], dy) for dy in range(1, 4)]
    info = column[:, count, :2].reshape(8).astype(jnp.int32)
    partner_column, info, place, kept, *moved = lax.optimization_barrier(
        (partner_column, info, place, pairs[0], *moved)
    )
    pairs = [kept] + moved
    partner_other = swap_cores(partner_column)
    partner_info = partner_column[:, count, :2].reshape(8).astype(jnp.int32)
    info = jnp.concatenate([info, partner_info, place[:1]])
    slab_own = turn(pairs)
    slab_back, slab_ahead = along_z(slab_own, 1), along_z(slab_own, 3)
    own_other = swap_cores(slab_own)

    grad_query, grad_heads, keep, give = attention(
        info, queries, grad_output, [column, partner_column], [column_other, partner_other]
    )
    heads = grad_heads.shape[0]
    grad_heads, keep, give, slab_own, slab_back, slab_ahead, own_other = lax.optimization_barrier(
        (grad_heads, keep, give, slab_own, slab_back, slab_ahead, own_other)
    )

    give, back_other = lax.optimization_barrier((swap_cores(give), swap_cores(slab_back)))
    summed = (keep.astype(jnp.float32) + give.astype(jnp.float32)).astype(jnp.bfloat16)
    summed = summed.reshape(2, 4, count, HD)
    from_1 = along_y(jnp.concatenate([grad_heads, summed[:, 3]]), 1)
    from_3 = along_y(jnp.concatenate([grad_heads, summed[:, 1]]), 3)
    rows_2 = along_y(summed[:, 2], 2)
    from_x = swap_x(grad_heads)
    slab_far = along_z(slab_own, 2)
    from_1, from_3, rows_2, from_x, slab_far = lax.optimization_barrier(
        (from_1, from_3, rows_2, from_x, slab_far)
    )
    rows_y = summed[:, 0].astype(jnp.float32)
    for term in (from_1[heads:], from_3[heads:], rows_2):
        rows_y = rows_y + term.astype(jnp.float32)
    rows_y = rows_y.astype(jnp.bfloat16)
    rows_x = swap_x(rows_y)
    from_2 = along_y(jnp.concatenate([grad_heads, from_x]), 2)
    far_other, ahead_other = swap_cores(slab_far), swap_cores(slab_ahead)
    to_x = jnp.concatenate([from_1[:heads], from_3[:heads]])
    rows_x, far_other, ahead_other, to_x = lax.optimization_barrier(
        (rows_x, far_other, ahead_other, to_x)
    )
    from_x13 = swap_x(to_x)
    both = (rows_y.astype(jnp.float32) + rows_x.astype(jnp.float32)[::-1]).astype(jnp.bfloat16)
    shared = [both] + by_source(*to_all_y(both))

    slabs = [slab_own, slab_ahead, slab_far, slab_back]
    slabs_other = [own_other, ahead_other, far_other, back_other]
    early = [(grad_heads, 0), (from_1, 0), (from_3, 0), (from_x, 0)]
    late = [(from_2, 0), (from_x13, 0), (from_2, heads), (from_x13, heads)]
    partial = weights(place, slabs, slabs_other, early, heads)
    grad_wq, grad_wk, grad_wv, grad_key, grad_value = weights(
        place, slabs, slabs_other, late, heads, partial, shared
    )
    return grad_query, grad_key.T, grad_value.T, grad_wq, grad_wk.T, grad_wv.T


def solution(mesh):
    in_specs = (
        P("ctx", None),
        P("ctx", "dp"),
        P("ctx", None),
        P("ctx", None),
        P("ctx", "dp"),
        P("ctx"),
    )
    out_specs = (P("ctx", "dp"),) * 6
    return jax.shard_map(local, mesh=mesh, in_specs=in_specs, out_specs=out_specs, check_vma=False)
```

```python
import functools
import math

import jax
import jax.numpy as jnp
from jax import lax
from jax.experimental import pallas as pl
from jax.experimental.pallas import tpu as pltpu
from jax.sharding import PartitionSpec as P

HD = 128
QH = 64
KVH = 8
RUN = 256
LOW = -1e30
LOG2E = 1.4426950408889634
VMEM_BYTES = 60 * 1024 * 1024
WEIGHT_VMEM_BYTES = 16 * 1024 * 1024


def contract(left, right, left_dim, right_dim):
    return lax.dot_general(
        left, right, (((left_dim,), (right_dim,)), ((), ())), preferred_element_type=jnp.float32
    )


def along_y(value, step):
    return lax.ppermute(value, "ctx", [(i, (i + 2 * step) % 8) for i in range(8)])


def swap_x(value):
    return lax.ppermute(value, "ctx", [(i, i ^ 1) for i in range(8)])


def along_z(value, step):
    return lax.ppermute(value, "dp", [(i, (i + 4 * step) % 16) for i in range(16)])


def swap_cores(value):
    return lax.ppermute(value, "dp", [(i, i ^ 1) for i in range(16)])


def to_all_y(value):
    return [along_y(value, step) for step in (1, 3, 2)]


def by_source(one, three, two):
    return [one, two, three]


def in_strides(count, step, state):
    done = 0
    for stride in (4, 2, 1):

        def several(j, state, done=done, stride=stride):
            for i in range(stride):
                state = step(done + j * stride + i, state)
            return state

        times = (count - done) // stride
        state = lax.fori_loop(0, times, several, state)
        done = done + times * stride
    return state


def attention_kernel(
    heads, info_ref, q_ref, g_ref, mine_refs, other_refs, dq_ref, dqh_ref, keep_ref, give_ref,
    ks, vs, kt, scores, grads, dka, dva, qh, gh, dqt,
):
    per_ref = mine_refs[0].shape[0]
    slots = per_ref * len(mine_refs)
    runs_per_slot = 2
    scale = 1.0 / math.sqrt(HD)
    core = info_ref[2 * slots]
    for b in range(slots * runs_per_slot):
        slot, part = b // runs_per_slot, b % runs_per_slot
        rows = slice(part * RUN, (part + 1) * RUN)
        at = pl.multiple_of(info_ref[b] * RUN, RUN)
        first = mine_refs[slot // per_ref][slot % per_ref, rows, :]
        second = other_refs[slot // per_ref][slot % per_ref, rows, :]
        key_block = jnp.where(core == 0, first, second)
        ks[pl.ds(at, RUN), :] = key_block
        kt[:, pl.ds(at, RUN)] = key_block.T
        vs[pl.ds(at, RUN), :] = jnp.where(core == 0, second, first)
    dka[...] = jnp.zeros_like(dka)
    dva[...] = jnp.zeros_like(dva)
    for half in range(2):
        run = info_ref[half]
        rows = slice(half * RUN, (half + 1) * RUN)
        for h in range(heads):
            qh[h * RUN : (h + 1) * RUN, :] = q_ref[rows, h * HD : (h + 1) * HD]
            gh[h * RUN : (h + 1) * RUN, :] = g_ref[rows, h * HD : (h + 1) * HD]

        def stat_step(j, state, diagonal):
            at = pl.multiple_of(j * RUN, RUN)
            key_block = ks[pl.ds(at, RUN), :]
            value_block = vs[pl.ds(at, RUN), :]
            new_state = []
            s_all = contract(key_block, qh[...], 1, 1) * (scale * LOG2E)
            dp_all = contract(value_block, gh[...], 1, 1)
            if diagonal:
                key_at = lax.broadcasted_iota(jnp.int32, (RUN, RUN), 0)
                query_at = lax.broadcasted_iota(jnp.int32, (RUN, RUN), 1)
                visible = jnp.concatenate([key_at <= query_at] * heads, axis=1)
                s_all = jnp.where(visible, s_all, LOW)
            scores[pl.ds(at, RUN), :] = s_all
            grads[pl.ds(at, RUN), :] = dp_all
            for h in range(heads):
                row_max, denom, weighted = state[h]
                cols = slice(h * RUN, (h + 1) * RUN)
                s3 = s_all[:, cols].reshape(RUN // 8, 8, RUN)
                dp3 = dp_all[:, cols].reshape(RUN // 8, 8, RUN)
                new_max = jnp.maximum(row_max, jnp.max(s3, axis=0))
                fade = jnp.exp2(row_max - new_max)
                expo = jnp.exp2(s3 - new_max[None])
                if diagonal:
                    expo = jnp.where(s3 > 0.5 * LOW, expo, 0.0)
                new_state.append(
                    (
                        new_max,
                        denom * fade + jnp.sum(expo, axis=0),
                        weighted * fade + jnp.sum(expo * dp3, axis=0),
                    )
                )
            return tuple(new_state)

        zeros = jnp.zeros((8, RUN), jnp.float32)
        state = tuple((jnp.full((8, RUN), LOW, jnp.float32), zeros, zeros) for _ in range(heads))
        state = in_strides(run, lambda j, st: stat_step(j, st, False), state)
        state = stat_step(run, state, True)
        lse, dots = [], []
        for h in range(heads):
            row_max, denom, weighted = state[h]
            top = jnp.max(row_max, axis=0, keepdims=True)
            fade = jnp.exp2(row_max - top)
            total = jnp.sum(denom * fade, axis=0, keepdims=True)
            lse.append(top + jnp.log2(total))
            dots.append(jnp.sum(weighted * fade, axis=0, keepdims=True) / total)
        dqt[...] = jnp.zeros_like(dqt)

        def grad_step(j, carry):
            at = pl.multiple_of(j * RUN, RUN)
            key_cols = kt[:, pl.ds(at, RUN)]
            probs_low, grad_scores = [], []
            for h in range(heads):
                cols = slice(h * RUN, (h + 1) * RUN)
                p = jnp.exp2(scores[pl.ds(at, RUN), cols] - lse[h])
                ds = p * (grads[pl.ds(at, RUN), cols] - dots[h])
                probs_low.append(p.astype(jnp.bfloat16))
                grad_scores.append(ds.astype(jnp.bfloat16))
            ds_all = jnp.concatenate(grad_scores, axis=1)
            dv = contract(jnp.concatenate(probs_low, axis=1), gh[...], 1, 0)
            dk = contract(ds_all, qh[...], 1, 0)
            dqt[...] += contract(key_cols, ds_all, 1, 0)
            dka[pl.ds(at, RUN), :] += dk
            dva[pl.ds(at, RUN), :] += dv
            return carry

        in_strides(run + 1, grad_step, 0)
        for h in range(heads):
            cols = slice(h * RUN, (h + 1) * RUN)
            dq = (dqt[:, cols] * scale).T.astype(jnp.bfloat16)
            dq_ref[rows, h * HD : (h + 1) * HD] = dq
            dqh_ref[h, rows, :] = dq
    half_head = HD // 2
    for b in range(slots * runs_per_slot):
        slot, part = b // runs_per_slot, b % runs_per_slot
        rows = slice(part * RUN, (part + 1) * RUN)
        at = pl.multiple_of(info_ref[b] * RUN, RUN)
        dk = dka[pl.ds(at, RUN), :] * scale
        dv = dva[pl.ds(at, RUN), :]
        low = jnp.concatenate([dk[:, :half_head], dv[:, :half_head]], axis=1)
        high = jnp.concatenate([dk[:, half_head:], dv[:, half_head:]], axis=1)
        keep_ref[slot, rows, :] = jnp.where(core == 0, low, high).astype(jnp.bfloat16)
        give_ref[slot, rows, :] = jnp.where(core == 0, high, low).astype(jnp.bfloat16)


def attention(info, queries, grad_output, mine, other):
    slots = mine[0].shape[0] * len(mine)
    count = slots * 2 * RUN
    heads = queries.shape[1] // HD
    wide = heads * RUN
    smem = pl.BlockSpec(memory_space=pltpu.SMEM)
    vmem = pl.BlockSpec(memory_space=pltpu.VMEM)
    shared = jax.ShapeDtypeStruct((slots, 2 * RUN, HD), jnp.bfloat16)
    pairs = heads * 2 * RUN * count // 2
    return pl.pallas_call(
        functools.partial(attention_kernel, heads),
        out_shape=(
            jax.ShapeDtypeStruct(queries.shape, jnp.bfloat16),
            jax.ShapeDtypeStruct((heads, 2 * RUN, HD), jnp.bfloat16),
            shared,
            shared,
        ),
        in_specs=[smem, vmem, vmem, [vmem] * len(mine), [vmem] * len(other)],
        out_specs=(vmem, vmem, vmem, vmem),
        scratch_shapes=[
            pltpu.VMEM((count, HD), jnp.bfloat16),
            pltpu.VMEM((count, HD), jnp.bfloat16),
            pltpu.VMEM((HD, count), jnp.bfloat16),
            pltpu.VMEM((count, wide), jnp.float32),
            pltpu.VMEM((count, wide), jnp.float32),
            pltpu.VMEM((count, HD), jnp.float32),
            pltpu.VMEM((count, HD), jnp.float32),
            pltpu.VMEM((wide, HD), jnp.bfloat16),
            pltpu.VMEM((wide, HD), jnp.bfloat16),
            pltpu.VMEM((HD, wide), jnp.float32),
        ],
        compiler_params=pltpu.CompilerParams(vmem_limit_bytes=VMEM_BYTES),
        cost_estimate=pl.CostEstimate(
            flops=5 * 4 * pairs * HD, bytes_accessed=8 * 1024 * 1024, transcendentals=2 * pairs
        ),
    )(info, queries, grad_output, mine, other)


def turn_kernel(in_refs, out_ref):
    for dy, ref in enumerate(in_refs):
        for dx in range(2):
            tokens = ref.shape[1]
            at = (dx * len(in_refs) + dy) * tokens
            out_ref[:, at : at + tokens] = ref[dx].T


def turn(pieces):
    vmem = pl.BlockSpec(memory_space=pltpu.VMEM)
    sides, tokens, lanes = pieces[0].shape
    return pl.pallas_call(
        turn_kernel,
        out_shape=jax.ShapeDtypeStruct((lanes, len(pieces) * sides * tokens), jnp.bfloat16),
        in_specs=[[vmem] * len(pieces)],
        out_specs=vmem,
        compiler_params=pltpu.CompilerParams(vmem_limit_bytes=VMEM_BYTES),
        cost_estimate=pl.CostEstimate(flops=0, bytes_accessed=2 * 1024 * 1024, transcendentals=0),
    )(list(pieces))


EARLY = (0, 1, 3, 4)
LATE = (2, 5, 6, 7)


def consecutive(slots):
    spans = []
    for at, slot in enumerate(slots):
        if spans and spans[-1][1] + spans[-1][2] == slot:
            spans[-1][2] += 1
        else:
            spans.append([at, slot, 1])
    return spans


def weight_kernel(last, starts, place_ref, own_refs, other_refs, grad_refs, *rest):
    if last:
        (sum_ref, shared_refs, wq_ref, wk_ref, wv_ref, k_ref, v_ref,
         inputs, grads, sums, shared, in_sems, grad_sems, sum_sems, shared_sems, out_sems) = rest
    else:
        wq_ref, inputs, grads, sums, in_sems, grad_sems, out_sems = rest
    core, z = place_ref[0], place_ref[1]
    tall = own_refs[0].shape[0]
    tokens, wide = grad_refs[0].shape[1:]
    heads = grads.shape[1] // wide
    slots = LATE if last else EARLY
    spans = [[0, 0, 8]] if last else consecutive(EARLY)
    grad_copies = [
        pltpu.make_async_copy(
            ref.at[start + h],
            grads.at[pl.ds(i * tokens, tokens), pl.ds(h * wide, wide)],
            grad_sems.at[i, h],
        )
        for i, (ref, start) in enumerate(zip(grad_refs, starts))
        for h in range(heads)
    ]
    for copy in grad_copies:
        copy.start()
    row = [pl.multiple_of(lax.rem(z + away, 4) * 2 * tall, 2 * tall) for away in range(4)]
    in_copies, sum_copies, shared_copies, out_copies = {}, [], [], []
    if last:
        shared_copies = [
            pltpu.make_async_copy(
                shared_refs[slot % 4].at[slot // 4],
                shared.at[pl.ds(slot * tokens, tokens)],
                shared_sems.at[slot],
            )
            for slot in range(8)
        ]
    for away in range(4):
        for n, (at, slot, many) in enumerate(spans):
            for which, ref in enumerate((own_refs[away], other_refs[away])):
                down = pl.multiple_of((core if which == 0 else 1 - core) * tall, tall)
                in_copies[away, n, which] = pltpu.make_async_copy(
                    ref.at[:, pl.ds(slot * tokens, many * tokens)],
                    inputs.at[away, pl.ds(down, tall), pl.ds(at * tokens, many * tokens)],
                    in_sems.at[away, n, which],
                )
        if last:
            sum_copies.append(
                pltpu.make_async_copy(
                    sum_ref.at[pl.ds(row[away], 2 * tall)], sums.at[away], sum_sems.at[away]
                )
            )

    def fetch(away):
        for n in range(len(spans)):
            for which in range(2):
                in_copies[away, n, which].start()
        if last:
            sum_copies[away].start()

    fetch(0)
    for copy in shared_copies:
        copy.start()
    fetch(1)
    for copy in grad_copies:
        copy.wait()
    norm = 1.0 / math.sqrt(8 * tokens)
    for away in range(4):
        for n in range(len(spans)):
            for which in range(2):
                in_copies[away, n, which].wait()
        if away + 2 < 4:
            fetch(away + 2)
        if last:
            total = sum(
                contract(
                    inputs[away, :, slot * tokens : (slot + many) * tokens],
                    grads[at * tokens : (at + many) * tokens],
                    1,
                    0,
                )
                for at, slot, many in consecutive(slots)
            )
        else:
            total = contract(inputs[away], grads[...], 1, 0)
        if last:
            sum_copies[away].wait()
            total = (total + sums[away]) * norm
        sums[away] = total
        out_copies.append(
            pltpu.make_async_copy(
                sums.at[away], wq_ref.at[pl.ds(row[away], 2 * tall)], out_sems.at[away]
            )
        )
        out_copies[away].start()
        if last:
            if away == 0:
                for copy in shared_copies:
                    copy.wait()
            part = (contract(inputs[away], shared[...], 1, 0) * norm).T
            wk_ref[:, pl.ds(row[away], 2 * tall)] = part[: tall // 2]
            wv_ref[:, pl.ds(row[away], 2 * tall)] = part[tall // 2 :]
    if last:
        here = shared[:tokens].T
        k_ref[...] = here[: here.shape[0] // 2]
        v_ref[...] = here[here.shape[0] // 2 :]
    for copy in out_copies:
        copy.wait()


def weights(place, own, other, grads, heads, total=None, shared=None):
    last = total is not None
    smem = pl.BlockSpec(memory_space=pltpu.SMEM)
    vmem = pl.BlockSpec(memory_space=pltpu.VMEM)
    hbm = pl.BlockSpec(memory_space=pl.ANY)
    tall, across = own[0].shape
    tokens, wide = grads[0][0].shape[1:]
    cols = heads * wide
    f32, bf16, sem = jnp.float32, jnp.bfloat16, pltpu.SemaphoreType.DMA
    wq = jax.ShapeDtypeStruct((8 * tall, cols), f32)
    narrow = jax.ShapeDtypeStruct((tall // 2, 8 * tall), f32)
    narrow_in = jax.ShapeDtypeStruct((tall // 2, tokens), bf16)
    spans = 1 if last else len(consecutive(EARLY))
    scratch = [
        pltpu.VMEM((4, 2 * tall, (8 if last else len(EARLY)) * tokens), bf16),
        pltpu.VMEM((len(grads) * tokens, cols), bf16),
        pltpu.VMEM((4, 2 * tall, cols), f32),
    ]
    if last:
        scratch += [pltpu.VMEM((across, tall), bf16)]
    scratch += [sem((4, spans, 2)), sem((len(grads), heads))]
    if last:
        scratch += [sem((4,)), sem((8,))]
    scratch += [sem((4,))]
    return pl.pallas_call(
        functools.partial(weight_kernel, last, tuple(start for _, start in grads)),
        out_shape=(wq, narrow, narrow, narrow_in, narrow_in) if last else wq,
        in_specs=[smem, [hbm] * 4, [hbm] * 4, [hbm] * 4] + ([hbm, [hbm] * 4] if last else []),
        out_specs=(hbm, vmem, vmem, vmem, vmem) if last else hbm,
        scratch_shapes=scratch,
        compiler_params=pltpu.CompilerParams(vmem_limit_bytes=WEIGHT_VMEM_BYTES),
        cost_estimate=pl.CostEstimate(
            flops=8 * tokens * cols * 8 * tall, bytes_accessed=10 * 1024 * 1024, transcendentals=0
        ),
    )(
        place,
        list(own),
        list(other),
        [array for array, _ in grads],
        *((total, list(shared)) if last else ()),
    )


def local(layer_input, queries, key_vectors, value_vectors, grad_output, positions):
    group = lax.axis_index("dp")
    member, head, z = group % 2, group // 2, group // 4
    here = lax.axis_index("ctx")
    y, x_hi = here // 2, here % 2
    count = queries.shape[0]
    width = layer_input.shape[1] // 8
    slab = width // 8
    first = member == 0
    place = jnp.stack([member, z]).astype(jnp.int32)

    key_local = lax.dynamic_slice_in_dim(key_vectors, head * HD, HD, 1)
    value_local = lax.dynamic_slice_in_dim(value_vectors, head * HD, HD, 1)
    runs_here = (positions[::RUN] // RUN).astype(jnp.bfloat16)
    tail = jnp.broadcast_to(jnp.pad(runs_here, (0, HD - 2))[None], (16, HD))
    own = jnp.concatenate([jnp.where(first, key_local, value_local), tail], axis=0)
    column = jnp.stack([own] + by_source(*to_all_y(own)))
    start = (2 * z + member) * slab

    def block(dy, dx):
        target = ((y + dy) % 4) * 2 + (x_hi + dx) % 2
        return lax.dynamic_slice(layer_input, (0, target * width + start), (count, slab))

    from_x = swap_x(jnp.stack([block(dy, 1) for dy in range(4)]))
    partner_column = swap_x(column)
    column_other = swap_cores(column)
    pairs = [jnp.stack([block(dy, 0), from_x[dy]]) for dy in range(4)]
    moved = [along_y(pairs[dy], dy) for dy in range(1, 4)]
    info = column[:, count, :2].reshape(8).astype(jnp.int32)
    partner_column, info, place, kept, *moved = lax.optimization_barrier(
        (partner_column, info, place, pairs[0], *moved)
    )
    pairs = [kept] + moved
    partner_other = swap_cores(partner_column)
    partner_info = partner_column[:, count, :2].reshape(8).astype(jnp.int32)
    info = jnp.concatenate([info, partner_info, place[:1]])
    slab_own = turn(pairs)
    slab_back, slab_ahead = along_z(slab_own, 1), along_z(slab_own, 3)
    own_other = swap_cores(slab_own)

    grad_query, grad_heads, keep, give = attention(
        info, queries, grad_output, [column, partner_column], [column_other, partner_other]
    )
    heads = grad_heads.shape[0]
    grad_heads, keep, give, slab_own, slab_back, slab_ahead, own_other = lax.optimization_barrier(
        (grad_heads, keep, give, slab_own, slab_back, slab_ahead, own_other)
    )

    give, back_other = lax.optimization_barrier((swap_cores(give), swap_cores(slab_back)))
    summed = (keep.astype(jnp.float32) + give.astype(jnp.float32)).astype(jnp.bfloat16)
    summed = summed.reshape(2, 4, count, HD)
    from_1 = along_y(jnp.concatenate([grad_heads, summed[:, 3]]), 1)
    from_3 = along_y(jnp.concatenate([grad_heads, summed[:, 1]]), 3)
    rows_2 = along_y(summed[:, 2], 2)
    from_x = swap_x(grad_heads)
    slab_far = along_z(slab_own, 2)
    from_1, from_3, rows_2, from_x, slab_far = lax.optimization_barrier(
        (from_1, from_3, rows_2, from_x, slab_far)
    )
    rows_y = summed[:, 0].astype(jnp.float32)
    for term in (from_1[heads:], from_3[heads:], rows_2):
        rows_y = rows_y + term.astype(jnp.float32)
    rows_y = rows_y.astype(jnp.bfloat16)
    rows_x = swap_x(rows_y)
    from_2 = along_y(jnp.concatenate([grad_heads, from_x]), 2)
    far_other, ahead_other = swap_cores(slab_far), swap_cores(slab_ahead)
    to_x = jnp.concatenate([from_1[:heads], from_3[:heads]])
    rows_x, far_other, ahead_other, to_x = lax.optimization_barrier(
        (rows_x, far_other, ahead_other, to_x)
    )
    from_x13 = swap_x(to_x)
    both = (rows_y.astype(jnp.float32) + rows_x.astype(jnp.float32)[::-1]).astype(jnp.bfloat16)
    shared = [both] + by_source(*to_all_y(both))

    slabs = [slab_own, slab_ahead, slab_far, slab_back]
    slabs_other = [own_other, ahead_other, far_other, back_other]
    early = [(grad_heads, 0), (from_1, 0), (from_3, 0), (from_x, 0)]
    late = [(from_2, 0), (from_x13, 0), (from_2, heads), (from_x13, heads)]
    partial = weights(place, slabs, slabs_other, early, heads)
    grad_wq, grad_wk, grad_wv, grad_key, grad_value = weights(
        place, slabs, slabs_other, late, heads, partial, shared
    )
    return grad_query, grad_key.T, grad_value.T, grad_wq, grad_wk.T, grad_wv.T


def solution(mesh):
    in_specs = (
        P("ctx", None),
        P("ctx", "dp"),
        P("ctx", None),
        P("ctx", None),
        P("ctx", "dp"),
        P("ctx"),
    )
    out_specs = (P("ctx", "dp"),) * 6
    return jax.shard_map(local, mesh=mesh, in_specs=in_specs, out_specs=out_specs, check_vma=False)
```
